32 devices in a mesh: expert: 8 (over z, y), shard: 4 (over x, core).
Axes of the slice: x: 2, y: 2, z: 4, core: 2. Of those that a mesh axis runs over, the one named last changes fastest.
Arguments:
- tokens: bfloat16 [128, 197, 512], P(('expert', 'shard')), may hold values from -12 to 12
- cotangent: bfloat16 [128, 197, 512], P(('expert', 'shard')), may hold values from -6 to 6
- routes: int32 [128, 197, 2], P(('expert', 'shard')), may hold values from 0 to 7, all different within a row
- batch_of_image: int32 [128], P(('expert', 'shard')), may hold values from 0 to 1, as said below
- w_qkv: bfloat16 [512, 1536], P(('expert', 'shard')), may hold values from -0.375 to 0.375
- w_attn_out: bfloat16 [512, 512], P(('expert', 'shard')), may hold values from -1.5 to 1.5
- w_router: bfloat16 [512, 8], P(('expert', 'shard')), may hold values from -0.5 to 0.5
- norm1_gain: bfloat16 [512], P(('expert', 'shard')), may hold values from 0.5 to 1.5
- norm1_bias: bfloat16 [512], P(('expert', 'shard')), may hold values from -1.75 to 1.75
- norm2_gain: bfloat16 [512], P(('expert', 'shard')), may hold values from 0.5 to 1.5
- norm2_bias: bfloat16 [512], P(('expert', 'shard')), may hold values from -1.75 to 1.75
- bias_query: bfloat16 [512], P(('expert', 'shard')), may hold values from -3 to 3
- bias_value: bfloat16 [512], P(('expert', 'shard')), may hold values from -3 to 3
- bias_attn_out: bfloat16 [512], P(('expert', 'shard')), may hold values from -3 to 3
- w_expert_in: bfloat16 [8, 512, 2048], P('expert', None, 'shard'), may hold values from -0.25 to 0.25
- w_expert_out: bfloat16 [8, 2048, 512], P('expert', 'shard'), may hold values from -1.5 to 1.5
- bias_expert_in: bfloat16 [8, 2048], P('expert', 'shard'), may hold values from -3 to 3
- bias_expert_out: bfloat16 [8, 512], P('expert', 'shard'), may hold values from -12 to 12
Outputs:
- layer_out: bfloat16 [128, 197, 512], P(('expert', 'shard'))
- grad_tokens: float32 [128, 197, 512], P(('expert', 'shard'))
- grad_w_qkv: float32 [512, 1536], P(('expert', 'shard'))
- grad_w_attn_out: float32 [512, 512], P(('expert', 'shard'))
- grad_w_router: float32 [512, 8], P(('expert', 'shard'))
- grad_norm1_gain: float32 [512], P(('expert', 'shard'))
- grad_norm1_bias: float32 [512], P(('expert', 'shard'))
- grad_norm2_gain: float32 [512], P(('expert', 'shard'))
- grad_norm2_bias: float32 [512], P(('expert', 'shard'))
- grad_bias_query: float32 [512], P(('expert', 'shard'))
- grad_bias_value: float32 [512], P(('expert', 'shard'))
- grad_bias_attn_out: float32 [512], P(('expert', 'shard'))
- grad_w_expert_in: float32 [8, 512, 2048], P('expert', None, 'shard')
- grad_w_expert_out: float32 [8, 2048, 512], P('expert', 'shard')
- grad_bias_expert_in: float32 [8, 2048], P('expert', 'shard')
- grad_bias_expert_out: float32 [8, 512], P('expert', 'shard')
The draws below stay inside these ranges and needn't reach their ends.
Inputs may be any that keep to these rules, and one draw needn't show every extreme that they name: `batch_of_image`: the 4 images of each device hold every micro-batch number exactly 2 times. The two routes of a token are different experts.
All inputs are finite; a program needn't handle non-finite values.
Results may differ from the reference program's by a relative error of at most 0.017.
The reference program's roundings to bfloat16 on the way count: a program that leaves them out, or rounds other values in their place, can miss the bound.
Values may be sent and summed in bfloat16 or wider, within the bound.
A program may use at most 192 MiB of HBM per device.

```python
import jax
import jax.numpy as jnp
from jax import lax

D = 512
HEADS = 8
HEAD = 64
FF = 2048
SEQ = 197
MICRO = 2
IMG_MB = 2
EXPERTS = 8
IMG_DEV = 4
IMAGES = 128
CAP = 157


def draw_batch_of_image(key, part):
    devices = IMAGES // IMG_DEV
    local_ids = jnp.arange(IMG_DEV, dtype=jnp.int32)
    scores = jax.random.randint(key, (devices, IMG_DEV), 0, 1 << 20) * IMG_DEV + local_ids[None, :]
    shuffled = jnp.argsort(scores, axis=1)
    return (shuffled // IMG_MB).astype(jnp.int32).reshape(IMAGES)


def with_spikes(entries, stream_key, source, target, parts, factor):
    def block_of(axis_at):
        return (jnp.arange(entries.shape[axis_at]) // (entries.shape[axis_at] // parts)).reshape((-1,) + (1,) * (entries.ndim - 1 - axis_at))

    one_side = jax.random.permutation(stream_key, parts)[block_of(target)]
    far = (block_of(target) + parts // 2) % parts
    return jnp.where((block_of(source) == one_side) | (block_of(source) == far), factor * entries, entries)


def block_scale(own_key, dims, cuts, low, top_value):
    gain = 1.0
    for dim, parts in cuts:
        draws = jax.random.uniform(jax.random.fold_in(jax.random.fold_in(own_key, 6), dim), (parts,), jnp.float32, low / len(cuts), top_value / len(cuts))
        gain = gain * jnp.repeat(jnp.exp(draws), dims[dim] // parts).reshape((-1,) + (1,) * (len(dims) - 1 - dim))
    return gain


def different_ones(own_key, rows, amount, top, lift):
    sequence = jax.random.permutation(jax.random.fold_in(own_key, 1), amount)
    boost = sequence
    for power in range(3):
        boost = boost * boost // amount
    boost = boost * lift // amount
    tickets = jax.random.randint(jax.random.fold_in(own_key, 2), (rows, amount), 0, 4096) + boost
    sure = jax.random.permutation(jax.random.fold_in(own_key, 3), rows)[jnp.arange(amount) % rows]
    tickets = jnp.where(jnp.arange(rows)[:, None] == sure[None, :], 1 << 14, tickets)
    priority = tickets * amount + jnp.arange(amount)
    return lax.top_k(priority.astype(jnp.int32), top)[1].astype(jnp.int32)


def bell_draw(rng, dims, scale, limit, shards=(), kind=jnp.bfloat16):
    factor_of = block_scale(rng, dims, shards, -0.22, 0.18) if shards else 1.0
    values = jax.random.normal(rng, dims, jnp.float32) * scale * factor_of
    return jnp.minimum(jnp.maximum(values, -limit), limit).astype(kind)


def noise_with(own_key, shape, deviation, most, shards, heavy, kind=jnp.bfloat16):
    drawn = deviation * jax.random.normal(own_key, shape, jnp.float32)
    if shards:
        drawn = drawn * block_scale(own_key, shape, shards, -0.22, 0.18)
    return jnp.clip(with_spikes(drawn, jax.random.fold_in(own_key, 3), *heavy), -most, most).astype(kind)


def setup_inputs(seed: int = 0) -> dict:
    arg_keys = jax.random.split(jax.random.key(seed), 19)
    return {
        "tokens": noise_with(arg_keys[0], (IMAGES, SEQ, D), 1.0, 12.0, ((0, 32),), (0, 2, 32, 2.75)),
        "cotangent": bell_draw(arg_keys[1], (IMAGES, SEQ, D), 1.0, 6.0, ((0, 32),)),
        "routes": different_ones(arg_keys[2], IMAGES * SEQ, EXPERTS, 2, 2048).reshape((IMAGES, SEQ, 2)),
        "batch_of_image": draw_batch_of_image(jax.random.fold_in(arg_keys[18], 71), 0),
        "w_qkv": bell_draw(arg_keys[4], (D, 3 * D), (D // 2) ** -0.5, 0.375, ((0, 32),)),
        "w_attn_out": bell_draw(arg_keys[5], (D, D), (D // 32) ** -0.5, 1.5, ((0, 32),)),
        "w_router": bell_draw(arg_keys[6], (D, EXPERTS), (D // 4) ** -0.5, 0.5, ((0, 32),)),
        "norm1_gain": jnp.clip(1.0 + 0.1 * jax.random.normal(arg_keys[7], (D,), jnp.float32), 0.5, 1.5).astype(jnp.bfloat16),
        "norm1_bias": bell_draw(arg_keys[8], (D,), 0.3, 1.75, ((0, 32),)),
        "norm2_gain": jnp.clip(1.0 + 0.1 * jax.random.normal(arg_keys[9], (D,), jnp.float32), 0.5, 1.5).astype(jnp.bfloat16),
        "norm2_bias": bell_draw(arg_keys[10], (D,), 0.3, 1.75, ((0, 32),)),
        "bias_query": bell_draw(arg_keys[11], (D,), 0.5, 3.0, ((0, 32),)),
        "bias_value": bell_draw(arg_keys[12], (D,), 0.5, 3.0, ((0, 32),)),
        "bias_attn_out": bell_draw(arg_keys[13], (D,), 0.5, 3.0, ((0, 32),)),
        "w_expert_in": bell_draw(arg_keys[14], (EXPERTS, D, FF), D ** -0.5, 0.25, ((0, 8), (2, 4))),
        "w_expert_out": bell_draw(arg_keys[15], (EXPERTS, FF, D), (FF // 128) ** -0.5, 1.5, ((0, 8), (1, 4))),
        "bias_expert_in": bell_draw(arg_keys[16], (EXPERTS, FF), 0.5, 3.0, ((0, 8), (1, 4))),
        "bias_expert_out": bell_draw(arg_keys[17], (EXPERTS, D), 2.0, 12.0, ((0, 8), (1, 4))),
    }


precise = lax.Precision.HIGHEST
epsilon = 1e-06

@jax.custom_vjp
def low(v):
    return lax.optimization_barrier(v.astype(jnp.bfloat16)).astype(jnp.float32)

@jax.custom_vjp
def low_back(v):
    return v

def low_keep(v):
    return (low(v), None)

def low_pass(kept, grad):
    return (grad,)

def back_keep(v):
    return (v, None)

def back_low(kept, grad):
    return (low(grad),)
low.defvjp(low_keep, low_pass)
low_back.defvjp(back_keep, back_low)

def round_both(values):
    return low(low_back(values))

def layer_norm(inputs, gain_vec, shift_vec):
    center = inputs - lax.optimization_barrier(jnp.mean(inputs, axis=-1, keepdims=True))
    spread = lax.optimization_barrier(jnp.mean(center * center, axis=-1, keepdims=True))
    return center * lax.rsqrt(spread + epsilon) * gain_vec + shift_vec

def group_forward(params, inputs, route_pair):
    w_qkv, w_attn_out, w_router, norm1_gain, norm1_bias, norm2_gain, norm2_bias, bias_query, bias_value, bias_attn_out, w_expert_in, w_expert_out, bias_expert_in, bias_expert_out = params
    tok_rows = inputs.shape[0]
    normed = low(layer_norm(inputs, norm1_gain, norm1_bias))
    project = jnp.dot(normed, w_qkv, precision=precise)
    queries = round_both(project[:, :D] + bias_query)
    keys_all = round_both(project[:, D:2 * D])
    values_all = round_both(project[:, 2 * D:] + bias_value)
    head_shape = (IMG_MB, SEQ, HEADS, HEAD)
    scores = low_back(jnp.einsum('bqhd,bkhd->bhqk', queries.reshape(head_shape), keys_all.reshape(head_shape), precision=precise) * HEAD ** (-0.5))
    attn_weights = low(jax.nn.softmax(scores, axis=-1))
    mixed_heads = jnp.einsum('bhqk,bkhd->bqhd', attn_weights, values_all.reshape(head_shape), precision=precise)
    mixed_heads = round_both(mixed_heads.reshape(tok_rows, D))
    branch = low_back(jnp.dot(mixed_heads, w_attn_out, precision=precise) + bias_attn_out)
    middle = inputs + branch
    routed_in = low(layer_norm(middle, norm2_gain, norm2_bias))
    logits = low_back(jnp.dot(routed_in, w_router, precision=precise))
    gate_probs = jax.nn.softmax(logits, axis=-1)
    expert_ids = jnp.arange(EXPERTS, dtype=jnp.int32)
    first_hot = (route_pair[:, 0:1] == expert_ids[None, :]).astype(jnp.int32)
    second_hot = (route_pair[:, 1:2] == expert_ids[None, :]).astype(jnp.int32)
    pair_hot = jnp.concatenate([first_hot, second_hot], axis=0)
    earlier = jnp.cumsum(pair_hot, axis=0) - pair_hot
    slot_index = lax.optimization_barrier(jnp.sum(pair_hot * earlier, axis=1))
    kept_pairs = slot_index < CAP
    target = jnp.concatenate([route_pair[:, 0], route_pair[:, 1]], axis=0) * CAP + slot_index
    slot_ids = jnp.arange(EXPERTS * CAP, dtype=jnp.int32)
    dispatch = ((target[:, None] == slot_ids[None, :]) & kept_pairs[:, None]).astype(inputs.dtype)
    first_map = dispatch[:tok_rows]
    second_map = dispatch[tok_rows:]
    buffer = low_back(jnp.dot((first_map + second_map).T, routed_in, precision=precise)).reshape(EXPERTS, CAP, D)
    hidden_pre = low_back(jnp.einsum('ecd,edf->ecf', buffer, w_expert_in, precision=precise) + bias_expert_in[:, None, :])
    hidden = low(jax.nn.gelu(hidden_pre, approximate=False))
    expert_out = round_both(jnp.einsum('ecf,efd->ecd', hidden, w_expert_out, precision=precise) + bias_expert_out[:, None, :]).reshape(EXPERTS * CAP, D)
    gate_first = lax.optimization_barrier(jnp.sum(gate_probs * first_hot.astype(inputs.dtype), axis=1))
    gate_second = lax.optimization_barrier(jnp.sum(gate_probs * second_hot.astype(inputs.dtype), axis=1))
    combine = first_map * gate_first[:, None] + second_map * gate_second[:, None]
    return middle + jnp.dot(combine, expert_out, precision=precise)

def arrange(values, image_order):
    devices = image_order.shape[0]
    trailing = values.shape[1:]
    shaped = values.reshape((devices, IMG_DEV) + trailing)
    gather_index = jnp.broadcast_to(image_order.reshape((devices, IMG_DEV) + (1,) * len(trailing)), shaped.shape)
    picked = jnp.take_along_axis(shaped, gather_index, axis=1)
    return picked.reshape((devices * MICRO, IMG_MB * SEQ) + trailing[1:])

def unarrange(results, inverse):
    devices = inverse.shape[0]
    shaped = results.reshape((devices, IMG_DEV, SEQ, D))
    gather_index = jnp.broadcast_to(inverse.reshape((devices, IMG_DEV, 1, 1)), shaped.shape)
    return jnp.take_along_axis(shaped, gather_index, axis=1).reshape((IMAGES, SEQ, D))

def reference(tokens, cotangent, routes, batch_of_image, w_qkv, w_attn_out, w_router, norm1_gain, norm1_bias, norm2_gain, norm2_bias, bias_query, bias_value, bias_attn_out, w_expert_in, w_expert_out, bias_expert_in, bias_expert_out):
    devices = IMAGES // IMG_DEV
    local_ids = jnp.arange(IMG_DEV, dtype=jnp.int32)
    image_order = jnp.argsort(batch_of_image.reshape(devices, IMG_DEV) * IMG_DEV + local_ids[None, :], axis=1).astype(jnp.int32)
    inverse = jnp.argsort(image_order, axis=1).astype(jnp.int32)
    routes_grouped = arrange(routes, image_order)
    params = tuple((weight.astype(jnp.float32) for weight in (w_qkv, w_attn_out, w_router, norm1_gain, norm1_bias, norm2_gain, norm2_bias, bias_query, bias_value, bias_attn_out, w_expert_in, w_expert_out, bias_expert_in, bias_expert_out)))
    group_step = jax.checkpoint(group_forward)

    def whole_layer(inputs, weights_all):
        grouped = arrange(inputs, image_order)
        results = lax.map(lambda members: group_step(weights_all, members[0], members[1]), (grouped, routes_grouped))
        return unarrange(results, inverse)
    layer_out, pullback = jax.vjp(whole_layer, tokens.astype(jnp.float32), params)
    grad_tokens, grads_all = pullback(cotangent.astype(jnp.float32))
    return (layer_out.astype(jnp.bfloat16), grad_tokens, grads_all[0], grads_all[1], grads_all[2], grads_all[3], grads_all[4], grads_all[5], grads_all[6], grads_all[7], grads_all[8], grads_all[9], grads_all[10], grads_all[11], grads_all[12], grads_all[13])
```

```python
import functools
import math

import jax
import jax.numpy as jnp
from jax import lax
from jax.experimental import pallas as pl
from jax.experimental.pallas import tpu as pltpu
from jax.sharding import PartitionSpec as P

HEADS = 8
MICRO = 2
EPS = 1e-06
F32 = jnp.float32
BF16 = jnp.bfloat16
MESH = pl.DeviceIdType.MESH
VMEM_LIMIT = 56 * 1024 * 1024
VMEM_SPEC = pl.BlockSpec(memory_space=pltpu.VMEM)
SMEM_SPEC = pl.BlockSpec(memory_space=pltpu.SMEM)
ANY_SPEC = pl.BlockSpec(memory_space=pl.ANY)


def round_up(value, unit):
    return (value + unit - 1) // unit * unit


def mm(left, right):
    return lax.dot_general(left, right, (((1,), (0,)), ((), ())), preferred_element_type=F32)


def mm_nt(left, right):
    return lax.dot_general(left, right, (((1,), (1,)), ((), ())), preferred_element_type=F32)


def mm_tn(left, right):
    return lax.dot_general(left, right, (((0,), (0,)), ((), ())), preferred_element_type=F32)


def cost(flops, nbytes, trans=0):
    return pl.CostEstimate(flops=int(flops), bytes_accessed=int(nbytes), transcendentals=int(trans))


def plain(name_cost):
    return dict(
        cost_estimate=name_cost,
        compiler_params=pltpu.CompilerParams(vmem_limit_bytes=VMEM_LIMIT),
    )


def image_order(batch_ref, n_img):
    keys = [batch_ref[i] * n_img + i for i in range(n_img)]
    ranks = []
    for i in range(n_img):
        rank = jnp.int32(0)
        for j in range(n_img):
            if j != i:
                rank = rank + jnp.where(keys[j] < keys[i], 1, 0)
        ranks.append(rank)
    order = []
    for k in range(n_img):
        place = jnp.int32(0)
        for i in range(n_img):
            place = place + jnp.where(ranks[i] == k, i, 0)
        order.append(place)
    return order


def flip(index, bit):
    return index + bit - 2 * bit * lax.rem(index // bit, 2)


def lanes(rows, width):
    return lax.broadcasted_iota(jnp.int32, (rows, width), 1)


def bit_orders(n_expert, n_shard):
    shard_bits = [1 << i for i in range(n_shard.bit_length() - 1)]
    expert_bits = [n_shard << i for i in range(n_expert.bit_length() - 1)]
    core = shard_bits[:1]
    across = shard_bits[1:]
    first = expert_bits[::-1] + across[::-1] + core
    second = across[::-1] + expert_bits[:0:-1] + expert_bits[:1] + core
    return first, second


def combos(bits):
    result = [0]
    for bit in bits:
        result = result + [held + bit for held in result]
    return result


def flip_all(index, combo):
    bit = 1
    while bit <= combo:
        if combo & bit:
            index = flip(index, bit)
        bit *= 2
    return index


def greet(me, bits, n_shard):
    barrier = pltpu.get_barrier_semaphore()
    for bit in bits:
        peer = flip(me, bit)
        pl.semaphore_signal(
            barrier, inc=1, device_id=(peer // n_shard, lax.rem(peer, n_shard)), device_id_type=MESH
        )
    pl.semaphore_wait(barrier, len(bits))


def gather_kernel(n_shard, orders, cuts, mine_ref, full_ref, local_sem, send_sems, recv_sems):
    me = lax.axis_index("expert") * n_shard + lax.axis_index("shard")
    greet(me, orders[0], n_shard)
    own = pltpu.make_async_copy(mine_ref, full_ref.at[me], local_sem)
    own.start()
    copies = []
    for step in range(len(orders[0])):
        started = []
        for part, order in enumerate(orders):
            bit = order[step]
            peer = flip(me, bit)
            low, high = cuts[part]
            for at, combo in enumerate(combos(order[:step])):
                chunk = flip_all(me, combo)
                source = mine_ref if combo == 0 else full_ref.at[chunk]
                copy = pltpu.make_async_remote_copy(
                    src_ref=source.at[:, low:high],
                    dst_ref=full_ref.at[chunk, :, low:high],
                    send_sem=send_sems.at[part, (1 << step) - 1 + at],
                    recv_sem=recv_sems.at[part, (1 << step) - 1 + at],
                    device_id=(peer // n_shard, lax.rem(peer, n_shard)),
                    device_id_type=MESH,
                )
                copy.start()
                started.append(copy)
        for copy in started:
            copy.wait_recv()
        copies.extend(started)
    for copy in copies:
        copy.wait_send()
    own.wait()


def gather_params(packed, n_expert, n_shard, collective_id):
    rows, width = packed.shape
    n_dev = n_expert * n_shard
    orders = bit_orders(n_expert, n_shard)
    middle = width // 256 * 128
    cuts = ((0, middle), (middle, width))
    full = pl.pallas_call(
        functools.partial(gather_kernel, n_shard, orders, cuts),
        out_shape=jax.ShapeDtypeStruct((n_dev, rows, width), packed.dtype),
        in_specs=[VMEM_SPEC],
        out_specs=VMEM_SPEC,
        scratch_shapes=[
            pltpu.SemaphoreType.DMA,
            pltpu.SemaphoreType.DMA((2, n_dev - 1)),
            pltpu.SemaphoreType.DMA((2, n_dev - 1)),
        ],
        compiler_params=pltpu.CompilerParams(
            collective_id=collective_id, has_side_effects=True, vmem_limit_bytes=VMEM_LIMIT
        ),
        cost_estimate=cost(1e6, 4 * n_dev * rows * width),
    )(packed)
    return full.reshape(n_dev * rows, width)


def scatter_kernel(n_shard, orders, cuts, full_ref, out_ref, acc, sends, recvs, send_sems, recv_sems):
    me = lax.axis_index("expert") * n_shard + lax.axis_index("shard")
    n_dev = full_ref.shape[0]
    greet(me, orders[0], n_shard)
    n_steps = len(orders[0])
    acc[...] = full_ref[...]
    copies = []
    for step in range(n_steps):
        started = []
        base = n_dev - (n_dev >> step)
        count = n_dev >> (step + 1)
        for part, order in enumerate(orders):
            bit = order[step]
            peer = flip(me, bit)
            low, high = cuts[part]
            for at, combo in enumerate(combos(order[step + 1 :])):
                chunk = flip_all(peer, combo)
                sends[base + at, :, low:high] = acc[chunk, :, low:high].astype(BF16)
            copy = pltpu.make_async_remote_copy(
                src_ref=sends.at[base : base + count, :, low:high],
                dst_ref=recvs.at[base : base + count, :, low:high],
                send_sem=send_sems.at[part, step],
                recv_sem=recv_sems.at[part, step],
                device_id=(peer // n_shard, lax.rem(peer, n_shard)),
                device_id_type=MESH,
            )
            copy.start()
            started.append(copy)
        for part, order in enumerate(orders):
            low, high = cuts[part]
            started[part].wait_recv()
            for at, combo in enumerate(combos(order[step + 1 :])):
                chunk = flip_all(me, combo)
                acc[chunk, :, low:high] += recvs[base + at, :, low:high].astype(F32)
        copies.extend(started)
    out_ref[...] = acc[me]
    for copy in copies:
        copy.wait_send()


def scatter_params(full, n_expert, n_shard, collective_id):
    n_dev = n_expert * n_shard
    width = full.shape[1]
    rows = full.shape[0] // n_dev
    gather_orders = bit_orders(n_expert, n_shard)
    orders = [order[::-1] for order in gather_orders]
    middle = width // 256 * 128
    cuts = ((0, middle), (middle, width))
    return pl.pallas_call(
        functools.partial(scatter_kernel, n_shard, orders, cuts),
        out_shape=jax.ShapeDtypeStruct((rows, width), F32),
        in_specs=[VMEM_SPEC],
        out_specs=VMEM_SPEC,
        scratch_shapes=[
            pltpu.VMEM((n_dev, rows, width), F32),
            pltpu.VMEM((n_dev, rows, width), BF16),
            pltpu.VMEM((n_dev, rows, width), BF16),
            pltpu.SemaphoreType.DMA((2, len(orders[0]))),
            pltpu.SemaphoreType.DMA((2, len(orders[0]))),
        ],
        compiler_params=pltpu.CompilerParams(
            collective_id=collective_id, has_side_effects=True, vmem_limit_bytes=VMEM_LIMIT
        ),
        cost_estimate=cost(1e6, 8 * n_dev * rows * width),
    )(full.reshape(n_dev, rows, width))


def route_kernel(dims, batch_ref, half_ref, routes_ref, cot_ref, col_ref, row_ref, csend_ref, cot_s, rt_s):
    n_img, seq, pad, group, n_pos, reps, cap, cap_pad = dims
    rows = group * pad
    msg = reps * cap_pad
    order = image_order(batch_ref, n_img)
    half = half_ref[0].astype(F32)
    lower = (
        lax.broadcasted_iota(jnp.int32, (rows, rows), 0)
        > lax.broadcasted_iota(jnp.int32, (rows, rows), 1)
    ).astype(F32).astype(BF16)
    ids = lanes(rows, 128)
    for micro in range(MICRO):
        rt_s[...] = jnp.full(rt_s.shape, -1, jnp.int32)
        cot_s[...] = jnp.zeros(cot_s.shape, F32)
        for n in range(group):
            place = order[micro * group + n]
            rt_s[n * pad : n * pad + seq, 0:2] = routes_ref[place]
            cot_s[n * pad : n * pad + seq, :] = cot_ref[place].astype(F32)
        first = rt_s[:, 0:1]
        second = rt_s[:, 1:2]
        hot_first = (ids == first).astype(F32)
        hot_second = (ids == second).astype(F32)
        earlier_first = mm(lower, hot_first.astype(BF16))
        earlier_second = mm(lower, hot_second.astype(BF16)) + jnp.sum(hot_first, axis=0, keepdims=True)
        table = jnp.where(ids == 0, first.astype(F32), jnp.where(ids == 1, second.astype(F32), 0.0))
        for lane, route, hot, earlier in (
            (2, first, hot_first, earlier_first),
            (3, second, hot_second, earlier_second),
        ):
            slot = jnp.sum(hot * earlier, axis=1, keepdims=True)
            route_f = route.astype(F32)
            upper = (route_f >= float(n_pos)).astype(F32) if reps > 1 else jnp.zeros_like(route_f)
            place = route_f - upper * float(n_pos)
            rel = jnp.abs(upper - half) if reps > 1 else upper
            target = place * float(msg) + rel * float(cap_pad) + slot
            target = jnp.where((slot < float(cap)) & (route_f >= 0.0), target, -1.0)
            table = jnp.where(ids == lane, target, table)
        col_ref[micro] = table
        turned = jnp.concatenate(
            [table, jnp.full((round_up(rows, 128) - rows, 128), -1.0, F32)], axis=0
        ).T
        row_ref[micro] = turned[0:8, :]
        row_first = turned[2:3, 0:rows]
        row_second = turned[3:4, 0:rows]
        cot = cot_s[...].astype(BF16)
        slots = lax.broadcasted_iota(jnp.int32, (msg, rows), 0)

        def send(pos, carry):
            here = (slots + pos * msg).astype(F32)
            chosen = ((here == row_first) | (here == row_second)).astype(F32).astype(BF16)
            csend_ref[pos, micro * msg : (micro + 1) * msg, :] = mm(chosen, cot).astype(BF16)
            return carry

        lax.fori_loop(0, n_pos, send, 0)


def load_group(ref, order, micro, group, seq, pad, buf):
    buf[...] = jnp.zeros(buf.shape, F32)
    for n in range(group):
        buf[n * pad : n * pad + seq, :] = ref[order[micro * group + n]].astype(F32)
    return buf[...]


def norm_parts(values):
    center = values - jnp.mean(values, axis=-1, keepdims=True)
    rate = lax.rsqrt(jnp.mean(center * center, axis=-1, keepdims=True) + EPS)
    return center * rate, rate


def forward_kernel(
    dims, micro, batch_ref, tok_ref, full_ref, col_ref, row_ref,
    a1_ref, qkv_ref, mix_ref, mid_ref, a2_ref, gate_ref, lse_ref, send_ref, x_s,
):
    n_img, seq, pad, group, n_pos, reps, cap, cap_pad, n_exp = dims
    rows = group * pad
    msg = reps * cap_pad
    width = tok_ref.shape[-1]
    head = width // HEADS
    per_pair = 128 // head
    order = image_order(batch_ref, n_img)
    x = load_group(tok_ref, order, micro, group, seq, pad, x_s)
    small = full_ref[:, 4 * width :]
    turned = small.astype(F32).T
    gain1, shift1, gain2, shift2, bias_q, bias_v, bias_o = [
        turned[n_exp + i : n_exp + i + 1, :] for i in range(7)
    ]
    normed, _ = norm_parts(x)
    a1 = (normed * gain1 + shift1).astype(BF16)
    a1_ref[...] = a1
    proj = mm(a1, full_ref[:, 0 : 3 * width])
    scale = head ** (-0.5)
    qkv_ref[:, 0:width] = ((proj[:, 0:width] + bias_q).astype(BF16).astype(F32) * scale).astype(BF16)
    qkv_ref[:, width : 2 * width] = proj[:, width : 2 * width].astype(BF16)
    qkv_ref[:, 2 * width :] = (proj[:, 2 * width :] + bias_v).astype(BF16)
    key_ok = lanes(pad, pad) < seq
    lane = lanes(pad, 128)
    for n in range(group):
        at = slice(n * pad, (n + 1) * pad)
        lse = jnp.zeros((pad, 128), F32)
        for pair in range(width // 128):
            cols = pair * 128
            q2 = qkv_ref[at, cols : cols + 128]
            k2 = qkv_ref[at, width + cols : width + cols + 128]
            v2 = qkv_ref[at, 2 * width + cols : 2 * width + cols + 128]
            mixed = None
            for sub in range(per_pair):
                mine = (lane >= sub * head) & (lane < (sub + 1) * head)
                scores = mm_nt(jnp.where(mine, q2, jnp.zeros_like(q2)), k2)
                scores = jnp.where(key_ok, scores, -jnp.inf)
                top = jnp.max(scores, axis=-1, keepdims=True)
                grown = jnp.exp(scores - top)
                total = jnp.sum(grown, axis=-1, keepdims=True)
                probs = (grown / total).astype(BF16)
                part = mm(probs, jnp.where(mine, v2, jnp.zeros_like(v2)))
                mixed = part if mixed is None else mixed + part
                lse = jnp.where(lane == pair * per_pair + sub, top + jnp.log(total), lse)
            mix_ref[at, cols : cols + 128] = mixed.astype(BF16)
        lse_ref[at, :] = lse
    mid = x + mm(mix_ref[...], full_ref[:, 3 * width : 4 * width]) + bias_o
    mid_ref[...] = mid
    normed2, _ = norm_parts(mid)
    a2 = (normed2 * gain2 + shift2).astype(BF16)
    a2_ref[...] = a2
    ids = lanes(rows, 128)
    logits = jnp.where(ids < n_exp, mm(a2, small), -jnp.inf)
    grown = jnp.exp(logits - jnp.max(logits, axis=-1, keepdims=True))
    gates = grown / jnp.sum(grown, axis=-1, keepdims=True)
    gate_ref[...] = gates
    table = col_ref[0]
    gate1 = jnp.sum(jnp.where(ids.astype(F32) == table[:, 0:1], gates, 0.0), axis=1, keepdims=True)
    gate2 = jnp.sum(jnp.where(ids.astype(F32) == table[:, 1:2], gates, 0.0), axis=1, keepdims=True)
    to1, to2 = table[:, 2:3], table[:, 3:4]
    row1, row2 = row_ref[0, 2:3, 0:rows], row_ref[0, 3:4, 0:rows]
    slots = lax.broadcasted_iota(jnp.int32, (msg, rows), 0)
    along = lanes(rows, cap_pad)
    for pos in range(n_pos):
        here = (slots + pos * msg).astype(F32)
        chosen = ((here == row1) | (here == row2)).astype(F32).astype(BF16)
        send_ref[pos, 0:msg, :] = mm(chosen, a2).astype(BF16)
        send_ref[pos, msg : msg + 16, :] = jnp.zeros((16, width), BF16)
        tail = jnp.zeros((16, cap_pad), F32)
        tail_id = lax.broadcasted_iota(jnp.int32, (16, cap_pad), 0)
        for rel in range(reps):
            there = (along + (pos * msg + rel * cap_pad)).astype(F32)
            gate_row = jnp.sum(
                jnp.where(there == to1, gate1, 0.0) + jnp.where(there == to2, gate2, 0.0),
                axis=0,
                keepdims=True,
            )
            high = gate_row.astype(BF16).astype(F32)
            tail = jnp.where(tail_id == 2 * rel, high, jnp.where(tail_id == 2 * rel + 1, gate_row - high, tail))
        send_ref[pos, msg : msg + 16, 0:cap_pad] = tail.astype(BF16)


def gelu_pair(v):
    size = jnp.abs(v)
    bell = jnp.exp(v * v * -0.5)
    t = 1.0 / (1.0 + (0.3275911 / math.sqrt(2.0)) * size)
    series = t * (
        0.5 * 0.254829592
        + t * (0.5 * -0.284496736 + t * (0.5 * 1.421413741 + t * (0.5 * -1.453152027 + t * (0.5 * 1.061405429))))
    )
    tail = series * bell
    share = jnp.where(v >= 0.0, 1.0 - tail, tail)
    return v * share, share + v * bell * (1.0 / math.sqrt(2.0 * math.pi))


def expert_kernel(dims, *refs):
    n_pos, reps, n_shard, cap_pad, width, ff, tail_rows = dims
    n_pieces = reps * n_shard
    in_refs = refs[:n_pieces]
    out_refs = refs[n_pieces : 2 * n_pieces]
    (a_ref, c_ref, eo_ref, dbuf_ref, hid_ref, dh_ref, deo_ref, buf_ref) = refs[2 * n_pieces : 2 * n_pieces + 8]
    (win, wout, pre, back, eo_acc, db_acc, bias_acc, sem_in, sem_out) = refs[2 * n_pieces + 8 :]
    step = pl.program_id(0)
    shard = lax.rem(step, n_shard)
    rel = step // n_shard
    msg = reps * cap_pad
    rows = n_pos * cap_pad

    @pl.when(step == 0)
    def _():
        for i in range(n_pieces):
            pltpu.make_async_copy(in_refs[i], win.at[i], sem_in.at[i]).start()
            pltpu.make_async_copy(out_refs[i], wout.at[i], sem_out.at[i]).start()
        eo_ref[...] = jnp.zeros(eo_ref.shape, BF16)
        dbuf_ref[...] = jnp.zeros(dbuf_ref.shape, BF16)

    @pl.when(shard == 0)
    def _():
        bias_acc[...] = jnp.zeros(bias_acc.shape, F32)
        tails = jnp.concatenate([a_ref[p, msg : msg + 16, :].astype(F32) for p in range(n_pos)], axis=0)
        pad_rows = round_up(n_pos * 16, 128) - n_pos * 16
        if pad_rows:
            tails = jnp.concatenate([tails, jnp.zeros((pad_rows, width), F32)], axis=0)
        turned = tails.T
        for r in range(reps):

            @pl.when(rel == r)
            def _():
                for p in range(n_pos):
                    there = slice(p * cap_pad, (p + 1) * cap_pad)
                    gate = (
                        turned[0:cap_pad, p * 16 + 2 * r : p * 16 + 2 * r + 1]
                        + turned[0:cap_pad, p * 16 + 2 * r + 1 : p * 16 + 2 * r + 2]
                    )
                    buf_ref[0, there, :] = a_ref[p, r * cap_pad : (r + 1) * cap_pad, :]
                    cot = c_ref[p, r * cap_pad : (r + 1) * cap_pad, :].astype(F32)
                    deo_ref[0, there, :] = (cot * gate).astype(BF16)

    for i in range(n_pieces):

        @pl.when(step == i)
        def _():
            pltpu.make_async_copy(in_refs[i], win.at[i], sem_in.at[i]).wait()
            pltpu.make_async_copy(out_refs[i], wout.at[i], sem_out.at[i]).wait()

    buf = buf_ref[0]
    deo = deo_ref[0]
    w_in = win[step, 0:width, :]
    w_out = wout[step]
    bias_in = win[step, width : width + 16, :].astype(F32)
    pre[...] = mm(buf, w_in) + bias_in[0:1, :]
    back[...] = mm_nt(deo, w_out)
    for p in range(n_pos):
        there = slice(p * cap_pad, (p + 1) * cap_pad)
        value, slope = gelu_pair(pre[there, :])
        hid_ref[0, there, :] = value.astype(BF16)
        dh_ref[0, there, :] = (back[there, :] * slope).astype(BF16)
    eo_part = mm(hid_ref[0], w_out)
    db_part = mm_nt(dh_ref[0], w_in)
    bias_acc[...] += jnp.concatenate([bias_in[1 + i : 2 + i, :] for i in range(width // ff)], axis=1)

    @pl.when(shard == 0)
    def _():
        eo_acc[...] = eo_part
        db_acc[...] = db_part

    @pl.when(shard > 0)
    def _():
        eo_acc[...] += eo_part
        db_acc[...] += db_part

    for r in range(reps):

        @pl.when((shard == n_shard - 1) & (rel == r))
        def _():
            tail_id = lax.broadcasted_iota(jnp.int32, (16, cap_pad), 0)
            ones = jnp.ones((16, width), BF16)
            for p in range(n_pos):
                there = slice(p * cap_pad, (p + 1) * cap_pad)
                here = slice(r * cap_pad, (r + 1) * cap_pad)
                eo = (eo_acc[there, :] + bias_acc[...]).astype(BF16)
                eo_ref[p, here, :] = eo
                dbuf_ref[p, here, :] = db_acc[there, :].astype(BF16)
                product = c_ref[p, here, :].astype(F32) * eo.astype(F32)
                high = product.astype(BF16)
                low = (product - high.astype(F32)).astype(BF16)
                dgate = mm_nt(ones, high) + mm_nt(ones, low)
                dg_high = dgate.astype(BF16).astype(F32)
                held = dbuf_ref[p, msg : msg + 16, 0:cap_pad].astype(F32)
                held = jnp.where(tail_id == 2 * r, dg_high, jnp.where(tail_id == 2 * r + 1, dgate - dg_high, held))
                dbuf_ref[p, msg : msg + 16, 0:cap_pad] = held.astype(BF16)


def run_expert(arrived, cots, micro, pieces, n_pos, reps, n_shard, cap_pad):
    width = arrived.shape[-1]
    ext, ff = pieces[0][0].shape
    msg = reps * cap_pad
    rows = n_pos * cap_pad
    n_pieces = reps * n_shard
    dims = (n_pos, reps, n_shard, cap_pad, width, ff, ext - width)
    whole = lambda *shape: pl.BlockSpec(shape, lambda i: (0,) * len(shape))
    per_rel = pl.BlockSpec((1, rows, width), lambda i: (i // n_shard, 0, 0))
    per_step = pl.BlockSpec((1, rows, ff), lambda i: (i // n_shard, 0, lax.rem(i, n_shard)))
    return pl.pallas_call(
        functools.partial(expert_kernel, dims),
        grid=(n_pieces,),
        out_shape=(
            jax.ShapeDtypeStruct((n_pos, msg, width), BF16),
            jax.ShapeDtypeStruct((n_pos, msg + 16, width), BF16),
            jax.ShapeDtypeStruct((reps, rows, n_shard * ff), BF16),
            jax.ShapeDtypeStruct((reps, rows, n_shard * ff), BF16),
            jax.ShapeDtypeStruct((reps, rows, width), BF16),
            jax.ShapeDtypeStruct((reps, rows, width), BF16),
        ),
        in_specs=[ANY_SPEC] * (2 * n_pieces)
        + [whole(n_pos, msg + 16, width), pl.BlockSpec((n_pos, msg, width), lambda i: (0, micro, 0))],
        out_specs=(whole(n_pos, msg, width), whole(n_pos, msg + 16, width), per_step, per_step, per_rel, per_rel),
        scratch_shapes=[
            pltpu.VMEM((n_pieces, ext, ff), BF16),
            pltpu.VMEM((n_pieces, ff, width), BF16),
            pltpu.VMEM((rows, ff), F32),
            pltpu.VMEM((rows, ff), F32),
            pltpu.VMEM((rows, width), F32),
            pltpu.VMEM((rows, width), F32),
            pltpu.VMEM((1, width), F32),
            pltpu.SemaphoreType.DMA((n_pieces,)),
            pltpu.SemaphoreType.DMA((n_pieces,)),
        ],
        **plain(cost(8.0 * n_pieces * rows * ff * width, 40e6, 2 * n_pieces * rows * ff)),
    )(*[p[0] for p in pieces], *[p[1] for p in pieces], arrived, cots)


def weight_grad_kernel(dims, *refs):
    n_shard, width, ff = dims
    bufs, deos, hids, dhs = refs[0:2], refs[2:4], refs[4:6], refs[6:8]
    gin_ref, gout_ref = refs[8:10]
    buf_t, deo_t, bias_s = refs[10:13]
    rows = bufs[0].shape[1]

    @pl.when(lax.rem(pl.program_id(0), n_shard) == 0)
    def _():
        total = None
        for m in range(2):
            buf_t[:, m * rows : (m + 1) * rows] = bufs[m][0].T
            deo_t[:, m * rows : (m + 1) * rows] = deos[m][0].T
            part = jnp.sum(deos[m][0].astype(F32), axis=0, keepdims=True)
            total = part if total is None else total + part
        bias_s[...] = total

    grad_in = None
    grad_out = None
    bias_in = None
    for m in range(2):
        here = slice(m * rows, (m + 1) * rows)
        dh = dhs[m][0]
        part_in = mm(buf_t[:, here], dh)
        part_out = mm(deo_t[:, here], hids[m][0])
        part_bias = jnp.sum(dh.astype(F32), axis=0, keepdims=True)
        grad_in = part_in if m == 0 else grad_in + part_in
        grad_out = part_out if m == 0 else grad_out + part_out
        bias_in = part_bias if m == 0 else bias_in + part_bias
    gin_ref[0, 0:width, :] = grad_in.astype(BF16)
    tail_id = lax.broadcasted_iota(jnp.int32, (16, ff), 0)
    tail = jnp.where(tail_id == 0, bias_in, 0.0)
    for i in range(width // ff):
        tail = jnp.where(tail_id == 1 + i, bias_s[0:1, i * ff : (i + 1) * ff], tail)
    gin_ref[0, width : width + 16, :] = tail.astype(BF16)
    gout_ref[0] = grad_out.astype(BF16)


def run_weight_grads(bufs, deos, hids, dhs, n_shard, ff):
    reps, rows, width = bufs[0].shape
    n_pieces = reps * n_shard
    per_rel = pl.BlockSpec((1, rows, width), lambda i: (i // n_shard, 0, 0))
    per_step = pl.BlockSpec((1, rows, ff), lambda i: (i // n_shard, 0, lax.rem(i, n_shard)))
    piece = lambda i: (lax.rem(i, n_shard) * reps + i // n_shard, 0, 0)
    return pl.pallas_call(
        functools.partial(weight_grad_kernel, (n_shard, width, ff)),
        grid=(n_pieces,),
        out_shape=(
            jax.ShapeDtypeStruct((n_pieces, width + 16, ff), BF16),
            jax.ShapeDtypeStruct((n_pieces, width, ff), BF16),
        ),
        in_specs=[per_rel] * 4 + [per_step] * 4,
        out_specs=(pl.BlockSpec((1, width + 16, ff), piece), pl.BlockSpec((1, width, ff), piece)),
        scratch_shapes=[
            pltpu.VMEM((width, 2 * rows), BF16),
            pltpu.VMEM((width, 2 * rows), BF16),
            pltpu.VMEM((1, width), F32),
        ],
        **plain(cost(8.0 * n_pieces * rows * ff * width, 40e6)),
    )(*bufs, *deos, *hids, *dhs)


def combine_kernel(dims, batch_ref, col_ref, gate0_ref, gate1_ref, mid0_ref, mid1_ref, eo0_ref, eo1_ref, out_ref):
    n_img, seq, pad, group, n_pos, reps, cap, cap_pad, n_exp = dims
    rows = group * pad
    msg = reps * cap_pad
    order = image_order(batch_ref, n_img)
    ids = lanes(rows, 128).astype(F32)
    along = lanes(rows, msg)
    for micro, gate_ref, mid_ref, eo_ref in ((0, gate0_ref, mid0_ref, eo0_ref), (1, gate1_ref, mid1_ref, eo1_ref)):
        table = col_ref[micro]
        gates = gate_ref[...]
        result = mid_ref[...]
        for lane in range(2):
            gate = jnp.sum(jnp.where(ids == table[:, lane : lane + 1], gates, 0.0), axis=1, keepdims=True)
            target = table[:, 2 + lane : 3 + lane]
            picked = None
            for pos in range(n_pos):
                chosen = ((along + pos * msg).astype(F32) == target).astype(F32).astype(BF16)
                part = mm(chosen, eo_ref[pos])
                picked = part if picked is None else picked + part
            result = result + gate * picked
        for n in range(group):
            out_ref[order[micro * group + n]] = result[n * pad : n * pad + seq, :].astype(BF16)


def backward_kernel(dims, micro, *refs):
    n_img, seq, pad, group, n_pos, reps, cap, cap_pad, n_exp = dims
    (batch_ref, tok_ref, cot_ref, full_ref, col_ref, a1_ref, qkv_ref, mix_ref, mid_ref, a2_ref, gate_ref, lse_ref,
     dbuf_ref) = refs[:13]
    refs = refs[13:]
    if micro > 0:
        prev_gtok_ref, prev_grad_ref = refs[:2]
        refs = refs[2:]
    gtok_ref, grad_ref, c_s, x_s, vec_s, dqkv_s, do_s = refs
    rows = group * pad
    msg = reps * cap_pad
    width = tok_ref.shape[-1]
    head = width // HEADS
    per_pair = 128 // head
    order = image_order(batch_ref, n_img)
    c = load_group(cot_ref, order, micro, group, seq, pad, c_s)
    x = load_group(tok_ref, order, micro, group, seq, pad, x_s)
    small = full_ref[:, 4 * width :]
    turned = small.astype(F32).T
    gain1 = turned[n_exp : n_exp + 1, :]
    gain2 = turned[n_exp + 2 : n_exp + 3, :]
    vec_s[...] = jnp.zeros(vec_s.shape, F32)

    table = col_ref[0]
    to1, to2 = table[:, 2:3], table[:, 3:4]
    along = lanes(rows, cap_pad)
    routed = None
    dg1 = jnp.zeros((rows, cap_pad), F32)
    dg2 = jnp.zeros((rows, cap_pad), F32)
    for pos in range(n_pos):
        for rel in range(reps):
            there = (along + (pos * msg + rel * cap_pad)).astype(F32)
            hit1 = there == to1
            hit2 = there == to2
            chosen = (hit1 | hit2).astype(F32).astype(BF16)
            part = mm(chosen, dbuf_ref[pos, rel * cap_pad : (rel + 1) * cap_pad, :])
            routed = part if routed is None else routed + part
            tail = dbuf_ref[pos, msg : msg + 16, 0:cap_pad].astype(F32)
            dgate = tail[2 * rel : 2 * rel + 1, :] + tail[2 * rel + 1 : 2 * rel + 2, :]
            dg1 = jnp.where(hit1, dgate, dg1)
            dg2 = jnp.where(hit2, dgate, dg2)
    dg1 = jnp.sum(dg1, axis=1, keepdims=True)
    dg2 = jnp.sum(dg2, axis=1, keepdims=True)
    ids = lanes(rows, 128).astype(F32)
    gates = gate_ref[...]
    dgates = jnp.where(ids == table[:, 0:1], dg1, 0.0) + jnp.where(ids == table[:, 1:2], dg2, 0.0)
    dlogits = (gates * (dgates - jnp.sum(gates * dgates, axis=1, keepdims=True))).astype(BF16)
    grad_small = mm_tn(a2_ref[...], dlogits)
    da2 = mm_nt(dlogits, small) + routed

    def norm_back(values, upstream, gain, at):
        normed, rate = norm_parts(values)
        vec_s[n_exp + at : n_exp + at + 1, :] = jnp.sum(upstream * normed, axis=0, keepdims=True)
        vec_s[n_exp + at + 1 : n_exp + at + 2, :] = jnp.sum(upstream, axis=0, keepdims=True)
        scaled = upstream * gain
        return rate * (
            scaled
            - jnp.mean(scaled, axis=-1, keepdims=True)
            - normed * jnp.mean(scaled * normed, axis=-1, keepdims=True)
        )

    dmid = c + norm_back(mid_ref[...], da2, gain2, 2)
    c_s[...] = dmid
    dbranch = dmid.astype(BF16)
    vec_s[n_exp + 6 : n_exp + 7, :] = jnp.sum(dbranch.astype(F32), axis=0, keepdims=True)
    grad_ref[:, 3 * width : 4 * width] = mm_tn(mix_ref[...], dbranch)
    do_s[...] = mm_nt(dbranch, full_ref[:, 3 * width : 4 * width]).astype(BF16)

    key_ok = lanes(pad, pad) < seq
    lane = lanes(pad, 128)
    scale = head ** (-0.5)
    for n in range(group):
        at = slice(n * pad, (n + 1) * pad)
        lse = lse_ref[at, :]
        for pair in range(width // 128):
            cols = pair * 128
            q2 = qkv_ref[at, cols : cols + 128]
            k2 = qkv_ref[at, width + cols : width + cols + 128]
            v2 = qkv_ref[at, 2 * width + cols : 2 * width + cols + 128]
            do2 = do_s[at, cols : cols + 128]
            dq2 = dk2 = dv2 = None
            for sub in range(per_pair):
                index = pair * per_pair + sub
                mine = (lane >= sub * head) & (lane < (sub + 1) * head)
                zero = jnp.zeros_like(q2)
                qh = jnp.where(mine, q2, zero)
                kh = jnp.where(mine, k2, zero)
                doh = jnp.where(mine, do2, zero)
                scores = jnp.where(key_ok, mm_nt(qh, k2), -jnp.inf)
                probs = jnp.exp(scores - lse[:, index : index + 1])
                dprobs = mm_nt(doh, v2)
                dscores = (probs * (dprobs - jnp.sum(probs * dprobs, axis=-1, keepdims=True))).astype(BF16)
                dv = mm_tn(probs.astype(BF16), doh)
                dq = mm(dscores, kh)
                dk = mm_tn(dscores, qh)
                dq2 = dq if dq2 is None else dq2 + dq
                dk2 = dk if dk2 is None else dk2 + dk
                dv2 = dv if dv2 is None else dv2 + dv
            dqkv_s[at, cols : cols + 128] = (dq2 * scale).astype(BF16)
            dqkv_s[at, width + cols : width + cols + 128] = dk2.astype(BF16)
            dqkv_s[at, 2 * width + cols : 2 * width + cols + 128] = dv2.astype(BF16)
    dqkv = dqkv_s[...]
    grad_ref[:, 0 : 3 * width] = mm_tn(a1_ref[...], dqkv)
    vec_s[n_exp + 4 : n_exp + 5, :] = jnp.sum(dqkv[:, 0:width].astype(F32), axis=0, keepdims=True)
    vec_s[n_exp + 5 : n_exp + 6, :] = jnp.sum(dqkv[:, 2 * width :].astype(F32), axis=0, keepdims=True)
    da1 = mm_nt(dqkv, full_ref[:, 0 : 3 * width])
    dx = c_s[...] + norm_back(x_s[...], da1, gain1, 0)
    if micro > 0:
        gtok_ref[...] = prev_gtok_ref[...]
    for n in range(group):
        gtok_ref[order[micro * group + n]] = dx[n * pad : n * pad + seq, :]
    grad_ref[:, 4 * width :] = grad_small + vec_s[...].T
    if micro > 0:
        grad_ref[...] += prev_grad_ref[...]


def on_device(
    tokens, cotangent, routes, batch_of_image, w_qkv, w_attn_out, w_router, norm1_gain, norm1_bias, norm2_gain,
    norm2_bias, bias_query, bias_value, bias_attn_out, w_expert_in, w_expert_out, bias_expert_in, bias_expert_out,
):
    n_img, seq, width = tokens.shape
    n_expert = lax.axis_size("expert")
    n_shard = lax.axis_size("shard")
    n_dev = n_expert * n_shard
    group = n_img // MICRO
    pad = round_up(seq, 16)
    rows = group * pad
    cap = 16 * group * seq // (5 * n_expert)
    cap_pad = round_up(cap, 16)
    reps = 2 if n_expert > 1 else 1
    n_pos = n_expert // reps
    msg = reps * cap_pad
    ff = w_expert_in.shape[2]
    dims = (n_img, seq, pad, group, n_pos, reps, cap, cap_pad, n_expert)
    my_expert = lax.axis_index("expert")
    my_shard = lax.axis_index("shard")
    half = (my_expert // n_pos).astype(jnp.int32).reshape(1)

    vectors = jnp.stack(
        [norm1_gain, norm1_bias, norm2_gain, norm2_bias, bias_query, bias_value, bias_attn_out], axis=1
    )
    blank = jnp.zeros((vectors.shape[0], 128 - n_expert - 7), BF16)
    packed = jnp.concatenate([w_qkv, w_attn_out, w_router, vectors, blank], axis=1)

    out_bias = lax.dynamic_update_slice(
        jnp.zeros((width,), BF16), bias_expert_out[0], (my_shard * (width // n_shard),)
    )
    tail = jnp.zeros((16, ff), BF16).at[0].set(bias_expert_in[0]).at[1 : 1 + width // ff].set(
        out_bias.reshape(width // ff, ff)
    )
    own_in = jnp.concatenate([w_expert_in[0], tail], axis=0)

    def swap(value, bit):
        return lax.ppermute(value, ("expert", "shard"), [(i, i ^ bit) for i in range(n_dev)])

    pieces = {0: (own_in, w_expert_out[0])}
    top = n_pos * n_shard
    steps = ([top] if reps > 1 else []) + [1 << i for i in range(n_shard.bit_length() - 1)][::-1]
    for bit in steps:
        for held in sorted(pieces):
            pieces[held + bit] = tuple(swap(member, bit) for member in pieces[held])
    ordered = [pieces[rel * top + s] for rel in range(reps) for s in range(n_shard)]

    groups = [[h * n_pos + i for i in range(n_pos)] for h in range(reps)]

    def exchange(value):
        return lax.all_to_all(
            value, "expert", split_axis=0, concat_axis=0, axis_index_groups=groups, tiled=True
        )

    cols, rws, csend = pl.pallas_call(
        functools.partial(route_kernel, dims[:-1]),
        out_shape=(
            jax.ShapeDtypeStruct((MICRO, rows, 128), F32),
            jax.ShapeDtypeStruct((MICRO, 8, round_up(rows, 128)), F32),
            jax.ShapeDtypeStruct((n_pos, MICRO * msg, width), BF16),
        ),
        in_specs=[SMEM_SPEC, SMEM_SPEC, VMEM_SPEC, VMEM_SPEC],
        out_specs=(VMEM_SPEC, VMEM_SPEC, VMEM_SPEC),
        scratch_shapes=[pltpu.VMEM((rows, width), F32), pltpu.VMEM((rows, 128), jnp.int32)],
        **plain(cost(4.0 * n_pos * msg * rows * width, 8e6)),
    )(batch_of_image, half, routes, cotangent)
    cots = exchange(csend)

    full = gather_params(packed, n_expert, n_shard, 0)

    col_spec = lambda micro: pl.BlockSpec((1, rows, 128), lambda i: (micro, 0, 0))
    row_spec = lambda micro: pl.BlockSpec((1, 8, round_up(rows, 128)), lambda i: (micro, 0, 0))
    whole = lambda array: pl.BlockSpec(array.shape, lambda i: (0,) * len(array.shape))
    states = []
    for micro in range(MICRO):
        shapes = (
            jax.ShapeDtypeStruct((rows, width), BF16),
            jax.ShapeDtypeStruct((rows, 3 * width), BF16),
            jax.ShapeDtypeStruct((rows, width), BF16),
            jax.ShapeDtypeStruct((rows, width), F32),
            jax.ShapeDtypeStruct((rows, width), BF16),
            jax.ShapeDtypeStruct((rows, 128), F32),
            jax.ShapeDtypeStruct((rows, 128), F32),
            jax.ShapeDtypeStruct((n_pos, msg + 16, width), BF16),
        )
        states.append(
            pl.pallas_call(
                functools.partial(forward_kernel, dims, micro),
                grid=(1,),
                out_shape=shapes,
                in_specs=[SMEM_SPEC, whole(tokens), whole(full), col_spec(micro), row_spec(micro)],
                out_specs=tuple(whole(s) for s in shapes),
                scratch_shapes=[pltpu.VMEM((rows, width), F32)],
                **plain(cost(8.0 * rows * width * width + 2.0 * n_pos * msg * rows * width, 10e6, 2e6)),
            )(batch_of_image, tokens, full, cols, rws)
        )
    arrived = [exchange(state[7]) for state in states]

    expert = []
    for micro in range(MICRO):
        expert.append(run_expert(arrived[micro], cots, micro, ordered, n_pos, reps, n_shard, cap_pad))
    dbufs = [exchange(result[1]) for result in expert]
    outs = [exchange(result[0]) for result in expert]
    grad_in, grad_out = run_weight_grads(
        [e[5] for e in expert], [e[4] for e in expert], [e[2] for e in expert], [e[3] for e in expert], n_shard, ff
    )

    def reduce_pieces(pieces_all):
        for bit in [1 << i for i in range(n_shard.bit_length() - 1)] + ([top] if reps > 1 else []):
            if bit == top and reps > 1:
                mine, theirs = pieces_all[0::2], pieces_all[1::2]
            else:
                split = pieces_all.reshape((-1, 2, reps) + pieces_all.shape[1:])
                mine = split[:, 0].reshape((-1,) + pieces_all.shape[1:])
                theirs = split[:, 1].reshape((-1,) + pieces_all.shape[1:])
            pieces_all = (mine.astype(F32) + swap(theirs, bit).astype(F32)).astype(BF16)
        return pieces_all[0].astype(F32)

    own_grad_in = reduce_pieces(grad_in)
    own_grad_out = reduce_pieces(grad_out)

    gtok = grad = None
    for micro in range(MICRO):
        a1, qkv, mix, mid, a2, gate, lse, _ = states[micro]
        operands = [batch_of_image, tokens, cotangent, full, cols, a1, qkv, mix, mid, a2, gate, lse, dbufs[micro]]
        specs = [SMEM_SPEC] + [whole(o) for o in operands[1:4]] + [col_spec(micro)] + [whole(o) for o in operands[5:]]
        if micro > 0:
            operands += [gtok, grad]
            specs += [whole(gtok), whole(grad)]
        shapes = (
            jax.ShapeDtypeStruct((n_img, seq, width), F32),
            jax.ShapeDtypeStruct((width, 4 * width + 128), F32),
        )
        gtok, grad = pl.pallas_call(
            functools.partial(backward_kernel, dims, micro),
            grid=(1,),
            out_shape=shapes,
            in_specs=specs,
            out_specs=tuple(whole(s) for s in shapes),
            scratch_shapes=[
                pltpu.VMEM((rows, width), F32),
                pltpu.VMEM((rows, width), F32),
                pltpu.VMEM((128, width), F32),
                pltpu.VMEM((rows, 3 * width), BF16),
                pltpu.VMEM((rows, width), BF16),
            ],
            **plain(cost(20.0 * rows * width * width + 2.0 * n_pos * msg * rows * width, 16e6, 1e6)),
        )(*operands)

    layer_out = pl.pallas_call(
        functools.partial(combine_kernel, dims),
        out_shape=jax.ShapeDtypeStruct((n_img, seq, width), BF16),
        in_specs=[SMEM_SPEC] + [VMEM_SPEC] * 7,
        out_specs=VMEM_SPEC,
        **plain(cost(8.0 * n_pos * msg * rows * width, 8e6)),
    )(batch_of_image, cols, states[0][5], states[1][5], states[0][3], states[1][3], outs[0], outs[1])

    mine = scatter_params(grad, n_expert, n_shard, 1)
    tail = own_grad_in[width:, :]
    out_bias_grad = tail[1 : 1 + width // ff, :].reshape(width)
    small = mine[:, 4 * width :]
    vec = [small[:, n_expert + i] for i in range(7)]
    return (
        layer_out,
        gtok,
        mine[:, 0 : 3 * width],
        mine[:, 3 * width : 4 * width],
        small[:, 0:n_expert],
        *vec,
        own_grad_in[0:width, :][None],
        own_grad_out.T[None],
        tail[0:1, :],
        lax.dynamic_slice(out_bias_grad, (my_shard * (width // n_shard),), (width // n_shard,))[None],
    )


def solution(mesh):
    both = ("expert", "shard")
    placed = (
        (P(both, None, None),) * 3
        + (P(both),)
        + (P(both, None),) * 3
        + (P(both),) * 7
        + (P("expert", None, "shard"), P("expert", "shard", None), P("expert", "shard"), P("expert", "shard"))
    )
    return jax.shard_map(
        on_device,
        mesh=mesh,
        in_specs=placed,
        out_specs=(P(both, None, None),) * 2
        + (P(both, None),) * 3
        + (P(both),) * 7
        + (P("expert", None, "shard"), P("expert", "shard", None), P("expert", "shard"), P("expert", "shard")),
        check_vma=False,
    )
```

```python
import functools
import math

import jax
import jax.numpy as jnp
from jax import lax
from jax.experimental import pallas as pl
from jax.experimental.pallas import tpu as pltpu
from jax.sharding import PartitionSpec as P

HEADS = 8
MICRO = 2
EPS = 1e-06
F32 = jnp.float32
BF16 = jnp.bfloat16
MESH = pl.DeviceIdType.MESH
VMEM_LIMIT = 56 * 1024 * 1024
VMEM_SPEC = pl.BlockSpec(memory_space=pltpu.VMEM)
SMEM_SPEC = pl.BlockSpec(memory_space=pltpu.SMEM)
ANY_SPEC = pl.BlockSpec(memory_space=pl.ANY)


def round_up(value, unit):
    return (value + unit - 1) // unit * unit


def mm(left, right):
    return lax.dot_general(left, right, (((1,), (0,)), ((), ())), preferred_element_type=F32)


def mm_nt(left, right):
    return lax.dot_general(left, right, (((1,), (1,)), ((), ())), preferred_element_type=F32)


def mm_tn(left, right):
    return lax.dot_general(left, right, (((0,), (0,)), ((), ())), preferred_element_type=F32)


def cost(flops, nbytes, trans=0):
    return pl.CostEstimate(flops=int(flops), bytes_accessed=int(nbytes), transcendentals=int(trans))


def plain(name_cost):
    return dict(
        cost_estimate=name_cost,
        compiler_params=pltpu.CompilerParams(vmem_limit_bytes=VMEM_LIMIT),
    )


def image_order(batch_ref, n_img):
    keys = [batch_ref[i] * n_img + i for i in range(n_img)]
    ranks = []
    for i in range(n_img):
        rank = jnp.int32(0)
        for j in range(n_img):
            if j != i:
                rank = rank + jnp.where(keys[j] < keys[i], 1, 0)
        ranks.append(rank)
    order = []
    for k in range(n_img):
        place = jnp.int32(0)
        for i in range(n_img):
            place = place + jnp.where(ranks[i] == k, i, 0)
        order.append(place)
    return order


def flip(index, bit):
    return index + bit - 2 * bit * lax.rem(index // bit, 2)


def lanes(rows, width):
    return lax.broadcasted_iota(jnp.int32, (rows, width), 1)


def bit_orders(n_expert, n_shard):
    shard_bits = [1 << i for i in range(n_shard.bit_length() - 1)]
    expert_bits = [n_shard << i for i in range(n_expert.bit_length() - 1)]
    core = shard_bits[:1]
    across = shard_bits[1:]
    first = expert_bits[::-1] + across[::-1] + core
    second = across[::-1] + expert_bits[:0:-1] + expert_bits[:1] + core
    return first, second


def combos(bits):
    result = [0]
    for bit in bits:
        result = result + [held + bit for held in result]
    return result


def flip_all(index, combo):
    bit = 1
    while bit <= combo:
        if combo & bit:
            index = flip(index, bit)
        bit *= 2
    return index


def greet(me, bits, n_shard):
    barrier = pltpu.get_barrier_semaphore()
    for bit in bits:
        peer = flip(me, bit)
        pl.semaphore_signal(
            barrier, inc=1, device_id=(peer // n_shard, lax.rem(peer, n_shard)), device_id_type=MESH
        )
    pl.semaphore_wait(barrier, len(bits))


def gather_kernel(n_shard, orders, cuts, mine_ref, full_ref, local_sem, send_sems, recv_sems):
    me = lax.axis_index("expert") * n_shard + lax.axis_index("shard")
    greet(me, orders[0], n_shard)
    own = pltpu.make_async_copy(mine_ref, full_ref.at[me], local_sem)
    own.start()
    copies = []
    for step in range(len(orders[0])):
        started = []
        for part, order in enumerate(orders):
            bit = order[step]
            peer = flip(me, bit)
            low, high = cuts[part]
            for at, combo in enumerate(combos(order[:step])):
                chunk = flip_all(me, combo)
                source = mine_ref if combo == 0 else full_ref.at[chunk]
                copy = pltpu.make_async_remote_copy(
                    src_ref=source.at[:, low:high],
                    dst_ref=full_ref.at[chunk, :, low:high],
                    send_sem=send_sems.at[part, (1 << step) - 1 + at],
                    recv_sem=recv_sems.at[part, (1 << step) - 1 + at],
                    device_id=(peer // n_shard, lax.rem(peer, n_shard)),
                    device_id_type=MESH,
                )
                copy.start()
                started.append(copy)
        for copy in started:
            copy.wait_recv()
        copies.extend(started)
    for copy in copies:
        copy.wait_send()
    own.wait()


def gather_params(packed, n_expert, n_shard, collective_id):
    rows, width = packed.shape
    n_dev = n_expert * n_shard
    orders = bit_orders(n_expert, n_shard)
    middle = width // 256 * 128
    cuts = ((0, middle), (middle, width))
    full = pl.pallas_call(
        functools.partial(gather_kernel, n_shard, orders, cuts),
        out_shape=jax.ShapeDtypeStruct((n_dev, rows, width), packed.dtype),
        in_specs=[VMEM_SPEC],
        out_specs=VMEM_SPEC,
        scratch_shapes=[
            pltpu.SemaphoreType.DMA,
            pltpu.SemaphoreType.DMA((2, n_dev - 1)),
            pltpu.SemaphoreType.DMA((2, n_dev - 1)),
        ],
        compiler_params=pltpu.CompilerParams(
            collective_id=collective_id, has_side_effects=True, vmem_limit_bytes=VMEM_LIMIT
        ),
        cost_estimate=cost(1e6, 4 * n_dev * rows * width),
    )(packed)
    return full.reshape(n_dev * rows, width)


def scatter_kernel(n_shard, orders, cuts, full_ref, out_ref, acc, sends, recvs, send_sems, recv_sems):
    me = lax.axis_index("expert") * n_shard + lax.axis_index("shard")
    n_dev = full_ref.shape[0]
    greet(me, orders[0], n_shard)
    n_steps = len(orders[0])
    acc[...] = full_ref[...]
    copies = []
    for step in range(n_steps):
        started = []
        base = n_dev - (n_dev >> step)
        count = n_dev >> (step + 1)
        for part, order in enumerate(orders):
            bit = order[step]
            peer = flip(me, bit)
            low, high = cuts[part]
            for at, combo in enumerate(combos(order[step + 1 :])):
                chunk = flip_all(peer, combo)
                sends[base + at, :, low:high] = acc[chunk, :, low:high].astype(BF16)
            copy = pltpu.make_async_remote_copy(
                src_ref=sends.at[base : base + count, :, low:high],
                dst_ref=recvs.at[base : base + count, :, low:high],
                send_sem=send_sems.at[part, step],
                recv_sem=recv_sems.at[part, step],
                device_id=(peer // n_shard, lax.rem(peer, n_shard)),
                device_id_type=MESH,
            )
            copy.start()
            started.append(copy)
        for part, order in enumerate(orders):
            low, high = cuts[part]
            started[part].wait_recv()
            for at, combo in enumerate(combos(order[step + 1 :])):
                chunk = flip_all(me, combo)
                acc[chunk, :, low:high] += recvs[base + at, :, low:high].astype(F32)
        copies.extend(started)
    out_ref[...] = acc[me]
    for copy in copies:
        copy.wait_send()


def scatter_params(full, n_expert, n_shard, collective_id):
    n_dev = n_expert * n_shard
    width = full.shape[1]
    rows = full.shape[0] // n_dev
    gather_orders = bit_orders(n_expert, n_shard)
    orders = [order[::-1] for order in gather_orders]
    middle = width // 256 * 128
    cuts = ((0, middle), (middle, width))
    return pl.pallas_call(
        functools.partial(scatter_kernel, n_shard, orders, cuts),
        out_shape=jax.ShapeDtypeStruct((rows, width), F32),
        in_specs=[VMEM_SPEC],
        out_specs=VMEM_SPEC,
        scratch_shapes=[
            pltpu.VMEM((n_dev, rows, width), F32),
            pltpu.VMEM((n_dev, rows, width), BF16),
            pltpu.VMEM((n_dev, rows, width), BF16),
            pltpu.SemaphoreType.DMA((2, len(orders[0]))),
            pltpu.SemaphoreType.DMA((2, len(orders[0]))),
        ],
        compiler_params=pltpu.CompilerParams(
            collective_id=collective_id, has_side_effects=True, vmem_limit_bytes=VMEM_LIMIT
        ),
        cost_estimate=cost(1e6, 8 * n_dev * rows * width),
    )(full.reshape(n_dev, rows, width))


def route_tables(dims, rt_s):
    n_img, seq, pad, group, n_pos, reps, cap, cap_pad, n_exp = dims
    rows = group * pad
    msg = reps * cap_pad
    lower = (
        lax.broadcasted_iota(jnp.int32, (rows, rows), 0)
        > lax.broadcasted_iota(jnp.int32, (rows, rows), 1)
    ).astype(F32).astype(BF16)
    ids = lanes(rows, 128)
    me = lax.axis_index("expert")
    first = rt_s[:, 0:1]
    second = rt_s[:, 1:2]
    hot_first = (ids == first).astype(F32)
    hot_second = (ids == second).astype(F32)
    earlier_first = mm(lower, hot_first.astype(BF16))
    earlier_second = mm(lower, hot_second.astype(BF16)) + jnp.sum(hot_first, axis=0, keepdims=True)
    table = jnp.where(ids == 0, first.astype(F32), jnp.where(ids == 1, second.astype(F32), 0.0))
    for lane, route, hot, earlier in (
        (2, first, hot_first, earlier_first),
        (3, second, hot_second, earlier_second),
    ):
        slot = jnp.sum(hot * earlier, axis=1, keepdims=True)
        away = jnp.bitwise_xor(jnp.maximum(route, 0), jnp.broadcast_to(me, route.shape)).astype(F32)
        rel = (away >= float(n_pos)).astype(F32)
        target = (away - rel * float(n_pos)) * float(msg) + rel * float(cap_pad) + slot
        target = jnp.where((slot < float(cap)) & (route >= 0), target, -1.0)
        table = jnp.where(ids == lane, target, table)
    spare = round_up(rows, 128) - rows
    turned = jnp.concatenate([table, jnp.full((spare, 128), -1.0, F32)], axis=0).T
    return table, turned[2:3, 0:rows], turned[3:4, 0:rows]


def norm_parts(values):
    center = values - jnp.mean(values, axis=-1, keepdims=True)
    rate = lax.rsqrt(jnp.mean(center * center, axis=-1, keepdims=True) + EPS)
    return center * rate, rate


def load_group(ref, order, micro, group, seq, pad, buf):
    buf[...] = jnp.zeros(buf.shape, F32)
    for n in range(group):
        buf[n * pad : n * pad + seq, :] = ref[order[micro * group + n]].astype(F32)
    return buf[...]


def attention_forward(dims, x, full_ref, out):
    n_img, seq, pad, group, n_pos, reps, cap, cap_pad, n_exp = dims
    a1_ref, qkv_ref, mix_ref, mid_ref, a2_ref, gate_ref, lse_ref = out
    rows = group * pad
    width = x.shape[-1]
    head = width // HEADS
    per_pair = 128 // head
    small = full_ref[:, 4 * width :]
    turned = small.astype(F32).T
    gain1, shift1, gain2, shift2, bias_q, bias_v, bias_o = [
        turned[n_exp + i : n_exp + i + 1, :] for i in range(7)
    ]
    normed, _ = norm_parts(x)
    a1 = (normed * gain1 + shift1).astype(BF16)
    a1_ref[...] = a1
    proj = mm(a1, full_ref[:, 0 : 3 * width])
    scale = head ** (-0.5)
    qkv_ref[:, 0:width] = ((proj[:, 0:width] + bias_q).astype(BF16).astype(F32) * scale).astype(BF16)
    qkv_ref[:, width : 2 * width] = proj[:, width : 2 * width].astype(BF16)
    qkv_ref[:, 2 * width :] = (proj[:, 2 * width :] + bias_v).astype(BF16)
    key_ok = lanes(pad, pad) < seq
    lane = lanes(pad, 128)
    for n in range(group):
        at = slice(n * pad, (n + 1) * pad)
        lse = jnp.zeros((pad, 128), F32)
        for pair in range(width // 128):
            cols = pair * 128
            q2 = qkv_ref[at, cols : cols + 128]
            k2 = qkv_ref[at, width + cols : width + cols + 128]
            v2 = qkv_ref[at, 2 * width + cols : 2 * width + cols + 128]
            mixed = None
            for sub in range(per_pair):
                mine = (lane >= sub * head) & (lane < (sub + 1) * head)
                scores = mm_nt(jnp.where(mine, q2, jnp.zeros_like(q2)), k2)
                scores = jnp.where(key_ok, scores, -jnp.inf)
                top = jnp.max(scores, axis=-1, keepdims=True)
                grown = jnp.exp(scores - top)
                total = jnp.sum(grown, axis=-1, keepdims=True)
                probs = (grown / total).astype(BF16)
                part = mm(probs, jnp.where(mine, v2, jnp.zeros_like(v2)))
                mixed = part if mixed is None else mixed + part
                lse = jnp.where(lane == pair * per_pair + sub, top + jnp.log(total), lse)
            mix_ref[at, cols : cols + 128] = mixed.astype(BF16)
        lse_ref[at, :] = lse
    mid = x + mm(mix_ref[...], full_ref[:, 3 * width : 4 * width]) + bias_o
    mid_ref[...] = mid
    normed2, _ = norm_parts(mid)
    a2 = (normed2 * gain2 + shift2).astype(BF16)
    a2_ref[...] = a2
    ids = lanes(rows, 128)
    logits = jnp.where(ids < n_exp, mm(a2, small), -jnp.inf)
    grown = jnp.exp(logits - jnp.max(logits, axis=-1, keepdims=True))
    gates = grown / jnp.sum(grown, axis=-1, keepdims=True)
    gate_ref[...] = gates


def fill_message(dims, pos, table, gates, a2, chosen, send_ref):
    n_img, seq, pad, group, n_pos, reps, cap, cap_pad, n_exp = dims
    rows = group * pad
    msg = reps * cap_pad
    width = a2.shape[-1]
    ids = lanes(rows, 128).astype(F32)
    gate1 = jnp.sum(jnp.where(ids == table[:, 0:1], gates, 0.0), axis=1, keepdims=True)
    gate2 = jnp.sum(jnp.where(ids == table[:, 1:2], gates, 0.0), axis=1, keepdims=True)
    to1, to2 = table[:, 2:3], table[:, 3:4]
    along = lanes(rows, cap_pad)
    send_ref[0:msg, :] = mm(chosen, a2).astype(BF16)
    send_ref[msg : msg + 16, :] = jnp.zeros((16, width), BF16)
    tail = jnp.zeros((16, cap_pad), F32)
    tail_id = lax.broadcasted_iota(jnp.int32, (16, cap_pad), 0)
    for rel in range(reps):
        there = (along + (pos * msg + rel * cap_pad)).astype(F32)
        gate_row = jnp.sum(
            jnp.where(there == to1, gate1, 0.0) + jnp.where(there == to2, gate2, 0.0), axis=0, keepdims=True
        )
        high = gate_row.astype(BF16).astype(F32)
        tail = jnp.where(tail_id == 2 * rel, high, jnp.where(tail_id == 2 * rel + 1, gate_row - high, tail))
    send_ref[msg : msg + 16, 0:cap_pad] = tail.astype(BF16)


def first_kernel(dims, n_shard, orders, cuts, gathered, *refs):
    n_img, seq, pad, group, n_pos, reps, cap, cap_pad, n_exp = dims
    (batch_ref, routes_ref, tok_ref, cot_ref, packed_ref, own_in_ref, own_out_ref) = refs[:7]
    refs = refs[7:]
    col_ref, full_out, win_ref, wout_ref, ain_ref, cin_ref = refs[:6]
    states = (refs[6:13], refs[13:20])
    (x_s, rt_s, chosen_s, asend, csend, local_sems, gsend, grecv, wsend, wrecv, dsend, drecv) = refs[20:]
    full_ref = packed_ref if gathered else full_out
    rows = group * pad
    msg = reps * cap_pad
    n_pieces = reps * n_shard
    top = n_pos * n_shard
    expert, shard = lax.axis_index("expert"), lax.axis_index("shard")
    me = expert * n_shard + shard

    def place(index):
        return (index // n_shard, lax.rem(index, n_shard))

    peers = sorted(set(orders[0]) | {pos * n_shard for pos in range(1, n_pos)})
    barrier = pltpu.get_barrier_semaphore()
    for peer in peers:
        pl.semaphore_signal(barrier, inc=1, device_id=place(flip_all(me, peer)), device_id_type=MESH)
    pl.semaphore_wait(barrier, len(peers))

    chunk_rows = full_ref.shape[0] // (n_exp * n_shard) if not gathered else 0
    gather_copies = []

    def at_chunk(ref, index, low, high):
        return ref.at[pl.ds(pl.multiple_of(index * chunk_rows, chunk_rows), chunk_rows), low:high]

    def gather_start(step):
        for part, order in enumerate(orders):
            low, high = cuts[part]
            for at, combo in enumerate(combos(order[:step])):
                chunk = flip_all(me, combo)
                source = packed_ref.at[:, low:high] if combo == 0 else at_chunk(full_ref, chunk, low, high)
                sem = (1 << step) - 1 + at
                copy = pltpu.make_async_remote_copy(
                    src_ref=source,
                    dst_ref=at_chunk(full_ref, chunk, low, high),
                    send_sem=gsend.at[part, sem],
                    recv_sem=grecv.at[part, sem],
                    device_id=place(flip(me, order[step])),
                    device_id_type=MESH,
                )
                copy.start()
                gather_copies.append(copy)

    def gather_next(step):
        if gathered:
            return
        count = 2 * (1 << step)
        for copy in gather_copies[-count:]:
            copy.wait_recv()
        if step + 1 < len(orders[0]):
            gather_start(step + 1)

    local = []
    if not gathered:
        gather_start(0)
        own = pltpu.make_async_copy(packed_ref, at_chunk(full_ref, me, 0, full_ref.shape[1]), local_sems.at[0])
        own.start()
        local.append(own)

    bits = ([top] if reps > 1 else []) + [1 << i for i in range(n_shard.bit_length() - 1)][::-1]

    def number(held):
        return (held // top) * n_shard + held % top

    weight_copies = {}

    def weights_start(kind, held, bit):
        source = ((own_in_ref, own_out_ref)[kind]) if held == 0 else (win_ref, wout_ref)[kind].at[number(held)]
        to = number(held + bit)
        copy = pltpu.make_async_remote_copy(
            src_ref=source,
            dst_ref=(win_ref, wout_ref)[kind].at[to],
            send_sem=wsend.at[kind, to],
            recv_sem=wrecv.at[kind, to],
            device_id=place(flip(me, bit)),
            device_id_type=MESH,
        )
        copy.start()
        weight_copies[kind, held + bit] = copy

    def weights_pass(kind, held):
        weight_copies[kind, held].wait_recv()
        last = min(bit for bit in bits if held & bit)
        for bit in bits:
            if bit < last:
                weights_start(kind, held, bit)

    for bit in bits:
        for kind in range(2):
            weights_start(kind, 0, bit)
    for kind, source in enumerate((own_in_ref, own_out_ref)):
        copy = pltpu.make_async_copy(source, (win_ref, wout_ref)[kind].at[0], local_sems.at[1 + kind])
        copy.start()
        local.append(copy)

    order = image_order(batch_ref, n_img)
    sent = []

    def dispatch(source, target, kind, micro):
        for pos in range(1, n_pos):
            copy = pltpu.make_async_remote_copy(
                src_ref=source.at[pos],
                dst_ref=target.at[micro, pos],
                send_sem=dsend.at[kind, micro, pos],
                recv_sem=drecv.at[kind, micro, pos],
                device_id=place(flip_all(me, pos * n_shard)),
                device_id_type=MESH,
            )
            copy.start()
            sent.append(copy)
        copy = pltpu.make_async_copy(source.at[0], target.at[micro, 0], dsend.at[kind, micro, 0])
        copy.start()
        local.append(copy)

    n_steps = len(orders[0])
    step = 0
    tables = []
    for micro in range(MICRO):
        rt_s[...] = jnp.full(rt_s.shape, -1, jnp.int32)
        for n in range(group):
            rt_s[n * pad : n * pad + seq, 0:2] = routes_ref[order[micro * group + n]]
        table, row_first, row_second = route_tables(dims, rt_s)
        col_ref[micro] = table
        if step < n_steps:
            gather_next(step)
            step += 1
        cot = load_group(cot_ref, order, micro, group, seq, pad, x_s).astype(BF16)
        slots = lax.broadcasted_iota(jnp.int32, (msg, rows), 0)
        for pos in range(n_pos):
            here = (slots + pos * msg).astype(F32)
            chosen = ((here == row_first) | (here == row_second)).astype(F32).astype(BF16)
            chosen_s[micro, pos] = chosen
            csend[micro, pos] = mm(chosen, cot).astype(BF16)
        dispatch(csend.at[micro], cin_ref, 0, micro)
        if step < n_steps:
            gather_next(step)
            step += 1
    while step < n_steps:
        gather_next(step)
        step += 1
    if not gathered:
        local[0].wait()
    inner = sorted((held for held in combos(bits) if held and not held & 1), key=lambda h: (-(h & -h), h))
    early = [held for held in inner if held < top]
    late = [held for held in inner if held > top]
    for micro in range(MICRO):
        x = load_group(tok_ref, order, micro, group, seq, pad, x_s)
        attention_forward(dims, x, full_ref, states[micro])
        table = col_ref[micro]
        gates = states[micro][5][...]
        a2 = states[micro][4][...]
        for pos in range(n_pos):
            fill_message(dims, pos, table, gates, a2, chosen_s[micro, pos], asend.at[micro, pos])
        dispatch(asend.at[micro], ain_ref, 1, micro)
        if micro == 0:
            for held in early:
                for kind in range(2):
                    weights_pass(kind, held)
            if reps > 1:
                weights_pass(0, top)
        elif reps > 1:
            weights_pass(1, top)
    for held in late:
        for kind in range(2):
            weights_pass(kind, held)
    for (kind, held), copy in weight_copies.items():
        if held & 1:
            copy.wait_recv()
    for copy in sent:
        copy.wait()
    for copy in local[1 if not gathered else 0 :]:
        copy.wait()
    for copy in gather_copies:
        copy.wait_send()
    for copy in weight_copies.values():
        copy.wait_send()


def run_first(dims, n_shard, batch, routes, tokens, cotangent, packed, own_in, own_out):
    n_img, seq, pad, group, n_pos, reps, cap, cap_pad, n_exp = dims
    width = tokens.shape[-1]
    rows = group * pad
    msg = reps * cap_pad
    n_dev = n_exp * n_shard
    n_pieces = reps * n_shard
    total = packed.shape[1]
    orders = bit_orders(n_exp, n_shard)
    middle = total // 256 * 128
    cuts = ((0, middle), (middle, total))
    gathered = packed.shape[0] % 16 != 0
    if gathered:
        packed = gather_params(packed, n_exp, n_shard, 3)
    state = (
        jax.ShapeDtypeStruct((rows, width), BF16),
        jax.ShapeDtypeStruct((rows, 3 * width), BF16),
        jax.ShapeDtypeStruct((rows, width), BF16),
        jax.ShapeDtypeStruct((rows, width), F32),
        jax.ShapeDtypeStruct((rows, width), BF16),
        jax.ShapeDtypeStruct((rows, 128), F32),
        jax.ShapeDtypeStruct((rows, 128), F32),
    )
    full_rows = 16 if gathered else n_dev * packed.shape[0]
    out = pl.pallas_call(
        functools.partial(first_kernel, dims, n_shard, orders, cuts, gathered),
        out_shape=(
            jax.ShapeDtypeStruct((MICRO, rows, 128), F32),
            jax.ShapeDtypeStruct((full_rows, total), BF16),
            jax.ShapeDtypeStruct((n_pieces,) + own_in.shape, BF16),
            jax.ShapeDtypeStruct((n_pieces,) + own_out.shape, BF16),
            jax.ShapeDtypeStruct((MICRO, n_pos, msg + 16, width), BF16),
            jax.ShapeDtypeStruct((MICRO, n_pos, msg, width), BF16),
            *state,
            *state,
        ),
        in_specs=[SMEM_SPEC] + [VMEM_SPEC] * 4 + [ANY_SPEC] * 2,
        out_specs=(VMEM_SPEC, VMEM_SPEC, ANY_SPEC, ANY_SPEC, ANY_SPEC, ANY_SPEC) + (VMEM_SPEC,) * 14,
        scratch_shapes=[
            pltpu.VMEM((rows, width), F32),
            pltpu.VMEM((rows, 128), jnp.int32),
            pltpu.VMEM((MICRO, n_pos, msg, rows), BF16),
            pltpu.VMEM((MICRO, n_pos, msg + 16, width), BF16),
            pltpu.VMEM((MICRO, n_pos, msg, width), BF16),
            pltpu.SemaphoreType.DMA((3,)),
            pltpu.SemaphoreType.DMA((2, n_dev - 1)),
            pltpu.SemaphoreType.DMA((2, n_dev - 1)),
            pltpu.SemaphoreType.DMA((2, n_pieces)),
            pltpu.SemaphoreType.DMA((2, n_pieces)),
            pltpu.SemaphoreType.DMA((2, MICRO, n_pos)),
            pltpu.SemaphoreType.DMA((2, MICRO, n_pos)),
        ],
        compiler_params=pltpu.CompilerParams(
            collective_id=0, has_side_effects=True, vmem_limit_bytes=VMEM_LIMIT
        ),
        cost_estimate=cost(20e9, 60e6, 4e6),
    )(batch, routes, tokens, cotangent, packed, own_in, own_out)
    cols, full, win, wout, ain, cin = out[:6]
    return cols, packed if gathered else full, win, wout, ain, cin, out[6:13], out[13:20]


def gelu_pair(v):
    size = jnp.abs(v)
    bell = jnp.exp(v * v * -0.5)
    t = 1.0 / (1.0 + (0.3275911 / math.sqrt(2.0)) * size)
    series = t * (
        0.5 * 0.254829592
        + t * (0.5 * -0.284496736 + t * (0.5 * 1.421413741 + t * (0.5 * -1.453152027 + t * (0.5 * 1.061405429))))
    )
    tail = series * bell
    share = jnp.where(v >= 0.0, 1.0 - tail, tail)
    return v * share, share + v * bell * (1.0 / math.sqrt(2.0 * math.pi))


def expert_kernel(dims, *refs):
    n_pos, reps, n_shard, cap_pad, width, ff, tail_rows = dims
    n_pieces = reps * n_shard
    win_ref, wout_ref = refs[:2]
    (a_ref, c_ref, eo_ref, dbuf_ref, hid_ref, dh_ref, deo_ref, buf_ref) = refs[2:10]
    (win, wout, pre, back, eo_acc, db_acc, bias_acc, sem_in, sem_out) = refs[10:]
    step = pl.program_id(0)
    shard = lax.rem(step, n_shard)
    rel = step // n_shard
    msg = reps * cap_pad
    rows = n_pos * cap_pad

    @pl.when(step == 0)
    def _():
        for i in range(n_pieces):
            pltpu.make_async_copy(win_ref.at[i], win.at[i], sem_in.at[i]).start()
            pltpu.make_async_copy(wout_ref.at[i], wout.at[i], sem_out.at[i]).start()
        eo_ref[...] = jnp.zeros(eo_ref.shape, BF16)
        dbuf_ref[...] = jnp.zeros(dbuf_ref.shape, BF16)

    @pl.when(shard == 0)
    def _():
        bias_acc[...] = jnp.zeros(bias_acc.shape, F32)
        tails = jnp.concatenate([a_ref[0, p, msg : msg + 16, :].astype(F32) for p in range(n_pos)], axis=0)
        pad_rows = round_up(n_pos * 16, 128) - n_pos * 16
        if pad_rows:
            tails = jnp.concatenate([tails, jnp.zeros((pad_rows, width), F32)], axis=0)
        turned = tails.T
        for r in range(reps):

            @pl.when(rel == r)
            def _():
                for p in range(n_pos):
                    there = slice(p * cap_pad, (p + 1) * cap_pad)
                    gate = (
                        turned[0:cap_pad, p * 16 + 2 * r : p * 16 + 2 * r + 1]
                        + turned[0:cap_pad, p * 16 + 2 * r + 1 : p * 16 + 2 * r + 2]
                    )
                    buf_ref[0, there, :] = a_ref[0, p, r * cap_pad : (r + 1) * cap_pad, :]
                    cot = c_ref[0, p, r * cap_pad : (r + 1) * cap_pad, :].astype(F32)
                    deo_ref[0, there, :] = (cot * gate).astype(BF16)

    for i in range(n_pieces):

        @pl.when(step == i)
        def _():
            pltpu.make_async_copy(win_ref.at[i], win.at[i], sem_in.at[i]).wait()
            pltpu.make_async_copy(wout_ref.at[i], wout.at[i], sem_out.at[i]).wait()

    buf = buf_ref[0]
    deo = deo_ref[0]
    w_in = win[step, 0:width, :]
    w_out = wout[step]
    bias_in = win[step, width : width + 16, :].astype(F32)
    pre[...] = mm(buf, w_in) + bias_in[0:1, :]
    back[...] = mm_nt(deo, w_out)
    for p in range(n_pos):
        there = slice(p * cap_pad, (p + 1) * cap_pad)
        value, slope = gelu_pair(pre[there, :])
        hid_ref[0, there, :] = value.astype(BF16)
        dh_ref[0, there, :] = (back[there, :] * slope).astype(BF16)
    eo_part = mm(hid_ref[0], w_out)
    db_part = mm_nt(dh_ref[0], w_in)
    bias_acc[...] += jnp.concatenate([bias_in[1 + i : 2 + i, :] for i in range(width // ff)], axis=1)

    @pl.when(shard == 0)
    def _():
        eo_acc[...] = eo_part
        db_acc[...] = db_part

    @pl.when(shard > 0)
    def _():
        eo_acc[...] += eo_part
        db_acc[...] += db_part

    for r in range(reps):

        @pl.when((shard == n_shard - 1) & (rel == r))
        def _():
            tail_id = lax.broadcasted_iota(jnp.int32, (16, cap_pad), 0)
            ones = jnp.ones((16, width), BF16)
            for p in range(n_pos):
                there = slice(p * cap_pad, (p + 1) * cap_pad)
                here = slice(r * cap_pad, (r + 1) * cap_pad)
                eo = (eo_acc[there, :] + bias_acc[...]).astype(BF16)
                eo_ref[p, here, :] = eo
                dbuf_ref[p, here, :] = db_acc[there, :].astype(BF16)
                product = c_ref[0, p, here, :].astype(F32) * eo.astype(F32)
                high = product.astype(BF16)
                low = (product - high.astype(F32)).astype(BF16)
                dgate = mm_nt(ones, high) + mm_nt(ones, low)
                dg_high = dgate.astype(BF16).astype(F32)
                held = dbuf_ref[p, msg : msg + 16, 0:cap_pad].astype(F32)
                held = jnp.where(tail_id == 2 * r, dg_high, jnp.where(tail_id == 2 * r + 1, dgate - dg_high, held))
                dbuf_ref[p, msg : msg + 16, 0:cap_pad] = held.astype(BF16)


def run_expert(arrived, cots, micro, win, wout, n_pos, reps, n_shard, cap_pad):
    width = arrived.shape[-1]
    ext, ff = win.shape[1:]
    msg = reps * cap_pad
    rows = n_pos * cap_pad
    n_pieces = reps * n_shard
    dims = (n_pos, reps, n_shard, cap_pad, width, ff, ext - width)
    whole = lambda *shape: pl.BlockSpec(shape, lambda i: (0,) * len(shape))
    per_rel = pl.BlockSpec((1, rows, width), lambda i: (i // n_shard, 0, 0))
    per_step = pl.BlockSpec((1, rows, ff), lambda i: (i // n_shard, 0, lax.rem(i, n_shard)))
    return pl.pallas_call(
        functools.partial(expert_kernel, dims),
        grid=(n_pieces,),
        out_shape=(
            jax.ShapeDtypeStruct((n_pos, msg, width), BF16),
            jax.ShapeDtypeStruct((n_pos, msg + 16, width), BF16),
            jax.ShapeDtypeStruct((reps, rows, n_shard * ff), BF16),
            jax.ShapeDtypeStruct((reps, rows, n_shard * ff), BF16),
            jax.ShapeDtypeStruct((reps, rows, width), BF16),
            jax.ShapeDtypeStruct((reps, rows, width), BF16),
        ),
        in_specs=[
            ANY_SPEC,
            ANY_SPEC,
            pl.BlockSpec((1, n_pos, msg + 16, width), lambda i: (micro, 0, 0, 0)),
            pl.BlockSpec((1, n_pos, msg, width), lambda i: (micro, 0, 0, 0)),
        ],
        out_specs=(whole(n_pos, msg, width), whole(n_pos, msg + 16, width), per_step, per_step, per_rel, per_rel),
        scratch_shapes=[
            pltpu.VMEM((n_pieces, ext, ff), BF16),
            pltpu.VMEM((n_pieces, ff, width), BF16),
            pltpu.VMEM((rows, ff), F32),
            pltpu.VMEM((rows, ff), F32),
            pltpu.VMEM((rows, width), F32),
            pltpu.VMEM((rows, width), F32),
            pltpu.VMEM((1, width), F32),
            pltpu.SemaphoreType.DMA((n_pieces,)),
            pltpu.SemaphoreType.DMA((n_pieces,)),
        ],
        **plain(cost(8.0 * n_pieces * rows * ff * width, 40e6, 2 * n_pieces * rows * ff)),
    )(win, wout, arrived, cots)


def weight_grad_kernel(dims, *refs):
    n_shard, width, ff = dims
    bufs, deos, hids, dhs = refs[0:2], refs[2:4], refs[4:6], refs[6:8]
    gin_ref, gout_ref = refs[8:10]
    buf_t, deo_t, bias_s = refs[10:13]
    rows = bufs[0].shape[1]

    @pl.when(lax.rem(pl.program_id(0), n_shard) == 0)
    def _():
        total = None
        for m in range(2):
            buf_t[:, m * rows : (m + 1) * rows] = bufs[m][0].T
            deo_t[:, m * rows : (m + 1) * rows] = deos[m][0].T
            part = jnp.sum(deos[m][0].astype(F32), axis=0, keepdims=True)
            total = part if total is None else total + part
        bias_s[...] = total

    grad_in = None
    grad_out = None
    bias_in = None
    for m in range(2):
        here = slice(m * rows, (m + 1) * rows)
        dh = dhs[m][0]
        part_in = mm(buf_t[:, here], dh)
        part_out = mm(deo_t[:, here], hids[m][0])
        part_bias = jnp.sum(dh.astype(F32), axis=0, keepdims=True)
        grad_in = part_in if m == 0 else grad_in + part_in
        grad_out = part_out if m == 0 else grad_out + part_out
        bias_in = part_bias if m == 0 else bias_in + part_bias
    gin_ref[0, 0:width, :] = grad_in.astype(BF16)
    tail_id = lax.broadcasted_iota(jnp.int32, (16, ff), 0)
    tail = jnp.where(tail_id == 0, bias_in, 0.0)
    for i in range(width // ff):
        tail = jnp.where(tail_id == 1 + i, bias_s[0:1, i * ff : (i + 1) * ff], tail)
    gin_ref[0, width : width + 16, :] = tail.astype(BF16)
    gout_ref[0] = grad_out.astype(BF16)


def run_weight_grads(bufs, deos, hids, dhs, n_shard, ff):
    reps, rows, width = bufs[0].shape
    n_pieces = reps * n_shard
    per_rel = pl.BlockSpec((1, rows, width), lambda i: (i // n_shard, 0, 0))
    per_step = pl.BlockSpec((1, rows, ff), lambda i: (i // n_shard, 0, lax.rem(i, n_shard)))
    piece = lambda i: (lax.rem(i, n_shard) * reps + i // n_shard, 0, 0)
    return pl.pallas_call(
        functools.partial(weight_grad_kernel, (n_shard, width, ff)),
        grid=(n_pieces,),
        out_shape=(
            jax.ShapeDtypeStruct((n_pieces, width + 16, ff), BF16),
            jax.ShapeDtypeStruct((n_pieces, width, ff), BF16),
        ),
        in_specs=[per_rel] * 4 + [per_step] * 4,
        out_specs=(pl.BlockSpec((1, width + 16, ff), piece), pl.BlockSpec((1, width, ff), piece)),
        scratch_shapes=[
            pltpu.VMEM((width, 2 * rows), BF16),
            pltpu.VMEM((width, 2 * rows), BF16),
            pltpu.VMEM((1, width), F32),
        ],
        **plain(cost(8.0 * n_pieces * rows * ff * width, 40e6)),
    )(*bufs, *deos, *hids, *dhs)


def combine_kernel(dims, batch_ref, col_ref, gate0_ref, gate1_ref, mid0_ref, mid1_ref, eo0_ref, eo1_ref, out_ref):
    n_img, seq, pad, group, n_pos, reps, cap, cap_pad, n_exp = dims
    rows = group * pad
    msg = reps * cap_pad
    order = image_order(batch_ref, n_img)
    ids = lanes(rows, 128).astype(F32)
    along = lanes(rows, msg)
    for micro, gate_ref, mid_ref, eo_ref in ((0, gate0_ref, mid0_ref, eo0_ref), (1, gate1_ref, mid1_ref, eo1_ref)):
        table = col_ref[micro]
        gates = gate_ref[...]
        result = mid_ref[...]
        for lane in range(2):
            gate = jnp.sum(jnp.where(ids == table[:, lane : lane + 1], gates, 0.0), axis=1, keepdims=True)
            target = table[:, 2 + lane : 3 + lane]
            picked = None
            for pos in range(n_pos):
                chosen = ((along + pos * msg).astype(F32) == target).astype(F32).astype(BF16)
                part = mm(chosen, eo_ref[pos])
                picked = part if picked is None else picked + part
            result = result + gate * picked
        for n in range(group):
            out_ref[order[micro * group + n]] = result[n * pad : n * pad + seq, :].astype(BF16)


def backward_kernel(dims, micro, *refs):
    n_img, seq, pad, group, n_pos, reps, cap, cap_pad, n_exp = dims
    (batch_ref, tok_ref, cot_ref, full_ref, col_ref, a1_ref, qkv_ref, mix_ref, mid_ref, a2_ref, gate_ref, lse_ref,
     dbuf_ref) = refs[:13]
    refs = refs[13:]
    if micro > 0:
        prev_gtok_ref, prev_grad_ref = refs[:2]
        refs = refs[2:]
    gtok_ref, grad_ref, c_s, x_s, vec_s, dqkv_s, do_s = refs
    rows = group * pad
    msg = reps * cap_pad
    width = tok_ref.shape[-1]
    head = width // HEADS
    per_pair = 128 // head
    order = image_order(batch_ref, n_img)
    c = load_group(cot_ref, order, micro, group, seq, pad, c_s)
    x = load_group(tok_ref, order, micro, group, seq, pad, x_s)
    small = full_ref[:, 4 * width :]
    turned = small.astype(F32).T
    gain1 = turned[n_exp : n_exp + 1, :]
    gain2 = turned[n_exp + 2 : n_exp + 3, :]
    vec_s[...] = jnp.zeros(vec_s.shape, F32)

    table = col_ref[0]
    to1, to2 = table[:, 2:3], table[:, 3:4]
    along = lanes(rows, cap_pad)
    routed = None
    dg1 = jnp.zeros((rows, cap_pad), F32)
    dg2 = jnp.zeros((rows, cap_pad), F32)
    for pos in range(n_pos):
        for rel in range(reps):
            there = (along + (pos * msg + rel * cap_pad)).astype(F32)
            hit1 = there == to1
            hit2 = there == to2
            chosen = (hit1 | hit2).astype(F32).astype(BF16)
            part = mm(chosen, dbuf_ref[pos, rel * cap_pad : (rel + 1) * cap_pad, :])
            routed = part if routed is None else routed + part
            tail = dbuf_ref[pos, msg : msg + 16, 0:cap_pad].astype(F32)
            dgate = tail[2 * rel : 2 * rel + 1, :] + tail[2 * rel + 1 : 2 * rel + 2, :]
            dg1 = jnp.where(hit1, dgate, dg1)
            dg2 = jnp.where(hit2, dgate, dg2)
    dg1 = jnp.sum(dg1, axis=1, keepdims=True)
    dg2 = jnp.sum(dg2, axis=1, keepdims=True)
    ids = lanes(rows, 128).astype(F32)
    gates = gate_ref[...]
    dgates = jnp.where(ids == table[:, 0:1], dg1, 0.0) + jnp.where(ids == table[:, 1:2], dg2, 0.0)
    dlogits = (gates * (dgates - jnp.sum(gates * dgates, axis=1, keepdims=True))).astype(BF16)
    grad_small = mm_tn(a2_ref[...], dlogits)
    da2 = mm_nt(dlogits, small) + routed

    def norm_back(values, upstream, gain, at):
        normed, rate = norm_parts(values)
        vec_s[n_exp + at : n_exp + at + 1, :] = jnp.sum(upstream * normed, axis=0, keepdims=True)
        vec_s[n_exp + at + 1 : n_exp + at + 2, :] = jnp.sum(upstream, axis=0, keepdims=True)
        scaled = upstream * gain
        return rate * (
            scaled
            - jnp.mean(scaled, axis=-1, keepdims=True)
            - normed * jnp.mean(scaled * normed, axis=-1, keepdims=True)
        )

    dmid = c + norm_back(mid_ref[...], da2, gain2, 2)
    c_s[...] = dmid
    dbranch = dmid.astype(BF16)
    vec_s[n_exp + 6 : n_exp + 7, :] = jnp.sum(dbranch.astype(F32), axis=0, keepdims=True)
    grad_ref[:, 3 * width : 4 * width] = mm_tn(mix_ref[...], dbranch)
    do_s[...] = mm_nt(dbranch, full_ref[:, 3 * width : 4 * width]).astype(BF16)

    key_ok = lanes(pad, pad) < seq
    lane = lanes(pad, 128)
    scale = head ** (-0.5)
    for n in range(group):
        at = slice(n * pad, (n + 1) * pad)
        lse = lse_ref[at, :]
        for pair in range(width // 128):
            cols = pair * 128
            q2 = qkv_ref[at, cols : cols + 128]
            k2 = qkv_ref[at, width + cols : width + cols + 128]
            v2 = qkv_ref[at, 2 * width + cols : 2 * width + cols + 128]
            do2 = do_s[at, cols : cols + 128]
            dq2 = dk2 = dv2 = None
            for sub in range(per_pair):
                index = pair * per_pair + sub
                mine = (lane >= sub * head) & (lane < (sub + 1) * head)
                zero = jnp.zeros_like(q2)
                qh = jnp.where(mine, q2, zero)
                kh = jnp.where(mine, k2, zero)
                doh = jnp.where(mine, do2, zero)
                scores = jnp.where(key_ok, mm_nt(qh, k2), -jnp.inf)
                probs = jnp.exp(scores - lse[:, index : index + 1])
                dprobs = mm_nt(doh, v2)
                dscores = (probs * (dprobs - jnp.sum(probs * dprobs, axis=-1, keepdims=True))).astype(BF16)
                dv = mm_tn(probs.astype(BF16), doh)
                dq = mm(dscores, kh)
                dk = mm_tn(dscores, qh)
                dq2 = dq if dq2 is None else dq2 + dq
                dk2 = dk if dk2 is None else dk2 + dk
                dv2 = dv if dv2 is None else dv2 + dv
            dqkv_s[at, cols : cols + 128] = (dq2 * scale).astype(BF16)
            dqkv_s[at, width + cols : width + cols + 128] = dk2.astype(BF16)
            dqkv_s[at, 2 * width + cols : 2 * width + cols + 128] = dv2.astype(BF16)
    dqkv = dqkv_s[...]
    grad_ref[:, 0 : 3 * width] = mm_tn(a1_ref[...], dqkv)
    vec_s[n_exp + 4 : n_exp + 5, :] = jnp.sum(dqkv[:, 0:width].astype(F32), axis=0, keepdims=True)
    vec_s[n_exp + 5 : n_exp + 6, :] = jnp.sum(dqkv[:, 2 * width :].astype(F32), axis=0, keepdims=True)
    da1 = mm_nt(dqkv, full_ref[:, 0 : 3 * width])
    dx = c_s[...] + norm_back(x_s[...], da1, gain1, 0)
    if micro > 0:
        gtok_ref[...] = prev_gtok_ref[...]
    for n in range(group):
        gtok_ref[order[micro * group + n]] = dx[n * pad : n * pad + seq, :]
    grad_ref[:, 4 * width :] = grad_small + vec_s[...].T
    if micro > 0:
        grad_ref[...] += prev_grad_ref[...]


def on_device(
    tokens, cotangent, routes, batch_of_image, w_qkv, w_attn_out, w_router, norm1_gain, norm1_bias, norm2_gain,
    norm2_bias, bias_query, bias_value, bias_attn_out, w_expert_in, w_expert_out, bias_expert_in, bias_expert_out,
):
    n_img, seq, width = tokens.shape
    n_expert = lax.axis_size("expert")
    n_shard = lax.axis_size("shard")
    n_dev = n_expert * n_shard
    group = n_img // MICRO
    pad = round_up(seq, 16)
    rows = group * pad
    cap = 16 * group * seq // (5 * n_expert)
    cap_pad = round_up(cap, 16)
    reps = 2 if n_expert > 1 else 1
    n_pos = n_expert // reps
    msg = reps * cap_pad
    ff = w_expert_in.shape[2]
    dims = (n_img, seq, pad, group, n_pos, reps, cap, cap_pad, n_expert)
    my_shard = lax.axis_index("shard")

    vectors = jnp.stack(
        [norm1_gain, norm1_bias, norm2_gain, norm2_bias, bias_query, bias_value, bias_attn_out], axis=1
    )
    blank = jnp.zeros((vectors.shape[0], 128 - n_expert - 7), BF16)
    packed = jnp.concatenate([w_qkv, w_attn_out, w_router, vectors, blank], axis=1)

    out_bias = lax.dynamic_update_slice(
        jnp.zeros((width,), BF16), bias_expert_out[0], (my_shard * (width // n_shard),)
    )
    tail = jnp.zeros((16, ff), BF16).at[0].set(bias_expert_in[0]).at[1 : 1 + width // ff].set(
        out_bias.reshape(width // ff, ff)
    )
    own_in = jnp.concatenate([w_expert_in[0], tail], axis=0)

    def swap(value, bit):
        return lax.ppermute(value, ("expert", "shard"), [(i, i ^ bit) for i in range(n_dev)])

    top = n_pos * n_shard
    groups = [[h * n_pos + i for i in range(n_pos)] for h in range(reps)]

    def exchange(value):
        turn = lax.rem(lax.axis_index("expert"), n_pos) ^ jnp.arange(n_pos)
        back = lax.all_to_all(
            value[turn], "expert", split_axis=0, concat_axis=0, axis_index_groups=groups, tiled=True
        )
        return back[turn]

    cols, full, win, wout, ain, cin, *states = run_first(
        dims, n_shard, batch_of_image, routes, tokens, cotangent, packed, own_in, w_expert_out[0]
    )
    if full.ndim == 3:
        full = full.reshape(n_dev * full.shape[1], full.shape[2])
    col_spec = lambda micro: pl.BlockSpec((1, rows, 128), lambda i: (micro, 0, 0))
    whole = lambda array: pl.BlockSpec(array.shape, lambda i: (0,) * len(array.shape))

    expert = []
    for micro in range(MICRO):
        expert.append(run_expert(ain, cin, micro, win, wout, n_pos, reps, n_shard, cap_pad))
    dbufs = [exchange(result[1]) for result in expert]
    outs = [exchange(result[0]) for result in expert]
    grad_in, grad_out = run_weight_grads(
        [e[5] for e in expert], [e[4] for e in expert], [e[2] for e in expert], [e[3] for e in expert], n_shard, ff
    )

    def reduce_pieces(pieces_all):
        for bit in [1 << i for i in range(n_shard.bit_length() - 1)] + ([top] if reps > 1 else []):
            if bit == top and reps > 1:
                mine, theirs = pieces_all[0::2], pieces_all[1::2]
            else:
                split = pieces_all.reshape((-1, 2, reps) + pieces_all.shape[1:])
                mine = split[:, 0].reshape((-1,) + pieces_all.shape[1:])
                theirs = split[:, 1].reshape((-1,) + pieces_all.shape[1:])
            pieces_all = (mine.astype(F32) + swap(theirs, bit).astype(F32)).astype(BF16)
        return pieces_all[0].astype(F32)

    own_grad_in = reduce_pieces(grad_in)
    own_grad_out = reduce_pieces(grad_out)

    gtok = grad = None
    for micro in range(MICRO):
        a1, qkv, mix, mid, a2, gate, lse = states[micro]
        operands = [batch_of_image, tokens, cotangent, full, cols, a1, qkv, mix, mid, a2, gate, lse, dbufs[micro]]
        specs = [SMEM_SPEC] + [whole(o) for o in operands[1:4]] + [col_spec(micro)] + [whole(o) for o in operands[5:]]
        if micro > 0:
            operands += [gtok, grad]
            specs += [whole(gtok), whole(grad)]
        shapes = (
            jax.ShapeDtypeStruct((n_img, seq, width), F32),
            jax.ShapeDtypeStruct((width, 4 * width + 128), F32),
        )
        gtok, grad = pl.pallas_call(
            functools.partial(backward_kernel, dims, micro),
            grid=(1,),
            out_shape=shapes,
            in_specs=specs,
            out_specs=tuple(whole(s) for s in shapes),
            scratch_shapes=[
                pltpu.VMEM((rows, width), F32),
                pltpu.VMEM((rows, width), F32),
                pltpu.VMEM((128, width), F32),
                pltpu.VMEM((rows, 3 * width), BF16),
                pltpu.VMEM((rows, width), BF16),
            ],
            **plain(cost(20.0 * rows * width * width + 2.0 * n_pos * msg * rows * width, 16e6, 1e6)),
        )(*operands)

    layer_out = pl.pallas_call(
        functools.partial(combine_kernel, dims),
        out_shape=jax.ShapeDtypeStruct((n_img, seq, width), BF16),
        in_specs=[SMEM_SPEC] + [VMEM_SPEC] * 7,
        out_specs=VMEM_SPEC,
        **plain(cost(8.0 * n_pos * msg * rows * width, 8e6)),
    )(batch_of_image, cols, states[0][5], states[1][5], states[0][3], states[1][3], outs[0], outs[1])

    mine = scatter_params(grad, n_expert, n_shard, 1)
    tail = own_grad_in[width:, :]
    out_bias_grad = tail[1 : 1 + width // ff, :].reshape(width)
    small = mine[:, 4 * width :]
    vec = [small[:, n_expert + i] for i in range(7)]
    return (
        layer_out,
        gtok,
        mine[:, 0 : 3 * width],
        mine[:, 3 * width : 4 * width],
        small[:, 0:n_expert],
        *vec,
        own_grad_in[0:width, :][None],
        own_grad_out.T[None],
        tail[0:1, :],
        lax.dynamic_slice(out_bias_grad, (my_shard * (width // n_shard),), (width // n_shard,))[None],
    )


def solution(mesh):
    both = ("expert", "shard")
    placed = (
        (P(both, None, None),) * 3
        + (P(both),)
        + (P(both, None),) * 3
        + (P(both),) * 7
        + (P("expert", None, "shard"), P("expert", "shard", None), P("expert", "shard"), P("expert", "shard"))
    )
    return jax.shard_map(
        on_device,
        mesh=mesh,
        in_specs=placed,
        out_specs=(P(both, None, None),) * 2
        + (P(both, None),) * 3
        + (P(both),) * 7
        + (P("expert", None, "shard"), P("expert", "shard", None), P("expert", "shard"), P("expert", "shard")),
        check_vma=False,
    )
```

```python
import functools
import math

import jax
import jax.numpy as jnp
from jax import lax
from jax.experimental import pallas as pl
from jax.experimental.pallas import tpu as pltpu
from jax.sharding import PartitionSpec as P

HEADS = 8
MICRO = 2
EPS = 1e-06
F32 = jnp.float32
BF16 = jnp.bfloat16
MESH = pl.DeviceIdType.MESH
OWN_FIRST = (0, 1, 2, 3)
VMEM_LIMIT = 56 * 1024 * 1024
VMEM_SPEC = pl.BlockSpec(memory_space=pltpu.VMEM)
SMEM_SPEC = pl.BlockSpec(memory_space=pltpu.SMEM)
ANY_SPEC = pl.BlockSpec(memory_space=pl.ANY)


def round_up(value, unit):
    return (value + unit - 1) // unit * unit


def mm(left, right):
    return lax.dot_general(left, right, (((1,), (0,)), ((), ())), preferred_element_type=F32)


def mm_nt(left, right):
    return lax.dot_general(left, right, (((1,), (1,)), ((), ())), preferred_element_type=F32)


def mm_tn(left, right):
    return lax.dot_general(left, right, (((0,), (0,)), ((), ())), preferred_element_type=F32)


def cost(flops, nbytes, trans=0):
    return pl.CostEstimate(flops=int(flops), bytes_accessed=int(nbytes), transcendentals=int(trans))


def plain(name_cost):
    return dict(
        cost_estimate=name_cost,
        compiler_params=pltpu.CompilerParams(vmem_limit_bytes=VMEM_LIMIT),
    )


def image_ranks(batch_ref, n_img):
    keys = [batch_ref[i] * n_img + i for i in range(n_img)]
    ranks = []
    for i in range(n_img):
        rank = jnp.int32(0)
        for j in range(n_img):
            if j != i:
                rank = rank + jnp.where(keys[j] < keys[i], 1, 0)
        ranks.append(rank)
    return ranks


def image_order(batch_ref, n_img):
    ranks = image_ranks(batch_ref, n_img)
    order = []
    for k in range(n_img):
        place = jnp.int32(0)
        for i in range(n_img):
            place = place + jnp.where(ranks[i] == k, i, 0)
        order.append(place)
    return order


def flip(index, bit):
    return index + bit - 2 * bit * lax.rem(index // bit, 2)


def lanes(rows, width):
    return lax.broadcasted_iota(jnp.int32, (rows, width), 1)


def bit_orders(n_expert, n_shard):
    shard_bits = [1 << i for i in range(n_shard.bit_length() - 1)]
    expert_bits = [n_shard << i for i in range(n_expert.bit_length() - 1)]
    core = shard_bits[:1]
    across = shard_bits[1:]
    first = expert_bits[::-1] + across[::-1] + core
    second = expert_bits[:0:-1] + across[::-1] + expert_bits[:1] + core
    return first, second


def combos(bits):
    result = [0]
    for bit in bits:
        result = result + [held + bit for held in result]
    return result


def flip_all(index, combo):
    bit = 1
    while bit <= combo:
        if combo & bit:
            index = flip(index, bit)
        bit *= 2
    return index


def greet(me, bits, n_shard):
    barrier = pltpu.get_barrier_semaphore()
    for bit in bits:
        peer = flip(me, bit)
        pl.semaphore_signal(
            barrier, inc=1, device_id=(peer // n_shard, lax.rem(peer, n_shard)), device_id_type=MESH
        )
    pl.semaphore_wait(barrier, len(bits))


def gather_kernel(n_shard, orders, cuts, mine_ref, full_ref, local_sem, send_sems, recv_sems):
    me = lax.axis_index("expert") * n_shard + lax.axis_index("shard")
    greet(me, orders[0], n_shard)
    own = pltpu.make_async_copy(mine_ref, full_ref.at[me], local_sem)
    own.start()
    copies = []
    for step in range(len(orders[0])):
        started = []
        for part, order in enumerate(orders):
            bit = order[step]
            peer = flip(me, bit)
            low, high = cuts[part]
            for at, combo in enumerate(combos(order[:step])):
                chunk = flip_all(me, combo)
                source = mine_ref if combo == 0 else full_ref.at[chunk]
                copy = pltpu.make_async_remote_copy(
                    src_ref=source.at[:, low:high],
                    dst_ref=full_ref.at[chunk, :, low:high],
                    send_sem=send_sems.at[part, (1 << step) - 1 + at],
                    recv_sem=recv_sems.at[part, (1 << step) - 1 + at],
                    device_id=(peer // n_shard, lax.rem(peer, n_shard)),
                    device_id_type=MESH,
                )
                copy.start()
                started.append(copy)
        for copy in started:
            copy.wait_recv()
        copies.extend(started)
    for copy in copies:
        copy.wait_send()
    own.wait()


def gather_params(packed, n_expert, n_shard, collective_id):
    rows, width = packed.shape
    n_dev = n_expert * n_shard
    orders = bit_orders(n_expert, n_shard)
    middle = width // 256 * 128
    cuts = ((0, middle), (middle, width))
    full = pl.pallas_call(
        functools.partial(gather_kernel, n_shard, orders, cuts),
        out_shape=jax.ShapeDtypeStruct((n_dev, rows, width), packed.dtype),
        in_specs=[VMEM_SPEC],
        out_specs=VMEM_SPEC,
        scratch_shapes=[
            pltpu.SemaphoreType.DMA,
            pltpu.SemaphoreType.DMA((2, n_dev - 1)),
            pltpu.SemaphoreType.DMA((2, n_dev - 1)),
        ],
        compiler_params=pltpu.CompilerParams(
            collective_id=collective_id, has_side_effects=True, vmem_limit_bytes=VMEM_LIMIT
        ),
        cost_estimate=cost(1e6, 4 * n_dev * rows * width),
    )(packed)
    return full.reshape(n_dev * rows, width)


def scatter_kernel(n_shard, orders, cuts, full_ref, out_ref, acc, sends, recvs, send_sems, recv_sems):
    me = lax.axis_index("expert") * n_shard + lax.axis_index("shard")
    n_dev = full_ref.shape[0]
    greet(me, orders[0], n_shard)
    n_steps = len(orders[0])
    acc[...] = full_ref[...]
    copies = []
    for step in range(n_steps):
        started = []
        base = n_dev - (n_dev >> step)
        count = n_dev >> (step + 1)
        for part, order in enumerate(orders):
            bit = order[step]
            peer = flip(me, bit)
            low, high = cuts[part]
            for at, combo in enumerate(combos(order[step + 1 :])):
                chunk = flip_all(peer, combo)
                sends[base + at, :, low:high] = acc[chunk, :, low:high].astype(BF16)
            copy = pltpu.make_async_remote_copy(
                src_ref=sends.at[base : base + count, :, low:high],
                dst_ref=recvs.at[base : base + count, :, low:high],
                send_sem=send_sems.at[part, step],
                recv_sem=recv_sems.at[part, step],
                device_id=(peer // n_shard, lax.rem(peer, n_shard)),
                device_id_type=MESH,
            )
            copy.start()
            started.append(copy)
        for part, order in enumerate(orders):
            low, high = cuts[part]
            started[part].wait_recv()
            for at, combo in enumerate(combos(order[step + 1 :])):
                chunk = flip_all(me, combo)
                acc[chunk, :, low:high] += recvs[base + at, :, low:high].astype(F32)
        copies.extend(started)
    out_ref[...] = acc[me]
    for copy in copies:
        copy.wait_send()


def scatter_params(full, n_expert, n_shard, collective_id):
    n_dev = n_expert * n_shard
    width = full.shape[1]
    rows = full.shape[0] // n_dev
    gather_orders = bit_orders(n_expert, n_shard)
    orders = [order[::-1] for order in gather_orders]
    middle = width // 256 * 128
    cuts = ((0, middle), (middle, width))
    return pl.pallas_call(
        functools.partial(scatter_kernel, n_shard, orders, cuts),
        out_shape=jax.ShapeDtypeStruct((rows, width), F32),
        in_specs=[VMEM_SPEC],
        out_specs=VMEM_SPEC,
        scratch_shapes=[
            pltpu.VMEM((n_dev, rows, width), F32),
            pltpu.VMEM((n_dev, rows, width), BF16),
            pltpu.VMEM((n_dev, rows, width), BF16),
            pltpu.SemaphoreType.DMA((2, len(orders[0]))),
            pltpu.SemaphoreType.DMA((2, len(orders[0]))),
        ],
        compiler_params=pltpu.CompilerParams(
            collective_id=collective_id, has_side_effects=True, vmem_limit_bytes=VMEM_LIMIT
        ),
        cost_estimate=cost(1e6, 8 * n_dev * rows * width),
    )(full.reshape(n_dev, rows, width))


def route_tables(dims, rt_s):
    n_img, seq, pad, group, n_pos, reps, cap, cap_pad, n_exp = dims
    rows = group * pad
    lower = (
        lax.broadcasted_iota(jnp.int32, (rows, rows), 0)
        > lax.broadcasted_iota(jnp.int32, (rows, rows), 1)
    ).astype(F32).astype(BF16)
    ids = lanes(rows, 128)
    me = lax.axis_index("expert")
    first = rt_s[:, 0:1]
    second = rt_s[:, 1:2]
    hot_first = (ids == first).astype(F32)
    hot_second = (ids == second).astype(F32)
    earlier_first = mm(lower, hot_first.astype(BF16))
    earlier_second = mm(lower, hot_second.astype(BF16)) + jnp.sum(hot_first, axis=0, keepdims=True)
    table = jnp.where(ids == 0, first.astype(F32), jnp.where(ids == 1, second.astype(F32), 0.0))
    for lane, route, hot, earlier in (
        (2, first, hot_first, earlier_first),
        (3, second, hot_second, earlier_second),
    ):
        slot = jnp.sum(hot * earlier, axis=1, keepdims=True)
        away = jnp.bitwise_xor(jnp.maximum(route, 0), jnp.broadcast_to(me, route.shape)).astype(F32)
        target = away * float(cap_pad) + slot
        target = jnp.where((slot < float(cap)) & (route >= 0), target, -1.0)
        table = jnp.where(ids == lane, target, table)
    spare = round_up(rows, 128) - rows
    turned = jnp.concatenate([table, jnp.full((spare, 128), -1.0, F32)], axis=0).T
    return table, turned[2:3, 0:rows], turned[3:4, 0:rows]


def norm_parts(values):
    center = values - jnp.mean(values, axis=-1, keepdims=True)
    rate = lax.rsqrt(jnp.mean(center * center, axis=-1, keepdims=True) + EPS)
    return center * rate, rate


def load_group(ref, order, micro, group, seq, pad, buf):
    buf[...] = jnp.zeros(buf.shape, F32)
    for n in range(group):
        buf[n * pad : n * pad + seq, :] = ref[order[micro * group + n]].astype(F32)
    return buf[...]


def attention_forward(dims, x, full_ref, out):
    n_img, seq, pad, group, n_pos, reps, cap, cap_pad, n_exp = dims
    a1_ref, qkv_ref, mix_ref, mid_ref, a2_ref, gate_ref, lse_ref = out
    rows = group * pad
    width = x.shape[-1]
    head = width // HEADS
    per_pair = 128 // head
    small = full_ref[:, 4 * width :]
    turned = small.astype(F32).T
    gain1, shift1, gain2, shift2, bias_q, bias_v, bias_o = [
        turned[n_exp + i : n_exp + i + 1, :] for i in range(7)
    ]
    normed, _ = norm_parts(x)
    a1 = (normed * gain1 + shift1).astype(BF16)
    a1_ref[...] = a1
    proj = mm(a1, full_ref[:, 0 : 3 * width])
    scale = head ** (-0.5)
    qkv_ref[:, 0:width] = ((proj[:, 0:width] + bias_q).astype(BF16).astype(F32) * scale).astype(BF16)
    qkv_ref[:, width : 2 * width] = proj[:, width : 2 * width].astype(BF16)
    qkv_ref[:, 2 * width :] = (proj[:, 2 * width :] + bias_v).astype(BF16)
    key_ok = lanes(pad, pad) < seq
    lane = lanes(pad, 128)
    for n in range(group):
        at = slice(n * pad, (n + 1) * pad)
        lse = jnp.zeros((pad, 128), F32)
        for pair in range(width // 128):
            cols = pair * 128
            q2 = qkv_ref[at, cols : cols + 128]
            k2 = qkv_ref[at, width + cols : width + cols + 128]
            v2 = qkv_ref[at, 2 * width + cols : 2 * width + cols + 128]
            mixed = None
            for sub in range(per_pair):
                mine = (lane >= sub * head) & (lane < (sub + 1) * head)
                scores = mm_nt(jnp.where(mine, q2, jnp.zeros_like(q2)), k2)
                scores = jnp.where(key_ok, scores, -jnp.inf)
                top = jnp.max(scores, axis=-1, keepdims=True)
                grown = jnp.exp(scores - top)
                total = jnp.sum(grown, axis=-1, keepdims=True)
                probs = (grown / total).astype(BF16)
                part = mm(probs, jnp.where(mine, v2, jnp.zeros_like(v2)))
                mixed = part if mixed is None else mixed + part
                lse = jnp.where(lane == pair * per_pair + sub, top + jnp.log(total), lse)
            mix_ref[at, cols : cols + 128] = mixed.astype(BF16)
        lse_ref[at, :] = lse
    mid = x + mm(mix_ref[...], full_ref[:, 3 * width : 4 * width]) + bias_o
    mid_ref[...] = mid
    normed2, _ = norm_parts(mid)
    a2 = (normed2 * gain2 + shift2).astype(BF16)
    a2_ref[...] = a2
    ids = lanes(rows, 128)
    logits = jnp.where(ids < n_exp, mm(a2, small), -jnp.inf)
    grown = jnp.exp(logits - jnp.max(logits, axis=-1, keepdims=True))
    gates = grown / jnp.sum(grown, axis=-1, keepdims=True)
    gate_ref[...] = gates


def fill_message(dims, table, gates, a2, chosen, send_ref, tail_ref):
    n_img, seq, pad, group, n_pos, reps, cap, cap_pad, n_exp = dims
    rows = group * pad
    part = n_pos * cap_pad
    ids = lanes(rows, 128).astype(F32)
    gate1 = jnp.sum(jnp.where(ids == table[:, 0:1], gates, 0.0), axis=1, keepdims=True)
    gate2 = jnp.sum(jnp.where(ids == table[:, 1:2], gates, 0.0), axis=1, keepdims=True)
    to1, to2 = table[:, 2:3], table[:, 3:4]
    send_ref[...] = mm(chosen, a2).astype(BF16)
    tail_ref[...] = jnp.zeros(tail_ref.shape, BF16)
    along = lanes(rows, part)
    tail_id = lax.broadcasted_iota(jnp.int32, (16, cap_pad), 0)
    tails = [jnp.zeros((16, cap_pad), F32) for _ in range(n_pos)]
    for rel in range(reps):
        there = (along + rel * part).astype(F32)
        gate_row = jnp.sum(
            jnp.where(there == to1, gate1, 0.0) + jnp.where(there == to2, gate2, 0.0), axis=0, keepdims=True
        )
        high = gate_row.astype(BF16).astype(F32)
        low = gate_row - high
        for pos in range(n_pos):
            at = slice(pos * cap_pad, (pos + 1) * cap_pad)
            tails[pos] = jnp.where(
                tail_id == 2 * rel, high[:, at], jnp.where(tail_id == 2 * rel + 1, low[:, at], tails[pos])
            )
    for pos in range(n_pos):
        tail_ref[pos * 16 : (pos + 1) * 16, 0:cap_pad] = tails[pos].astype(BF16)


class Messages:
    def __init__(self, n_shard, me, n_pos, reps, cap_pad):
        self.n_shard, self.me, self.n_pos, self.reps, self.cap_pad = n_shard, me, n_pos, reps, cap_pad
        self.pending = []

    def move(self, source, target, send_sem, recv_sem, pos):
        if pos == 0:
            copy = pltpu.make_async_copy(source, target, recv_sem)
            copy.start()
            self.pending.append((copy, False))
        else:
            peer = flip_all(self.me, pos * self.n_shard)
            copy = pltpu.make_async_remote_copy(
                src_ref=source,
                dst_ref=target,
                send_sem=send_sem,
                recv_sem=recv_sem,
                device_id=(peer // self.n_shard, lax.rem(peer, self.n_shard)),
                device_id_type=MESH,
            )
            copy.start()
            self.pending.append((copy, True))
        return copy, pos > 0

    def rows(self, source, target, send_sems, recv_sems, rels=None):
        started = []
        for rel in range(self.reps) if rels is None else rels:
            for pos in range(self.n_pos):
                block = rel * self.n_pos + pos
                at = pl.ds(block * self.cap_pad, self.cap_pad)
                started.append(
                    self.move(source.at[at], target.at[at], send_sems.at[block], recv_sems.at[block], pos)
                )
        return started

    def tails(self, source, target, send_sems, recv_sems, blocks):
        started = []
        for block in blocks:
            at = pl.ds(block * 16, 16)
            started.append(
                self.move(source.at[at], target.at[at], send_sems.at[block], recv_sems.at[block], block % self.n_pos)
            )
        return started


def arrive(started):
    for copy, remote in started:
        if remote:
            copy.wait_recv()
        else:
            copy.wait()


def arrive_remote(started):
    arrive([member for member in started if member[1]])


def leave(started):
    for copy, remote in started:
        if remote:
            copy.wait_send()


def first_kernel(dims, n_shard, orders, cuts, gathered, *refs):
    n_img, seq, pad, group, n_pos, reps, cap, cap_pad, n_exp = dims
    (batch_ref, routes_ref, tok_ref, cot_ref, packed_ref, own_in_ref, own_out_ref) = refs[:7]
    refs = refs[7:]
    col_ref, full_out, win_ref, wout_ref, buf_ref, tail_ref, cot_slots_ref = refs[:7]
    next_out, next_tail_out, next_cot_out = refs[7:10]
    state_outs = (refs[10:17], refs[17:24])
    refs = refs[24:]
    states = (refs[0:7], refs[7:14])
    (next_ref, next_tail_ref, next_cot_ref, full_s, x_s, rt_s, chosen_s, asend, tsend, csend, keep_sems, own_sem,
     gsend, grecv, wsend, wrecv, dsend, drecv) = refs[14:]
    full_ref = packed_ref if gathered else full_s
    kept_copies = []

    def keep(source, target):
        copy = pltpu.make_async_copy(source, target, keep_sems.at[len(kept_copies)])
        copy.start()
        kept_copies.append(copy)

    rows = group * pad
    n_slots = reps * n_pos * cap_pad
    top = n_pos * n_shard
    expert, shard = lax.axis_index("expert"), lax.axis_index("shard")
    me = expert * n_shard + shard

    def place(index):
        return (index // n_shard, lax.rem(index, n_shard))

    peers = sorted(set(orders[0]) | {pos * n_shard for pos in range(1, n_pos)})
    barrier = pltpu.get_barrier_semaphore()
    for peer in peers:
        pl.semaphore_signal(barrier, inc=1, device_id=place(flip_all(me, peer)), device_id_type=MESH)
    pl.semaphore_wait(barrier, len(peers))

    chunk_rows = full_ref.shape[0] // (n_exp * n_shard) if not gathered else 0
    gather_copies = []

    def at_chunk(ref, index, low, high):
        return ref.at[pl.ds(pl.multiple_of(index * chunk_rows, chunk_rows), chunk_rows), low:high]

    def gather_start(step):
        for part, order in enumerate(orders):
            low, high = cuts[part]
            for at, combo in enumerate(combos(order[:step])):
                chunk = flip_all(me, combo)
                source = packed_ref.at[:, low:high] if combo == 0 else at_chunk(full_ref, chunk, low, high)
                sem = (1 << step) - 1 + at
                copy = pltpu.make_async_remote_copy(
                    src_ref=source,
                    dst_ref=at_chunk(full_ref, chunk, low, high),
                    send_sem=gsend.at[part, sem],
                    recv_sem=grecv.at[part, sem],
                    device_id=place(flip(me, order[step])),
                    device_id_type=MESH,
                )
                copy.start()
                gather_copies.append(copy)

    def gather_next(step):
        if gathered:
            return
        count = 2 * (1 << step)
        for copy in gather_copies[-count:]:
            copy.wait_recv()
        if step + 1 < len(orders[0]):
            gather_start(step + 1)

    if not gathered:
        gather_start(0)
        own = pltpu.make_async_copy(packed_ref, at_chunk(full_ref, me, 0, full_ref.shape[1]), own_sem)
        own.start()

    bits = ([top] if reps > 1 else []) + [1 << i for i in range(n_shard.bit_length() - 1)][::-1]

    def number(held):
        return (held // top) * n_shard + held % top

    weight_copies = {}

    ext, ff = own_in_ref.shape
    spans = [(0, 0, ext // 32 * 16), (0, ext // 32 * 16, ext), (1, 0, ff // 32 * 16), (1, ff // 32 * 16, ff)]

    def weights_start(span, held, bit):
        kind, low, high = spans[span]
        at = pl.ds(low, high - low)
        source = ((own_in_ref, own_out_ref)[kind]) if held == 0 else (win_ref, wout_ref)[kind].at[number(held)]
        to = number(held + bit)
        copy = pltpu.make_async_remote_copy(
            src_ref=source.at[at],
            dst_ref=(win_ref, wout_ref)[kind].at[to, at],
            send_sem=wsend.at[span, to],
            recv_sem=wrecv.at[span, to],
            device_id=place(flip(me, bit)),
            device_id_type=MESH,
        )
        copy.start()
        weight_copies[span, held + bit] = copy

    def weights_pass(span, held):
        weight_copies[span, held].wait_recv()
        last = min(bit for bit in bits if held & bit)
        for bit in bits:
            if bit < last:
                weights_start(span, held, bit)

    inner_bits = [bit for bit in bits if bit < top]
    if reps > 1:
        weights_start(0, 0, top)
        weights_start(1, 0, top)
    for span in OWN_FIRST:
        for bit in inner_bits:
            weights_start(span, 0, bit)

    order = image_order(batch_ref, n_img)
    messages = Messages(n_shard, me, n_pos, reps, cap_pad)
    arrivals = []

    n_steps = len(orders[0])
    step = 0
    tables = []
    for micro in range(MICRO):
        rt_s[...] = jnp.full(rt_s.shape, -1, jnp.int32)
        for n in range(group):
            rt_s[n * pad : n * pad + seq, 0:2] = routes_ref[order[micro * group + n]]
        table, row_first, row_second = route_tables(dims, rt_s)
        col_ref[micro] = table
        if step < n_steps:
            gather_next(step)
            step += 1
        cot = load_group(cot_ref, order, micro, group, seq, pad, x_s).astype(BF16)
        here = lax.broadcasted_iota(jnp.int32, (n_slots, rows), 0).astype(F32)
        chosen = ((here == row_first) | (here == row_second)).astype(F32).astype(BF16)
        chosen_s[micro] = chosen
        if micro == 0:
            csend[...] = mm(chosen, cot).astype(BF16)
            arrivals += messages.rows(csend, cot_slots_ref, dsend.at[0], drecv.at[0])
        else:
            next_cot_ref[...] = mm(chosen, cot).astype(BF16)
            keep(next_cot_ref, next_cot_out)
        if step < n_steps:
            gather_next(step)
            step += 1
    if reps > 1:
        weights_start(2, 0, top)
    while step < n_steps:
        gather_next(step)
        step += 1
    if not gathered:
        own.wait()
        keep(full_ref, full_out)
    if reps > 1:
        for span in range(2):
            weights_pass(span, top)
        weights_start(3, 0, top)
    for span in range(4):
        if span not in OWN_FIRST:
            for bit in inner_bits:
                weights_start(span, 0, bit)
    inner = sorted((held for held in combos(bits) if held and not held & 1), key=lambda h: (-(h & -h), h))
    early = [held for held in inner if held < top]
    late = [held for held in inner if held > top]
    for micro in range(MICRO):
        x = load_group(tok_ref, order, micro, group, seq, pad, x_s)
        attention_forward(dims, x, full_ref, states[micro])
        table = col_ref[micro]
        gates = states[micro][5][...]
        a2 = states[micro][4][...]
        if micro == 0:
            fill_message(dims, table, gates, a2, chosen_s[micro], asend, tsend)
            arrivals += messages.rows(asend, buf_ref, dsend.at[1], drecv.at[1])
            arrivals += messages.tails(tsend, tail_ref, dsend.at[2], drecv.at[2], range(n_pos))
        else:
            fill_message(dims, table, gates, a2, chosen_s[micro], next_ref, next_tail_ref)
            keep(next_ref, next_out)
            keep(next_tail_ref, next_tail_out)
        for held, kept in zip(states[micro], state_outs[micro]):
            keep(held, kept)
    for span in range(4):
        for held in early:
            weights_pass(span, held)
        if reps > 1 and span >= 2:
            weights_pass(span, top)
        if span < 2:
            for held in late:
                weights_pass(span, held)
    for span in range(2, 4):
        for held in late:
            weights_pass(span, held)
    for (_, held), copy in weight_copies.items():
        if held & 1:
            copy.wait_recv()
    arrive(arrivals)
    leave(arrivals)
    for copy in kept_copies:
        copy.wait()
    for copy in gather_copies:
        copy.wait_send()
    for copy in weight_copies.values():
        copy.wait_send()


def run_first(dims, n_shard, batch, routes, tokens, cotangent, packed, own_in, own_out):
    n_img, seq, pad, group, n_pos, reps, cap, cap_pad, n_exp = dims
    width = tokens.shape[-1]
    rows = group * pad
    n_slots = reps * n_pos * cap_pad
    tail_wide = round_up(cap_pad, 128)
    n_dev = n_exp * n_shard
    n_pieces = reps * n_shard
    total = packed.shape[1]
    orders = bit_orders(n_exp, n_shard)
    middle = total // 256 * 128
    cuts = ((0, middle), (middle, total))
    gathered = packed.shape[0] % 16 != 0
    if gathered:
        packed = gather_params(packed, n_exp, n_shard, 3)
    state = (
        jax.ShapeDtypeStruct((rows, width), BF16),
        jax.ShapeDtypeStruct((rows, 3 * width), BF16),
        jax.ShapeDtypeStruct((rows, width), BF16),
        jax.ShapeDtypeStruct((rows, width), F32),
        jax.ShapeDtypeStruct((rows, width), BF16),
        jax.ShapeDtypeStruct((rows, 128), F32),
        jax.ShapeDtypeStruct((rows, 128), F32),
    )
    full_rows = 16 if gathered else n_dev * packed.shape[0]
    out = pl.pallas_call(
        functools.partial(first_kernel, dims, n_shard, orders, cuts, gathered),
        out_shape=(
            jax.ShapeDtypeStruct((MICRO, rows, 128), F32),
            jax.ShapeDtypeStruct((full_rows, total), BF16),
            jax.ShapeDtypeStruct((n_pieces,) + own_in.shape, BF16),
            jax.ShapeDtypeStruct((n_pieces,) + own_out.shape, BF16),
            jax.ShapeDtypeStruct((n_slots, width), BF16),
            jax.ShapeDtypeStruct((n_pos * 16, tail_wide), BF16),
            jax.ShapeDtypeStruct((n_slots, width), BF16),
            jax.ShapeDtypeStruct((n_slots, width), BF16),
            jax.ShapeDtypeStruct((n_pos * 16, tail_wide), BF16),
            jax.ShapeDtypeStruct((n_slots, width), BF16),
            *state,
            *state,
        ),
        in_specs=[SMEM_SPEC] + [VMEM_SPEC] * 4 + [ANY_SPEC] * 2,
        out_specs=(VMEM_SPEC,) + (ANY_SPEC,) * 23,
        scratch_shapes=[
            *[pltpu.VMEM(shape.shape, shape.dtype) for shape in state + state],
            pltpu.VMEM((n_slots, width), BF16),
            pltpu.VMEM((n_pos * 16, tail_wide), BF16),
            pltpu.VMEM((n_slots, width), BF16),
            pltpu.VMEM((full_rows, total), BF16),
            pltpu.VMEM((rows, width), F32),
            pltpu.VMEM((rows, 128), jnp.int32),
            pltpu.VMEM((MICRO, n_slots, rows), BF16),
            pltpu.VMEM((n_slots, width), BF16),
            pltpu.VMEM((n_pos * 16, tail_wide), BF16),
            pltpu.VMEM((n_slots, width), BF16),
            pltpu.SemaphoreType.DMA((18,)),
            pltpu.SemaphoreType.DMA,
            pltpu.SemaphoreType.DMA((2, n_dev - 1)),
            pltpu.SemaphoreType.DMA((2, n_dev - 1)),
            pltpu.SemaphoreType.DMA((4, n_pieces)),
            pltpu.SemaphoreType.DMA((4, n_pieces)),
            pltpu.SemaphoreType.DMA((3, n_exp)),
            pltpu.SemaphoreType.DMA((3, n_exp)),
        ],
        compiler_params=pltpu.CompilerParams(
            collective_id=0, has_side_effects=True, vmem_limit_bytes=VMEM_LIMIT
        ),
        cost_estimate=cost(20e9, 60e6, 4e6),
    )(batch, routes, tokens, cotangent, packed, own_in, own_out)
    return out[0], packed if gathered else out[1], out[2:4], out[4:10], out[10:17], out[17:24]


def gelu_pair(v):
    size = jnp.abs(v)
    bell = jnp.exp(v * v * -0.5)
    t = 1.0 / (1.0 + (0.3275911 / math.sqrt(2.0)) * size)
    series = t * (
        0.5 * 0.254829592
        + t * (0.5 * -0.284496736 + t * (0.5 * 1.421413741 + t * (0.5 * -1.453152027 + t * (0.5 * 1.061405429))))
    )
    tail = series * bell
    share = jnp.where(v >= 0.0, 1.0 - tail, tail)
    return v * share, share + v * bell * (1.0 / math.sqrt(2.0 * math.pi))


def second_kernel(dims, n_shard, chunk, *refs):
    n_img, seq, pad, group, n_pos, reps, cap, cap_pad, n_exp = dims
    own_in_ref, own_out_ref, win_ref, wout_ref, buf0, tail0, cot0, next_ref, next_tail_ref, next_cot_ref = refs[:10]
    eo_ret, db_ret, dt_ret, gin_ref, gout_ref = refs[10:15]
    (buf1, tail1, cot1, w_in, w_out, hid_s, dh_s, deo_s, pre, back, eo_acc, db_acc, eo_send, db_send, dt_send,
     turned_s, gin_s, wsems, dsend, drecv, rsend, rrecv, gsems) = refs[15:]
    width = buf0.shape[-1]
    ff = win_ref.shape[-1]
    part = n_pos * cap_pad
    n_pieces = reps * n_shard
    n_chunks = n_shard * ff // chunk
    expert, shard = lax.axis_index("expert"), lax.axis_index("shard")
    me = expert * n_shard + shard
    peers = [pos * n_shard for pos in range(1, n_pos)]
    if peers:
        barrier = pltpu.get_barrier_semaphore()
        for peer in peers:
            to = flip_all(me, peer)
            pl.semaphore_signal(
                barrier, inc=1, device_id=(to // n_shard, lax.rem(to, n_shard)), device_id_type=MESH
            )
        pl.semaphore_wait(barrier, len(peers))
    messages = Messages(n_shard, me, n_pos, reps, cap_pad)
    coming = messages.rows(next_ref, buf1, dsend.at[0], drecv.at[0])
    coming += messages.tails(next_tail_ref, tail1, dsend.at[2], drecv.at[2], range(n_pos))
    coming += messages.rows(next_cot_ref, cot1, dsend.at[1], drecv.at[1])
    loads = []
    for rel in range(reps):
        for s in range(n_shard):
            piece = rel * n_shard + s
            cols = pl.ds(s * ff, ff)
            from_in = win_ref.at[piece] if piece else own_in_ref
            from_out = wout_ref.at[piece] if piece else own_out_ref
            copies = (
                pltpu.make_async_copy(from_in, w_in.at[rel, :, cols], wsems.at[0, piece]),
                pltpu.make_async_copy(from_out, w_out.at[rel, cols, :], wsems.at[1, piece]),
            )
            for copy in copies:
                copy.start()
            loads.append(copies)
    returns = ([], [])
    tail_id = lax.broadcasted_iota(jnp.int32, (16, cap_pad), 0)
    ones = jnp.ones((16, width), BF16)
    db_tail_wide = dt_send.shape[-1]
    for micro in range(MICRO):
        buf, tail, cot = ((buf0, tail0, cot0), (buf1, tail1, cot1))[micro]
        if micro == 1:
            arrive(coming)
        tails = tail[...].astype(F32)
        spare = round_up(n_pos * 16, 128) - n_pos * 16
        if spare:
            tails = jnp.concatenate([tails, jnp.zeros((spare, tails.shape[1]), F32)], axis=0)
        turned = tails.T
        for rel in range(reps):
            for pos in range(n_pos):
                at = slice(rel * part + pos * cap_pad, rel * part + (pos + 1) * cap_pad)
                lane = pos * 16 + 2 * rel
                gate = turned[0:cap_pad, lane : lane + 1] + turned[0:cap_pad, lane + 1 : lane + 2]
                deo_s[micro, at, :] = (cot[at, :].astype(F32) * gate).astype(BF16)
            if micro == 0:
                for s in range(n_shard):
                    for copy in loads[rel * n_shard + s]:
                        copy.wait()
            bias = w_in[rel, width : width + 16, :].astype(F32)
            bias_out = None
            for s in range(n_shard):
                row = jnp.concatenate(
                    [bias[1 + i : 2 + i, s * ff : (s + 1) * ff] for i in range(width // ff)], axis=1
                )
                bias_out = row if bias_out is None else bias_out + row
            if micro > 0:
                leave(returns[0][rel])
                arrive([member for member in returns[0][rel] if not member[1]])
            for pos_low in range(0, n_pos, pre.shape[0] // cap_pad):
                here = slice(rel * part + pos_low * cap_pad, rel * part + pos_low * cap_pad + pre.shape[0])
                kept = slice(micro * part + pos_low * cap_pad, micro * part + pos_low * cap_pad + pre.shape[0])
                eo_acc[...] = jnp.broadcast_to(bias_out, eo_acc.shape)
                db_acc[...] = jnp.zeros(db_acc.shape, F32)

                def piece(c, carry, rel=rel, micro=micro, here=here, kept=kept, buf=buf):
                    cols = pl.ds(pl.multiple_of(c * chunk, chunk), chunk)
                    bias = w_in[rel, width : width + 16, cols].astype(F32)[0:1, :]
                    pre[...] = mm(buf[here, :], w_in[rel, 0:width, cols])
                    back[...] = mm_nt(deo_s[micro, here, :], w_out[rel, cols, :])
                    for pos in range(pre.shape[0] // cap_pad):
                        at = slice(pos * cap_pad, (pos + 1) * cap_pad)
                        to = slice(kept.start + pos * cap_pad, kept.start + (pos + 1) * cap_pad)
                        value, slope = gelu_pair(pre[at, :] + bias)
                        hid_s[rel, to, cols] = value.astype(BF16)
                        dh_s[rel, to, cols] = (back[at, :] * slope).astype(BF16)
                    eo_acc[...] += mm(hid_s[rel, kept, cols], w_out[rel, cols, :])
                    db_acc[...] += mm_nt(dh_s[rel, kept, cols], w_in[rel, 0:width, cols])
                    return carry

                lax.fori_loop(0, n_chunks, piece, 0)
                for pos in range(pos_low, pos_low + pre.shape[0] // cap_pad):
                    at = slice((pos - pos_low) * cap_pad, (pos - pos_low + 1) * cap_pad)
                    to = slice(rel * part + pos * cap_pad, rel * part + (pos + 1) * cap_pad)
                    eo = eo_acc[at, :].astype(BF16)
                    eo_send[to, :] = eo
                    db_send[to, :] = db_acc[at, :].astype(BF16)
                    product = cot[to, :].astype(F32) * eo.astype(F32)
                    high = product.astype(BF16)
                    low = (product - high.astype(F32)).astype(BF16)
                    dgate = mm_nt(ones, high) + mm_nt(ones, low)
                    dg_high = dgate.astype(BF16).astype(F32)
                    block = rel * n_pos + pos
                    rows16 = slice(block * 16, (block + 1) * 16)
                    dt_send[micro, rows16, :] = jnp.zeros((16, db_tail_wide), BF16)
                    dt_send[micro, rows16, 0:cap_pad] = jnp.where(
                        tail_id == 0, dg_high, jnp.where(tail_id == 1, dgate - dg_high, 0.0)
                    ).astype(BF16)
            blocks = range(rel * n_pos, (rel + 1) * n_pos)
            sent = messages.rows(db_send, db_ret.at[micro], rsend.at[micro, 0], rrecv.at[micro, 0], (rel,))
            sent += messages.tails(
                dt_send.at[micro], dt_ret.at[micro], rsend.at[micro, 1], rrecv.at[micro, 1], blocks
            )
            sent += messages.rows(eo_send, eo_ret.at[micro], rsend.at[micro, 2], rrecv.at[micro, 2], (rel,))
            returns[micro].append(sent)

    stores = []

    def store(kind, slot, c, rel):
        staged, target = ((gin_s, gin_ref), (gin_s.at[:, 0:width, :], gout_ref))[kind]
        started = []
        for s in range(c * chunk // ff, (c + 1) * chunk // ff):
            index = s * reps + rel
            copy = pltpu.make_async_copy(
                staged.at[slot, :, pl.ds(s * ff - c * chunk, ff)], target.at[index], gsems.at[kind, index]
            )
            copy.start()
            started.append(copy)
        stores.append(started)

    def next_slot():
        if len(stores) >= 2:
            for copy in stores[-2]:
                copy.wait()
        return len(stores) % 2

    wide_id = lax.broadcasted_iota(jnp.int32, (16, ff), 0)
    for rel in range(reps)[::-1]:
        here = slice(rel * part, (rel + 1) * part)
        deo_bias = None
        for micro, buf in enumerate((buf0, buf1)):
            turned_s[:, micro * part : (micro + 1) * part] = buf[here, :].T
            total = jnp.sum(deo_s[micro, here, :].astype(F32), axis=0, keepdims=True)
            deo_bias = total if deo_bias is None else deo_bias + total
        for c in range(n_chunks):
            cols = slice(c * chunk, (c + 1) * chunk)
            slot = next_slot()
            dh = dh_s[rel, :, cols]
            gin_s[slot, 0:width, :] = mm(turned_s[...], dh).astype(BF16)
            bias_in = jnp.sum(dh.astype(F32), axis=0, keepdims=True)
            for s in range(c * chunk // ff, (c + 1) * chunk // ff):
                at = slice(s * ff - c * chunk, (s + 1) * ff - c * chunk)
                tail = jnp.where(wide_id == 0, bias_in[:, at], 0.0)
                for i in range(width // ff):
                    tail = jnp.where(wide_id == 1 + i, deo_bias[:, i * ff : (i + 1) * ff], tail)
                gin_s[slot, width : width + 16, at] = tail.astype(BF16)
            store(0, slot, c, rel)
        for micro in range(MICRO):
            turned_s[:, micro * part : (micro + 1) * part] = deo_s[micro, here, :].T
        for c in range(n_chunks):
            slot = next_slot()
            gin_s[slot, 0:width, :] = mm(turned_s[...], hid_s[rel, :, c * chunk : (c + 1) * chunk]).astype(BF16)
            store(1, slot, c, rel)
    for started in stores[-2:]:
        for copy in started:
            copy.wait()
    for sent in returns[0]:
        arrive_remote(sent)
    for sent in returns[1]:
        arrive(sent)
        leave(sent)
    leave(coming)


def run_second(dims, n_shard, own, weights, slots):
    n_img, seq, pad, group, n_pos, reps, cap, cap_pad, n_exp = dims
    win, wout = weights
    width = slots[0].shape[-1]
    ext, ff = win.shape[1:]
    total = n_shard * ff
    part = n_pos * cap_pad
    n_slots = reps * part
    chunk = max(ff, min(total, 1024 if n_slots <= 1280 else 256))
    block_rows = part if n_slots <= 1280 else n_pos // 4 * cap_pad
    tail_wide = round_up(cap_pad, 128)
    n_pieces = reps * n_shard
    return pl.pallas_call(
        functools.partial(second_kernel, dims, n_shard, chunk),
        out_shape=(
            jax.ShapeDtypeStruct((MICRO, n_slots, width), BF16),
            jax.ShapeDtypeStruct((MICRO, n_slots, width), BF16),
            jax.ShapeDtypeStruct((MICRO, n_exp * 16, tail_wide), BF16),
            jax.ShapeDtypeStruct((n_pieces, ext, ff), BF16),
            jax.ShapeDtypeStruct((n_pieces, width, ff), BF16),
        ),
        in_specs=[ANY_SPEC] * 4 + [VMEM_SPEC] * 3 + [ANY_SPEC] * 3,
        out_specs=(ANY_SPEC,) * 5,
        scratch_shapes=[
            pltpu.VMEM((n_slots, width), BF16),
            pltpu.VMEM((n_pos * 16, tail_wide), BF16),
            pltpu.VMEM((n_slots, width), BF16),
            pltpu.VMEM((reps, ext, total), BF16),
            pltpu.VMEM((reps, total, width), BF16),
            pltpu.VMEM((reps, MICRO * part, total), BF16),
            pltpu.VMEM((reps, MICRO * part, total), BF16),
            pltpu.VMEM((MICRO, n_slots, width), BF16),
            pltpu.VMEM((block_rows, chunk), F32),
            pltpu.VMEM((block_rows, chunk), F32),
            pltpu.VMEM((block_rows, width), F32),
            pltpu.VMEM((block_rows, width), F32),
            pltpu.VMEM((n_slots, width), BF16),
            pltpu.VMEM((n_slots, width), BF16),
            pltpu.VMEM((MICRO, n_exp * 16, tail_wide), BF16),
            pltpu.VMEM((width, MICRO * part), BF16),
            pltpu.VMEM((2, ext, chunk), BF16),
            pltpu.SemaphoreType.DMA((2, n_pieces)),
            pltpu.SemaphoreType.DMA((3, n_exp)),
            pltpu.SemaphoreType.DMA((3, n_exp)),
            pltpu.SemaphoreType.DMA((MICRO, 3, n_exp)),
            pltpu.SemaphoreType.DMA((MICRO, 3, n_exp)),
            pltpu.SemaphoreType.DMA((2, n_pieces)),
        ],
        compiler_params=pltpu.CompilerParams(
            collective_id=1, has_side_effects=True, vmem_limit_bytes=62 * 1024 * 1024
        ),
        cost_estimate=cost(32e9, 60e6, 10e6),
    )(*own, win, wout, *slots)


def combine_group(dims, micro, table, gates, mid, eo, out_ref):
    n_img, seq, pad, group, n_pos, reps, cap, cap_pad, n_exp = dims
    rows = group * pad
    n_slots = reps * n_pos * cap_pad
    ids = lanes(rows, 128).astype(F32)
    along = lanes(rows, n_slots).astype(F32)
    result = mid
    for lane in range(2):
        gate = jnp.sum(jnp.where(ids == table[:, lane : lane + 1], gates, 0.0), axis=1, keepdims=True)
        chosen = (along == table[:, 2 + lane : 3 + lane]).astype(F32).astype(BF16)
        result = result + gate * mm(chosen, eo)
    for n in range(group):
        out_ref[micro * group + n] = result[n * pad : n * pad + seq, :].astype(BF16)


def backward_group(dims, micro, order, hook, refs):
    n_img, seq, pad, group, n_pos, reps, cap, cap_pad, n_exp = dims
    (tok_ref, cot_ref, full_ref, table, state, db, dt, gtok_ref, grad_ref, c_s, x_s, vec_s, dqkv_s, do_s, dg_s) = refs
    a1_ref, qkv_ref, mix_ref, mid_ref, a2_ref, gate_ref, lse_ref = state
    rows = group * pad
    n_slots = reps * n_pos * cap_pad
    width = tok_ref.shape[-1]
    head = width // HEADS
    per_pair = 128 // head
    c = load_group(cot_ref, order, micro, group, seq, pad, c_s)
    small = full_ref[:, 4 * width :]
    turned = small.astype(F32).T
    gain1 = turned[n_exp : n_exp + 1, :]
    gain2 = turned[n_exp + 2 : n_exp + 3, :]
    if micro == 0:
        vec_s[...] = jnp.zeros(vec_s.shape, F32)

    def add_vec(at, value):
        vec_s[n_exp + at : n_exp + at + 1, :] += value

    along = lanes(rows, n_slots).astype(F32)
    chosen = ((along == table[:, 2:3]) | (along == table[:, 3:4])).astype(F32).astype(BF16)
    tails = dt[...].astype(F32)
    spare = round_up(tails.shape[0], 128) - tails.shape[0]
    if spare:
        tails = jnp.concatenate([tails, jnp.zeros((spare, tails.shape[1]), F32)], axis=0)
    tails = tails.T
    lane_slot = lanes(cap_pad, 128)
    me = lax.axis_index("expert")
    for block in range(reps * n_pos):
        at = slice(block * cap_pad, (block + 1) * cap_pad)
        lane = block * 16
        column = tails[0:cap_pad, lane : lane + 1] + tails[0:cap_pad, lane + 1 : lane + 2]
        expert = flip_all(me, block)
        dg_s[at, :] = jnp.where(lane_slot == expert, column, 0.0)
    dg = dg_s[...]
    dg_high = dg.astype(BF16)
    dg_low = (dg - dg_high.astype(F32)).astype(BF16)
    dgates = mm(chosen, dg_high) + mm(chosen, dg_low)
    routed = mm(chosen, db[...])
    gates = gate_ref[...]
    dlogits = (gates * (dgates - jnp.sum(gates * dgates, axis=1, keepdims=True))).astype(BF16)
    grad_small = mm_tn(a2_ref[...], dlogits)
    da2 = mm_nt(dlogits, small) + routed

    def norm_back(values, upstream, gain, at):
        normed, rate = norm_parts(values)
        add_vec(at, jnp.sum(upstream * normed, axis=0, keepdims=True))
        add_vec(at + 1, jnp.sum(upstream, axis=0, keepdims=True))
        scaled = upstream * gain
        return rate * (
            scaled
            - jnp.mean(scaled, axis=-1, keepdims=True)
            - normed * jnp.mean(scaled * normed, axis=-1, keepdims=True)
        )

    def add_grad(low, high, value):
        if micro == 0:
            grad_ref[:, low:high] = value
        else:
            grad_ref[:, low:high] += value

    dmid = c + norm_back(mid_ref[...], da2, gain2, 2)
    c_s[...] = dmid
    dbranch = dmid.astype(BF16)
    add_vec(6, jnp.sum(dbranch.astype(F32), axis=0, keepdims=True))
    add_grad(3 * width, 4 * width, mm_tn(mix_ref[...], dbranch))
    do_s[...] = mm_nt(dbranch, full_ref[:, 3 * width : 4 * width]).astype(BF16)
    hook()

    key_ok = lanes(pad, pad) < seq
    lane = lanes(pad, 128)
    scale = head ** (-0.5)
    for n in range(group):
        at = slice(n * pad, (n + 1) * pad)
        lse = lse_ref[at, :]
        for pair in range(width // 128):
            cols = pair * 128
            q2 = qkv_ref[at, cols : cols + 128]
            k2 = qkv_ref[at, width + cols : width + cols + 128]
            v2 = qkv_ref[at, 2 * width + cols : 2 * width + cols + 128]
            do2 = do_s[at, cols : cols + 128]
            dq2 = dk2 = dv2 = None
            for sub in range(per_pair):
                index = pair * per_pair + sub
                mine = (lane >= sub * head) & (lane < (sub + 1) * head)
                zero = jnp.zeros_like(q2)
                qh = jnp.where(mine, q2, zero)
                kh = jnp.where(mine, k2, zero)
                doh = jnp.where(mine, do2, zero)
                scores = jnp.where(key_ok, mm_nt(qh, k2), -jnp.inf)
                probs = jnp.exp(scores - lse[:, index : index + 1])
                dprobs = mm_nt(doh, v2)
                dscores = (probs * (dprobs - jnp.sum(probs * dprobs, axis=-1, keepdims=True))).astype(BF16)
                dv = mm_tn(probs.astype(BF16), doh)
                dq = mm(dscores, kh)
                dk = mm_tn(dscores, qh)
                dq2 = dq if dq2 is None else dq2 + dq
                dk2 = dk if dk2 is None else dk2 + dk
                dv2 = dv if dv2 is None else dv2 + dv
            dqkv_s[at, cols : cols + 128] = (dq2 * scale).astype(BF16)
            dqkv_s[at, width + cols : width + cols + 128] = dk2.astype(BF16)
            dqkv_s[at, 2 * width + cols : 2 * width + cols + 128] = dv2.astype(BF16)
        hook()
    dqkv = dqkv_s[...]
    add_grad(0, 3 * width, mm_tn(a1_ref[...], dqkv))
    add_vec(4, jnp.sum(dqkv[:, 0:width].astype(F32), axis=0, keepdims=True))
    add_vec(5, jnp.sum(dqkv[:, 2 * width :].astype(F32), axis=0, keepdims=True))
    da1 = mm_nt(dqkv, full_ref[:, 0 : 3 * width])
    x = load_group(tok_ref, order, micro, group, seq, pad, x_s)
    dx = c_s[...] + norm_back(x, da1, gain1, 0)
    for n in range(group):
        gtok_ref[micro * group + n] = dx[n * pad : n * pad + seq, :]
    if micro == MICRO - 1:
        grad_small = grad_small + vec_s[...].T
    add_grad(4 * width, 4 * width + 128, grad_small)


def third_kernel(dims, n_shard, orders, cuts, separate, *refs):
    n_img, seq, pad, group, n_pos, reps, cap, cap_pad, n_exp = dims
    batch_ref, tok_ref, cot_ref, full_ref, col_ref = refs[:5]
    states = (refs[5:12], refs[12:19])
    eo_ref, db_ref, dt_ref, gin_ref, gout_ref = refs[19:24]
    out_ref, gtok_ref, mine_ref, own_in_ref, own_out_ref = refs[24:29]
    (out_s, gtok_s, acc_in, acc_out, land_in, land_out, c_s, x_s, vec_s, dqkv_s, do_s, dg_s, grad_s, sends, recvs,
     load_sems, esend, erecv, send_sems, recv_sems) = refs[29:]
    top = n_pos * n_shard
    me = lax.axis_index("expert") * n_shard + lax.axis_index("shard")

    def place(index):
        return (index // n_shard, lax.rem(index, n_shard))

    greet(me, orders[0], n_shard)
    order = image_order(batch_ref, n_img)

    levels = n_shard.bit_length() - 1
    bases = [0]
    for level in range(levels):
        bases.append(bases[-1] + (n_shard >> (level + 1)) * reps)
    pieces = ((gin_ref, acc_in, land_in), (gout_ref, acc_out, land_out))
    arriving = {}
    sending = []

    def ship(kind, source, slot, bit):
        copy = pltpu.make_async_remote_copy(
            src_ref=source,
            dst_ref=pieces[kind][2].at[slot],
            send_sem=esend.at[kind, slot],
            recv_sem=erecv.at[kind, slot],
            device_id=place(flip(me, bit)),
            device_id_type=MESH,
        )
        copy.start()
        arriving[kind, slot] = copy
        sending.append(copy)

    loads = {}
    for rel in range(reps)[::-1]:
        for j in range(n_shard // 2):
            for kind in range(2):
                source, acc, _ = pieces[kind]
                ship(kind, source.at[(2 * j + 1) * reps + rel], j * reps + rel, 1)
                copy = pltpu.make_async_copy(
                    source.at[2 * j * reps + rel], acc.at[j * reps + rel], load_sems.at[kind, j * reps + rel]
                )
                copy.start()
                loads[kind, j * reps + rel] = copy

    def stage(level, rel):
        for kind in range(2):
            _, acc, land = pieces[kind]
            for j in list(range(n_shard >> (level + 1)))[::-1]:
                at = (j << level) * reps + rel
                slot = bases[level] + j * reps + rel
                if level == 0:
                    loads[kind, at].wait()
                arriving[kind, slot].wait_recv()
                acc[at] = (acc[at].astype(F32) + land[slot].astype(F32)).astype(BF16)
                if level + 1 < levels:
                    if j % 2:
                        ship(kind, acc.at[at], bases[level + 1] + j // 2 * reps + rel, 2 << level)
                elif rel:
                    ship(kind, acc.at[at], bases[levels], top)

    def last():
        total = []
        for kind in range(2):
            _, acc, land = pieces[kind]
            value = acc[0].astype(F32)
            if reps > 1:
                arriving[kind, bases[levels]].wait_recv()
                value = value + land[bases[levels]].astype(F32)
            total.append(value)
        own_in_ref[...] = total[0]
        own_out_ref[...] = total[1].T

    stages = [functools.partial(stage, level, rel) for level in range(levels) for rel in range(reps)[::-1]]

    def hook():
        if len(stages) > 1:
            stages.pop(0)()

    for micro in range(MICRO):
        backward_group(
            dims, micro, order, hook,
            (tok_ref, cot_ref, full_ref, col_ref[micro], states[micro], db_ref.at[micro], dt_ref.at[micro],
             gtok_s, grad_s, c_s, x_s, vec_s, dqkv_s, do_s, dg_s),
        )

    def combine(micro):
        combine_group(
            dims, micro, col_ref[micro], states[micro][5][...], states[micro][3][...], eo_ref[micro], out_s
        )

    if separate:
        for micro in range(MICRO):
            combine(micro)
        mine_ref[...] = grad_s[...]
    else:
        n_dev, chunk_rows = sends.shape[:2]
        copies = []

        def rows_of(chunk):
            return pl.ds(pl.multiple_of(chunk * chunk_rows, chunk_rows), chunk_rows)

        for step in range(len(orders[0])):
            started = []
            base = n_dev - (n_dev >> step)
            count = n_dev >> (step + 1)
            for part, bits in enumerate(orders):
                peer = flip(me, bits[step])
                low, high = cuts[part]
                for at, combo in enumerate(combos(bits[step + 1 :])):
                    sends[base + at, :, low:high] = grad_s[rows_of(flip_all(peer, combo)), low:high].astype(BF16)
                copy = pltpu.make_async_remote_copy(
                    src_ref=sends.at[base : base + count, :, low:high],
                    dst_ref=recvs.at[base : base + count, :, low:high],
                    send_sem=send_sems.at[part, step],
                    recv_sem=recv_sems.at[part, step],
                    device_id=place(peer),
                    device_id_type=MESH,
                )
                copy.start()
                started.append(copy)
            if step < MICRO:
                combine(step)
            for part, bits in enumerate(orders):
                low, high = cuts[part]
                started[part].wait_recv()
                for at, combo in enumerate(combos(bits[step + 1 :])):
                    grad_s[rows_of(flip_all(me, combo)), low:high] += recvs[base + at, :, low:high].astype(F32)
            copies.extend(started)
        mine_ref[...] = grad_s[rows_of(me), :]
        for copy in copies:
            copy.wait_send()
    for image, rank in enumerate(image_ranks(batch_ref, n_img)):
        out_ref[image] = out_s[rank]
        gtok_ref[image] = gtok_s[rank]
    while stages:
        stages.pop(0)()
    last()
    for copy in sending:
        copy.wait_send()


def run_third(dims, n_shard, batch, tokens, cotangent, full, cols, states, returned, grads, chunk_rows):
    n_img, seq, pad, group, n_pos, reps, cap, cap_pad, n_exp = dims
    width = tokens.shape[-1]
    rows = group * pad
    n_slots = reps * n_pos * cap_pad
    n_dev = n_exp * n_shard
    total = full.shape[1]
    ext, ff = grads[0].shape[1:]
    orders = [bits[::-1] for bits in bit_orders(n_exp, n_shard)]
    middle = total // 256 * 128
    cuts = ((0, middle), (middle, total))
    separate = chunk_rows % 16 != 0
    land = (n_shard - 1) * reps + 1
    mine = (width, total) if separate else (chunk_rows, total)
    buffer = (1, 16, 128) if separate else (n_dev, chunk_rows, total)
    return pl.pallas_call(
        functools.partial(third_kernel, dims, n_shard, orders, cuts, separate),
        out_shape=(
            jax.ShapeDtypeStruct((n_img, seq, width), BF16),
            jax.ShapeDtypeStruct((n_img, seq, width), F32),
            jax.ShapeDtypeStruct(mine, F32),
            jax.ShapeDtypeStruct((ext, ff), F32),
            jax.ShapeDtypeStruct((ff, width), F32),
        ),
        in_specs=[SMEM_SPEC] + [VMEM_SPEC] * 21 + [ANY_SPEC] * 2,
        out_specs=(VMEM_SPEC,) * 5,
        scratch_shapes=[
            pltpu.VMEM((n_img, seq, width), BF16),
            pltpu.VMEM((n_img, seq, width), F32),
            pltpu.VMEM((n_shard // 2 * reps, ext, ff), BF16),
            pltpu.VMEM((n_shard // 2 * reps, width, ff), BF16),
            pltpu.VMEM((land, ext, ff), BF16),
            pltpu.VMEM((land, width, ff), BF16),
            pltpu.VMEM((rows, width), F32),
            pltpu.VMEM((rows, width), F32),
            pltpu.VMEM((128, width), F32),
            pltpu.VMEM((rows, 3 * width), BF16),
            pltpu.VMEM((rows, width), BF16),
            pltpu.VMEM((n_slots, 128), F32),
            pltpu.VMEM((width, total), F32),
            pltpu.VMEM(buffer, BF16),
            pltpu.VMEM(buffer, BF16),
            pltpu.SemaphoreType.DMA((2, n_shard // 2 * reps)),
            pltpu.SemaphoreType.DMA((2, land)),
            pltpu.SemaphoreType.DMA((2, land)),
            pltpu.SemaphoreType.DMA((2, len(orders[0]))),
            pltpu.SemaphoreType.DMA((2, len(orders[0]))),
        ],
        compiler_params=pltpu.CompilerParams(
            collective_id=2, has_side_effects=True, vmem_limit_bytes=62 * 1024 * 1024
        ),
        cost_estimate=cost(20e9, 60e6, 4e6),
    )(batch, tokens, cotangent, full, cols, *states[0], *states[1], *returned, *grads)


def on_device(
    tokens, cotangent, routes, batch_of_image, w_qkv, w_attn_out, w_router, norm1_gain, norm1_bias, norm2_gain,
    norm2_bias, bias_query, bias_value, bias_attn_out, w_expert_in, w_expert_out, bias_expert_in, bias_expert_out,
):
    n_img, seq, width = tokens.shape
    n_expert = lax.axis_size("expert")
    n_shard = lax.axis_size("shard")
    n_dev = n_expert * n_shard
    group = n_img // MICRO
    pad = round_up(seq, 16)
    rows = group * pad
    cap = 16 * group * seq // (5 * n_expert)
    cap_pad = round_up(cap, 16)
    reps = 2 if n_expert > 1 else 1
    n_pos = n_expert // reps
    ff = w_expert_in.shape[2]
    dims = (n_img, seq, pad, group, n_pos, reps, cap, cap_pad, n_expert)
    my_shard = lax.axis_index("shard")

    vectors = jnp.concatenate(
        [norm1_gain, norm1_bias, norm2_gain, norm2_bias, bias_query, bias_value, bias_attn_out]
    ).reshape(7, -1).T
    blank = jnp.zeros((vectors.shape[0], 128 - n_expert - 7), BF16)
    packed = jnp.concatenate([w_qkv, w_attn_out, w_router, vectors, blank], axis=1)

    quarter = width // n_shard
    out_bias = jnp.where(jnp.arange(width) // quarter == my_shard, jnp.tile(bias_expert_out[0], n_shard), 0)
    tail = jnp.concatenate(
        [bias_expert_in, out_bias.astype(BF16).reshape(-1, ff), jnp.zeros((15 - width // ff, ff), BF16)], axis=0
    )
    own_in = jnp.concatenate([w_expert_in[0], tail], axis=0)

    cols, full, weights, slots, *states = run_first(
        dims, n_shard, batch_of_image, routes, tokens, cotangent, packed, own_in, w_expert_out[0]
    )
    eo, db, dt, grad_in, grad_out = run_second(dims, n_shard, (own_in, w_expert_out[0]), weights, slots)
    layer_out, gtok, mine, own_grad_in, own_grad_out = run_third(
        dims, n_shard, batch_of_image, tokens, cotangent, full, cols, states, (eo, db, dt), (grad_in, grad_out),
        packed.shape[0],
    )
    if mine.shape[0] != packed.shape[0]:
        mine = scatter_params(mine, n_expert, n_shard, 4)
    tail = own_grad_in[width:, :]
    out_bias_grad = tail[1 : 1 + width // ff, :].reshape(width)
    small = mine[:, 4 * width :]
    vec = [small[:, n_expert + i] for i in range(7)]
    return (
        layer_out,
        gtok,
        mine[:, 0 : 3 * width],
        mine[:, 3 * width : 4 * width],
        small[:, 0:n_expert],
        *vec,
        own_grad_in[0:width, :][None],
        own_grad_out[None],
        tail[0:1, :],
        lax.dynamic_slice(out_bias_grad, (my_shard * (width // n_shard),), (width // n_shard,))[None],
    )


def solution(mesh):
    both = ("expert", "shard")
    placed = (
        (P(both, None, None),) * 3
        + (P(both),)
        + (P(both, None),) * 3
        + (P(both),) * 7
        + (P("expert", None, "shard"), P("expert", "shard", None), P("expert", "shard"), P("expert", "shard"))
    )
    return jax.shard_map(
        on_device,
        mesh=mesh,
        in_specs=placed,
        out_specs=(P(both, None, None),) * 2
        + (P(both, None),) * 3
        + (P(both),) * 7
        + (P("expert", None, "shard"), P("expert", "shard", None), P("expert", "shard"), P("expert", "shard")),
        check_vma=False,
    )
```

```python
import functools
import math

import jax
import jax.numpy as jnp
from jax import lax
from jax.experimental import pallas as pl
from jax.experimental.pallas import tpu as pltpu
from jax.sharding import PartitionSpec as P

HEADS = 8
MICRO = 2
EPS = 1e-06
F32 = jnp.float32
BF16 = jnp.bfloat16
MESH = pl.DeviceIdType.MESH
OWN_FIRST = (0, 1, 2, 3)
STAGES_AT = {1: 1, 4: 1, 8: 1, 11: 2, 14: 1}
VMEM_LIMIT = 56 * 1024 * 1024
VMEM_SPEC = pl.BlockSpec(memory_space=pltpu.VMEM)
SMEM_SPEC = pl.BlockSpec(memory_space=pltpu.SMEM)
ANY_SPEC = pl.BlockSpec(memory_space=pl.ANY)


def round_up(value, unit):
    return (value + unit - 1) // unit * unit


def mm(left, right):
    return lax.dot_general(left, right, (((1,), (0,)), ((), ())), preferred_element_type=F32)


def mm_nt(left, right):
    return lax.dot_general(left, right, (((1,), (1,)), ((), ())), preferred_element_type=F32)


def mm_tn(left, right):
    return lax.dot_general(left, right, (((0,), (0,)), ((), ())), preferred_element_type=F32)


def cost(flops, nbytes, trans=0):
    return pl.CostEstimate(flops=int(flops), bytes_accessed=int(nbytes), transcendentals=int(trans))


def plain(name_cost):
    return dict(
        cost_estimate=name_cost,
        compiler_params=pltpu.CompilerParams(vmem_limit_bytes=VMEM_LIMIT),
    )


def image_ranks(batch_ref, n_img):
    keys = [batch_ref[i] * n_img + i for i in range(n_img)]
    ranks = []
    for i in range(n_img):
        rank = jnp.int32(0)
        for j in range(n_img):
            if j != i:
                rank = rank + jnp.where(keys[j] < keys[i], 1, 0)
        ranks.append(rank)
    return ranks


def image_order(batch_ref, n_img):
    ranks = image_ranks(batch_ref, n_img)
    order = []
    for k in range(n_img):
        place = jnp.int32(0)
        for i in range(n_img):
            place = place + jnp.where(ranks[i] == k, i, 0)
        order.append(place)
    return order


def flip(index, bit):
    return index + bit - 2 * bit * lax.rem(index // bit, 2)


def lanes(rows, width):
    return lax.broadcasted_iota(jnp.int32, (rows, width), 1)


def bit_orders(n_expert, n_shard):
    shard_bits = [1 << i for i in range(n_shard.bit_length() - 1)]
    expert_bits = [n_shard << i for i in range(n_expert.bit_length() - 1)]
    core = shard_bits[:1]
    across = shard_bits[1:]
    first = expert_bits[::-1] + across[::-1] + core
    second = expert_bits[:0:-1] + across[::-1] + expert_bits[:1] + core
    return first, second


def combos(bits):
    result = [0]
    for bit in bits:
        result = result + [held + bit for held in result]
    return result


def flip_all(index, combo):
    bit = 1
    while bit <= combo:
        if combo & bit:
            index = flip(index, bit)
        bit *= 2
    return index


def greet(me, bits, n_shard):
    barrier = pltpu.get_barrier_semaphore()
    for bit in bits:
        peer = flip_all(me, bit)
        pl.semaphore_signal(
            barrier, inc=1, device_id=(peer // n_shard, lax.rem(peer, n_shard)), device_id_type=MESH
        )
    pl.semaphore_wait(barrier, len(bits))


def gather_kernel(n_shard, orders, cuts, mine_ref, full_ref, local_sem, send_sems, recv_sems):
    me = lax.axis_index("expert") * n_shard + lax.axis_index("shard")
    greet(me, orders[0], n_shard)
    own = pltpu.make_async_copy(mine_ref, full_ref.at[me], local_sem)
    own.start()
    copies = []
    for step in range(len(orders[0])):
        started = []
        for part, order in enumerate(orders):
            bit = order[step]
            peer = flip(me, bit)
            low, high = cuts[part]
            for at, combo in enumerate(combos(order[:step])):
                chunk = flip_all(me, combo)
                source = mine_ref if combo == 0 else full_ref.at[chunk]
                copy = pltpu.make_async_remote_copy(
                    src_ref=source.at[:, low:high],
                    dst_ref=full_ref.at[chunk, :, low:high],
                    send_sem=send_sems.at[part, (1 << step) - 1 + at],
                    recv_sem=recv_sems.at[part, (1 << step) - 1 + at],
                    device_id=(peer // n_shard, lax.rem(peer, n_shard)),
                    device_id_type=MESH,
                )
                copy.start()
                started.append(copy)
        for copy in started:
            copy.wait_recv()
        copies.extend(started)
    for copy in copies:
        copy.wait_send()
    own.wait()


def gather_params(packed, n_expert, n_shard, collective_id):
    rows, width = packed.shape
    n_dev = n_expert * n_shard
    orders = bit_orders(n_expert, n_shard)
    middle = width // 256 * 128
    cuts = ((0, middle), (middle, width))
    full = pl.pallas_call(
        functools.partial(gather_kernel, n_shard, orders, cuts),
        out_shape=jax.ShapeDtypeStruct((n_dev, rows, width), packed.dtype),
        in_specs=[VMEM_SPEC],
        out_specs=VMEM_SPEC,
        scratch_shapes=[
            pltpu.SemaphoreType.DMA,
            pltpu.SemaphoreType.DMA((2, n_dev - 1)),
            pltpu.SemaphoreType.DMA((2, n_dev - 1)),
        ],
        compiler_params=pltpu.CompilerParams(
            collective_id=collective_id, has_side_effects=True, vmem_limit_bytes=VMEM_LIMIT
        ),
        cost_estimate=cost(1e6, 4 * n_dev * rows * width),
    )(packed)
    return full.reshape(n_dev * rows, width)


def scatter_kernel(n_shard, orders, cuts, full_ref, out_ref, acc, sends, recvs, send_sems, recv_sems):
    me = lax.axis_index("expert") * n_shard + lax.axis_index("shard")
    n_dev = full_ref.shape[0]
    greet(me, orders[0], n_shard)
    n_steps = len(orders[0])
    acc[...] = full_ref[...]
    copies = []
    for step in range(n_steps):
        started = []
        base = n_dev - (n_dev >> step)
        count = n_dev >> (step + 1)
        for part, order in enumerate(orders):
            bit = order[step]
            peer = flip(me, bit)
            low, high = cuts[part]
            for at, combo in enumerate(combos(order[step + 1 :])):
                chunk = flip_all(peer, combo)
                sends[base + at, :, low:high] = acc[chunk, :, low:high].astype(BF16)
            copy = pltpu.make_async_remote_copy(
                src_ref=sends.at[base : base + count, :, low:high],
                dst_ref=recvs.at[base : base + count, :, low:high],
                send_sem=send_sems.at[part, step],
                recv_sem=recv_sems.at[part, step],
                device_id=(peer // n_shard, lax.rem(peer, n_shard)),
                device_id_type=MESH,
            )
            copy.start()
            started.append(copy)
        for part, order in enumerate(orders):
            low, high = cuts[part]
            started[part].wait_recv()
            for at, combo in enumerate(combos(order[step + 1 :])):
                chunk = flip_all(me, combo)
                acc[chunk, :, low:high] += recvs[base + at, :, low:high].astype(F32)
        copies.extend(started)
    out_ref[...] = acc[me]
    for copy in copies:
        copy.wait_send()


def scatter_params(full, n_expert, n_shard, collective_id):
    n_dev = n_expert * n_shard
    width = full.shape[1]
    rows = full.shape[0] // n_dev
    gather_orders = bit_orders(n_expert, n_shard)
    orders = [order[::-1] for order in gather_orders]
    middle = width // 256 * 128
    cuts = ((0, middle), (middle, width))
    return pl.pallas_call(
        functools.partial(scatter_kernel, n_shard, orders, cuts),
        out_shape=jax.ShapeDtypeStruct((rows, width), F32),
        in_specs=[VMEM_SPEC],
        out_specs=VMEM_SPEC,
        scratch_shapes=[
            pltpu.VMEM((n_dev, rows, width), F32),
            pltpu.VMEM((n_dev, rows, width), BF16),
            pltpu.VMEM((n_dev, rows, width), BF16),
            pltpu.SemaphoreType.DMA((2, len(orders[0]))),
            pltpu.SemaphoreType.DMA((2, len(orders[0]))),
        ],
        compiler_params=pltpu.CompilerParams(
            collective_id=collective_id, has_side_effects=True, vmem_limit_bytes=VMEM_LIMIT
        ),
        cost_estimate=cost(1e6, 8 * n_dev * rows * width),
    )(full.reshape(n_dev, rows, width))


def route_tables(dims, rt_s):
    n_img, seq, pad, group, n_pos, reps, cap, cap_pad, n_exp = dims
    rows = group * pad
    lower = (
        lax.broadcasted_iota(jnp.int32, (rows, rows), 0)
        > lax.broadcasted_iota(jnp.int32, (rows, rows), 1)
    ).astype(F32).astype(BF16)
    ids = lanes(rows, 128)
    me = lax.axis_index("expert")
    first = rt_s[:, 0:1]
    second = rt_s[:, 1:2]
    hot_first = (ids == first).astype(F32)
    hot_second = (ids == second).astype(F32)
    earlier_first = mm(lower, hot_first.astype(BF16))
    earlier_second = mm(lower, hot_second.astype(BF16)) + jnp.sum(hot_first, axis=0, keepdims=True)
    table = jnp.where(ids == 0, first.astype(F32), jnp.where(ids == 1, second.astype(F32), 0.0))
    for lane, route, hot, earlier in (
        (2, first, hot_first, earlier_first),
        (3, second, hot_second, earlier_second),
    ):
        slot = jnp.sum(hot * earlier, axis=1, keepdims=True)
        away = jnp.bitwise_xor(jnp.maximum(route, 0), jnp.broadcast_to(me, route.shape)).astype(F32)
        target = away * float(cap_pad) + slot
        target = jnp.where((slot < float(cap)) & (route >= 0), target, -1.0)
        table = jnp.where(ids == lane, target, table)
    spare = round_up(rows, 128) - rows
    turned = jnp.concatenate([table, jnp.full((spare, 128), -1.0, F32)], axis=0).T
    return table, turned[2:3, 0:rows], turned[3:4, 0:rows]


def norm_parts(values):
    center = values - jnp.mean(values, axis=-1, keepdims=True)
    rate = lax.rsqrt(jnp.mean(center * center, axis=-1, keepdims=True) + EPS)
    return center * rate, rate


def load_group(ref, order, micro, group, seq, pad, buf):
    buf[...] = jnp.zeros(buf.shape, F32)
    for n in range(group):
        buf[n * pad : n * pad + seq, :] = ref[order[micro * group + n]].astype(F32)
    return buf[...]


def attention_forward(dims, x, full_ref, out):
    n_img, seq, pad, group, n_pos, reps, cap, cap_pad, n_exp = dims
    a1_ref, qkv_ref, mix_ref, mid_ref, a2_ref, gate_ref, lse_ref = out
    rows = group * pad
    width = x.shape[-1]
    head = width // HEADS
    per_pair = 128 // head
    small = full_ref[:, 4 * width :]
    turned = small.astype(F32).T
    gain1, shift1, gain2, shift2, bias_q, bias_v, bias_o = [
        turned[n_exp + i : n_exp + i + 1, :] for i in range(7)
    ]
    normed, _ = norm_parts(x)
    a1 = (normed * gain1 + shift1).astype(BF16)
    a1_ref[...] = a1
    proj = mm(a1, full_ref[:, 0 : 3 * width])
    scale = head ** (-0.5)
    qkv_ref[:, 0:width] = ((proj[:, 0:width] + bias_q).astype(BF16).astype(F32) * scale).astype(BF16)
    qkv_ref[:, width : 2 * width] = proj[:, width : 2 * width].astype(BF16)
    qkv_ref[:, 2 * width :] = (proj[:, 2 * width :] + bias_v).astype(BF16)
    key_ok = lanes(pad, pad) < seq
    lane = lanes(pad, 128)
    for n in range(group):
        at = slice(n * pad, (n + 1) * pad)
        lse = jnp.zeros((pad, 128), F32)
        for pair in range(width // 128):
            cols = pair * 128
            q2 = qkv_ref[at, cols : cols + 128]
            k2 = qkv_ref[at, width + cols : width + cols + 128]
            v2 = qkv_ref[at, 2 * width + cols : 2 * width + cols + 128]
            mixed = None
            for sub in range(per_pair):
                mine = (lane >= sub * head) & (lane < (sub + 1) * head)
                scores = mm_nt(jnp.where(mine, q2, jnp.zeros_like(q2)), k2)
                scores = jnp.where(key_ok, scores, -jnp.inf)
                top = jnp.max(scores, axis=-1, keepdims=True)
                grown = jnp.exp(scores - top)
                total = jnp.sum(grown, axis=-1, keepdims=True)
                probs = (grown / total).astype(BF16)
                part = mm(probs, jnp.where(mine, v2, jnp.zeros_like(v2)))
                mixed = part if mixed is None else mixed + part
                lse = jnp.where(lane == pair * per_pair + sub, top + jnp.log(total), lse)
            mix_ref[at, cols : cols + 128] = mixed.astype(BF16)
        lse_ref[at, :] = lse
    mid = x + mm(mix_ref[...], full_ref[:, 3 * width : 4 * width]) + bias_o
    mid_ref[...] = mid
    normed2, _ = norm_parts(mid)
    a2 = (normed2 * gain2 + shift2).astype(BF16)
    a2_ref[...] = a2
    ids = lanes(rows, 128)
    logits = jnp.where(ids < n_exp, mm(a2, small), -jnp.inf)
    grown = jnp.exp(logits - jnp.max(logits, axis=-1, keepdims=True))
    gates = grown / jnp.sum(grown, axis=-1, keepdims=True)
    gate_ref[...] = gates


def fill_message(dims, table, gates, a2, chosen, send_ref, tail_ref):
    n_img, seq, pad, group, n_pos, reps, cap, cap_pad, n_exp = dims
    rows = group * pad
    part = n_pos * cap_pad
    ids = lanes(rows, 128).astype(F32)
    gate1 = jnp.sum(jnp.where(ids == table[:, 0:1], gates, 0.0), axis=1, keepdims=True)
    gate2 = jnp.sum(jnp.where(ids == table[:, 1:2], gates, 0.0), axis=1, keepdims=True)
    to1, to2 = table[:, 2:3], table[:, 3:4]
    send_ref[...] = mm(chosen, a2).astype(BF16)
    tail_ref[...] = jnp.zeros(tail_ref.shape, BF16)
    along = lanes(rows, part)
    tail_id = lax.broadcasted_iota(jnp.int32, (16, cap_pad), 0)
    tails = [jnp.zeros((16, cap_pad), F32) for _ in range(n_pos)]
    for rel in range(reps):
        there = (along + rel * part).astype(F32)
        gate_row = jnp.sum(
            jnp.where(there == to1, gate1, 0.0) + jnp.where(there == to2, gate2, 0.0), axis=0, keepdims=True
        )
        high = gate_row.astype(BF16).astype(F32)
        low = gate_row - high
        for pos in range(n_pos):
            at = slice(pos * cap_pad, (pos + 1) * cap_pad)
            tails[pos] = jnp.where(
                tail_id == 2 * rel, high[:, at], jnp.where(tail_id == 2 * rel + 1, low[:, at], tails[pos])
            )
    for pos in range(n_pos):
        tail_ref[pos * 16 : (pos + 1) * 16, 0:cap_pad] = tails[pos].astype(BF16)


class Messages:
    def __init__(self, n_shard, me, n_pos, reps, cap_pad):
        self.n_shard, self.me, self.n_pos, self.reps, self.cap_pad = n_shard, me, n_pos, reps, cap_pad
        self.pending = []

    def move(self, source, target, send_sem, recv_sem, pos):
        if pos == 0:
            copy = pltpu.make_async_copy(source, target, recv_sem)
            copy.start()
            self.pending.append((copy, False))
        else:
            peer = flip_all(self.me, pos * self.n_shard)
            copy = pltpu.make_async_remote_copy(
                src_ref=source,
                dst_ref=target,
                send_sem=send_sem,
                recv_sem=recv_sem,
                device_id=(peer // self.n_shard, lax.rem(peer, self.n_shard)),
                device_id_type=MESH,
            )
            copy.start()
            self.pending.append((copy, True))
        return copy, pos > 0

    def rows(self, source, target, send_sems, recv_sems, rels=None):
        started = []
        for rel in range(self.reps) if rels is None else rels:
            for pos in range(self.n_pos):
                block = rel * self.n_pos + pos
                at = pl.ds(block * self.cap_pad, self.cap_pad)
                started.append(
                    self.move(source.at[at], target.at[at], send_sems.at[block], recv_sems.at[block], pos)
                )
        return started

    def tails(self, source, target, send_sems, recv_sems, blocks):
        started = []
        for block in blocks:
            at = pl.ds(block * 16, 16)
            started.append(
                self.move(source.at[at], target.at[at], send_sems.at[block], recv_sems.at[block], block % self.n_pos)
            )
        return started


def arrive(started):
    for copy, remote in started:
        if remote:
            copy.wait_recv()
        else:
            copy.wait()


def arrive_remote(started):
    arrive([member for member in started if member[1]])


def leave(started):
    for copy, remote in started:
        if remote:
            copy.wait_send()


def first_kernel(dims, n_shard, orders, cuts, gathered, *refs):
    n_img, seq, pad, group, n_pos, reps, cap, cap_pad, n_exp = dims
    (batch_ref, routes_ref, tok_ref, cot_ref, packed_ref, own_in_ref, own_out_ref) = refs[:7]
    refs = refs[7:]
    col_ref, full_out, win_ref, wout_ref, buf_ref, tail_ref, cot_slots_ref = refs[:7]
    next_out, next_tail_out, next_cot_out = refs[7:10]
    state_outs = (refs[10:17], refs[17:24])
    refs = refs[24:]
    states = (refs[0:7], refs[7:14])
    (next_ref, next_tail_ref, next_cot_ref, full_s, x_s, rt_s, chosen_s, asend, tsend, csend, keep_sems, own_sem,
     gsend, grecv, wsend, wrecv, dsend, drecv) = refs[14:]
    full_ref = packed_ref if gathered else full_s
    kept_copies = []

    def keep(source, target):
        copy = pltpu.make_async_copy(source, target, keep_sems.at[len(kept_copies)])
        copy.start()
        kept_copies.append(copy)

    rows = group * pad
    n_slots = reps * n_pos * cap_pad
    top = n_pos * n_shard
    expert, shard = lax.axis_index("expert"), lax.axis_index("shard")
    me = expert * n_shard + shard

    def place(index):
        return (index // n_shard, lax.rem(index, n_shard))

    peers = sorted(set(orders[0]) | {pos * n_shard for pos in range(1, n_pos)})
    barrier = pltpu.get_barrier_semaphore()
    for peer in peers:
        pl.semaphore_signal(barrier, inc=1, device_id=place(flip_all(me, peer)), device_id_type=MESH)
    pl.semaphore_wait(barrier, len(peers))

    chunk_rows = full_ref.shape[0] // (n_exp * n_shard) if not gathered else 0
    gather_copies = []

    def at_chunk(ref, index, low, high):
        return ref.at[pl.ds(pl.multiple_of(index * chunk_rows, chunk_rows), chunk_rows), low:high]

    def gather_start(step):
        for part, order in enumerate(orders):
            low, high = cuts[part]
            for at, combo in enumerate(combos(order[:step])):
                chunk = flip_all(me, combo)
                source = packed_ref.at[:, low:high] if combo == 0 else at_chunk(full_ref, chunk, low, high)
                sem = (1 << step) - 1 + at
                copy = pltpu.make_async_remote_copy(
                    src_ref=source,
                    dst_ref=at_chunk(full_ref, chunk, low, high),
                    send_sem=gsend.at[part, sem],
                    recv_sem=grecv.at[part, sem],
                    device_id=place(flip(me, order[step])),
                    device_id_type=MESH,
                )
                copy.start()
                gather_copies.append(copy)

    def gather_next(step):
        if gathered:
            return
        count = 2 * (1 << step)
        for copy in gather_copies[-count:]:
            copy.wait_recv()
        if step + 1 < len(orders[0]):
            gather_start(step + 1)

    if not gathered:
        gather_start(0)
        own = pltpu.make_async_copy(packed_ref, at_chunk(full_ref, me, 0, full_ref.shape[1]), own_sem)
        own.start()

    bits = ([top] if reps > 1 else []) + [1 << i for i in range(n_shard.bit_length() - 1)][::-1]

    def number(held):
        return (held // top) * n_shard + held % top

    weight_copies = {}

    ext, ff = own_in_ref.shape
    spans = [(0, 0, ext // 32 * 16), (0, ext // 32 * 16, ext), (1, 0, ff // 32 * 16), (1, ff // 32 * 16, ff)]

    def weights_start(span, held, bit):
        kind, low, high = spans[span]
        at = pl.ds(low, high - low)
        source = ((own_in_ref, own_out_ref)[kind]) if held == 0 else (win_ref, wout_ref)[kind].at[number(held)]
        to = number(held + bit)
        copy = pltpu.make_async_remote_copy(
            src_ref=source.at[at],
            dst_ref=(win_ref, wout_ref)[kind].at[to, at],
            send_sem=wsend.at[span, to],
            recv_sem=wrecv.at[span, to],
            device_id=place(flip(me, bit)),
            device_id_type=MESH,
        )
        copy.start()
        weight_copies[span, held + bit] = copy

    def weights_pass(span, held):
        weight_copies[span, held].wait_recv()
        last = min(bit for bit in bits if held & bit)
        for bit in bits:
            if bit < last:
                weights_start(span, held, bit)

    inner_bits = [bit for bit in bits if bit < top]
    if reps > 1:
        weights_start(0, 0, top)
        weights_start(1, 0, top)
    for span in OWN_FIRST:
        for bit in inner_bits:
            weights_start(span, 0, bit)

    order = image_order(batch_ref, n_img)
    messages = Messages(n_shard, me, n_pos, reps, cap_pad)
    arrivals = []

    n_steps = len(orders[0])
    step = 0
    tables = []
    for micro in range(MICRO):
        rt_s[...] = jnp.full(rt_s.shape, -1, jnp.int32)
        for n in range(group):
            rt_s[n * pad : n * pad + seq, 0:2] = routes_ref[order[micro * group + n]]
        table, row_first, row_second = route_tables(dims, rt_s)
        col_ref[micro] = table
        if step < n_steps:
            gather_next(step)
            step += 1
        cot = load_group(cot_ref, order, micro, group, seq, pad, x_s).astype(BF16)
        here = lax.broadcasted_iota(jnp.int32, (n_slots, rows), 0).astype(F32)
        chosen = ((here == row_first) | (here == row_second)).astype(F32).astype(BF16)
        chosen_s[micro] = chosen
        if micro == 0:
            csend[...] = mm(chosen, cot).astype(BF16)
            arrivals += messages.rows(csend, cot_slots_ref, dsend.at[0], drecv.at[0])
        else:
            next_cot_ref[...] = mm(chosen, cot).astype(BF16)
            keep(next_cot_ref, next_cot_out)
        if step < n_steps:
            gather_next(step)
            step += 1
    if reps > 1:
        weights_start(2, 0, top)
    while step < n_steps:
        gather_next(step)
        step += 1
    if not gathered:
        own.wait()
        keep(full_ref, full_out)
    if reps > 1:
        for span in range(2):
            weights_pass(span, top)
        weights_start(3, 0, top)
    for span in range(4):
        if span not in OWN_FIRST:
            for bit in inner_bits:
                weights_start(span, 0, bit)
    inner = sorted((held for held in combos(bits) if held and not held & 1), key=lambda h: (-(h & -h), h))
    early = [held for held in inner if held < top]
    late = [held for held in inner if held > top]
    for micro in range(MICRO):
        x = load_group(tok_ref, order, micro, group, seq, pad, x_s)
        attention_forward(dims, x, full_ref, states[micro])
        table = col_ref[micro]
        gates = states[micro][5][...]
        a2 = states[micro][4][...]
        if micro == 0:
            fill_message(dims, table, gates, a2, chosen_s[micro], asend, tsend)
            arrivals += messages.rows(asend, buf_ref, dsend.at[1], drecv.at[1])
            arrivals += messages.tails(tsend, tail_ref, dsend.at[2], drecv.at[2], range(n_pos))
        else:
            fill_message(dims, table, gates, a2, chosen_s[micro], next_ref, next_tail_ref)
            keep(next_ref, next_out)
            keep(next_tail_ref, next_tail_out)
        for held, kept in zip(states[micro], state_outs[micro]):
            keep(held, kept)
    for span in range(4):
        for held in early:
            weights_pass(span, held)
        if reps > 1 and span >= 2:
            weights_pass(span, top)
        if span < 2:
            for held in late:
                weights_pass(span, held)
    for span in range(2, 4):
        for held in late:
            weights_pass(span, held)
    for (_, held), copy in weight_copies.items():
        if held & 1:
            copy.wait_recv()
    arrive(arrivals)
    leave(arrivals)
    for copy in kept_copies:
        copy.wait()
    for copy in gather_copies:
        copy.wait_send()
    for copy in weight_copies.values():
        copy.wait_send()


def run_first(dims, n_shard, batch, routes, tokens, cotangent, packed, own_in, own_out):
    n_img, seq, pad, group, n_pos, reps, cap, cap_pad, n_exp = dims
    width = tokens.shape[-1]
    rows = group * pad
    n_slots = reps * n_pos * cap_pad
    tail_wide = round_up(cap_pad, 128)
    n_dev = n_exp * n_shard
    n_pieces = reps * n_shard
    total = packed.shape[1]
    orders = bit_orders(n_exp, n_shard)
    middle = total // 256 * 128
    cuts = ((0, middle), (middle, total))
    gathered = packed.shape[0] % 16 != 0
    if gathered:
        packed = gather_params(packed, n_exp, n_shard, 3)
    state = (
        jax.ShapeDtypeStruct((rows, width), BF16),
        jax.ShapeDtypeStruct((rows, 3 * width), BF16),
        jax.ShapeDtypeStruct((rows, width), BF16),
        jax.ShapeDtypeStruct((rows, width), F32),
        jax.ShapeDtypeStruct((rows, width), BF16),
        jax.ShapeDtypeStruct((rows, 128), F32),
        jax.ShapeDtypeStruct((rows, 128), F32),
    )
    full_rows = 16 if gathered else n_dev * packed.shape[0]
    out = pl.pallas_call(
        functools.partial(first_kernel, dims, n_shard, orders, cuts, gathered),
        out_shape=(
            jax.ShapeDtypeStruct((MICRO, rows, 128), F32),
            jax.ShapeDtypeStruct((full_rows, total), BF16),
            jax.ShapeDtypeStruct((n_pieces,) + own_in.shape, BF16),
            jax.ShapeDtypeStruct((n_pieces,) + own_out.shape, BF16),
            jax.ShapeDtypeStruct((n_slots, width), BF16),
            jax.ShapeDtypeStruct((n_pos * 16, tail_wide), BF16),
            jax.ShapeDtypeStruct((n_slots, width), BF16),
            jax.ShapeDtypeStruct((n_slots, width), BF16),
            jax.ShapeDtypeStruct((n_pos * 16, tail_wide), BF16),
            jax.ShapeDtypeStruct((n_slots, width), BF16),
            *state,
            *state,
        ),
        in_specs=[SMEM_SPEC] + [VMEM_SPEC] * 4 + [ANY_SPEC] * 2,
        out_specs=(VMEM_SPEC,) + (ANY_SPEC,) * 23,
        scratch_shapes=[
            *[pltpu.VMEM(shape.shape, shape.dtype) for shape in state + state],
            pltpu.VMEM((n_slots, width), BF16),
            pltpu.VMEM((n_pos * 16, tail_wide), BF16),
            pltpu.VMEM((n_slots, width), BF16),
            pltpu.VMEM((full_rows, total), BF16),
            pltpu.VMEM((rows, width), F32),
            pltpu.VMEM((rows, 128), jnp.int32),
            pltpu.VMEM((MICRO, n_slots, rows), BF16),
            pltpu.VMEM((n_slots, width), BF16),
            pltpu.VMEM((n_pos * 16, tail_wide), BF16),
            pltpu.VMEM((n_slots, width), BF16),
            pltpu.SemaphoreType.DMA((18,)),
            pltpu.SemaphoreType.DMA,
            pltpu.SemaphoreType.DMA((2, n_dev - 1)),
            pltpu.SemaphoreType.DMA((2, n_dev - 1)),
            pltpu.SemaphoreType.DMA((4, n_pieces)),
            pltpu.SemaphoreType.DMA((4, n_pieces)),
            pltpu.SemaphoreType.DMA((4, n_exp)),
            pltpu.SemaphoreType.DMA((4, n_exp)),
        ],
        compiler_params=pltpu.CompilerParams(
            collective_id=0, has_side_effects=True, vmem_limit_bytes=VMEM_LIMIT
        ),
        cost_estimate=cost(20e9, 60e6, 4e6),
    )(batch, routes, tokens, cotangent, packed, own_in, own_out)
    return out[0], packed if gathered else out[1], out[2:4], out[4:10], out[10:17], out[17:24]


def gelu_pair(v):
    size = jnp.abs(v)
    bell = jnp.exp(v * v * -0.5)
    t = 1.0 / (1.0 + (0.3275911 / math.sqrt(2.0)) * size)
    series = t * (
        0.5 * 0.254829592
        + t * (0.5 * -0.284496736 + t * (0.5 * 1.421413741 + t * (0.5 * -1.453152027 + t * (0.5 * 1.061405429))))
    )
    tail = series * bell
    share = jnp.where(v >= 0.0, 1.0 - tail, tail)
    return v * share, share + v * bell * (1.0 / math.sqrt(2.0 * math.pi))


def second_kernel(dims, n_shard, chunk, *refs):
    n_img, seq, pad, group, n_pos, reps, cap, cap_pad, n_exp = dims
    own_in_ref, own_out_ref, win_ref, wout_ref, buf0, tail0, cot0, next_ref, next_tail_ref, next_cot_ref = refs[:10]
    eo_ret, eo_next, db_ret, dt_ret, gin_ref, gout_ref, gin_core, gout_core = refs[10:18]
    (buf1, tail1, cot1, w_in, w_out, hid_s, dh_s, deo_s, pre, back, eo_acc, db_acc, eo_send, db_send, dt_send,
     turned_s, gin_s, wsems, dsend, drecv, rsend, rrecv, gsems, hsend, hrecv) = refs[18:]
    width = buf0.shape[-1]
    ff = win_ref.shape[-1]
    part = n_pos * cap_pad
    n_pieces = reps * n_shard
    n_chunks = n_shard * ff // chunk
    expert, shard = lax.axis_index("expert"), lax.axis_index("shard")
    me = expert * n_shard + shard
    peers = [1] + [pos * n_shard for pos in range(1, n_pos)]
    if peers:
        barrier = pltpu.get_barrier_semaphore()
        for peer in peers:
            to = flip_all(me, peer)
            pl.semaphore_signal(
                barrier, inc=1, device_id=(to // n_shard, lax.rem(to, n_shard)), device_id_type=MESH
            )
        pl.semaphore_wait(barrier, len(peers))
    messages = Messages(n_shard, me, n_pos, reps, cap_pad)

    def come(rel):
        started = messages.rows(next_ref, buf1, dsend.at[0], drecv.at[0], (rel,))
        started += messages.rows(next_cot_ref, cot1, dsend.at[1], drecv.at[1], (rel,))
        if rel == 0:
            started += messages.tails(next_tail_ref, tail1, dsend.at[2], drecv.at[2], range(n_pos))
        return started

    coming = [come(0)]
    loads = []
    for rel in range(reps):
        for s in range(n_shard):
            piece = rel * n_shard + s
            cols = pl.ds(s * ff, ff)
            from_in = win_ref.at[piece] if piece else own_in_ref
            from_out = wout_ref.at[piece] if piece else own_out_ref
            copies = (
                pltpu.make_async_copy(from_in, w_in.at[rel, :, cols], wsems.at[0, piece]),
                pltpu.make_async_copy(from_out, w_out.at[rel, cols, :], wsems.at[1, piece]),
            )
            for copy in copies:
                copy.start()
            loads.append(copies)
    returns = ([], [])
    tail_id = lax.broadcasted_iota(jnp.int32, (16, cap_pad), 0)
    ones = jnp.ones((16, width), BF16)
    db_tail_wide = dt_send.shape[-1]
    for micro in range(MICRO):
        buf, tail, cot = ((buf0, tail0, cot0), (buf1, tail1, cot1))[micro]
        if micro == 1:
            arrive(coming[0])
        tails = tail[...].astype(F32)
        spare = round_up(n_pos * 16, 128) - n_pos * 16
        if spare:
            tails = jnp.concatenate([tails, jnp.zeros((spare, tails.shape[1]), F32)], axis=0)
        turned = tails.T
        for rel in range(reps):
            if micro > 0 and rel > 0:
                arrive(coming[rel])
            for pos in range(n_pos):
                at = slice(rel * part + pos * cap_pad, rel * part + (pos + 1) * cap_pad)
                lane = pos * 16 + 2 * rel
                gate = turned[0:cap_pad, lane : lane + 1] + turned[0:cap_pad, lane + 1 : lane + 2]
                deo_s[micro, at, :] = (cot[at, :].astype(F32) * gate).astype(BF16)
            if micro == 0:
                for s in range(n_shard):
                    for copy in loads[rel * n_shard + s]:
                        copy.wait()
            bias = w_in[rel, width : width + 16, :].astype(F32)
            bias_out = None
            for s in range(n_shard):
                row = jnp.concatenate(
                    [bias[1 + i : 2 + i, s * ff : (s + 1) * ff] for i in range(width // ff)], axis=1
                )
                bias_out = row if bias_out is None else bias_out + row
            if micro > 0:
                leave(returns[0][rel])
                arrive([member for member in returns[0][rel] if not member[1]])
            for pos_low in range(0, n_pos, pre.shape[0] // cap_pad):
                here = slice(rel * part + pos_low * cap_pad, rel * part + pos_low * cap_pad + pre.shape[0])
                kept = slice(micro * part + pos_low * cap_pad, micro * part + pos_low * cap_pad + pre.shape[0])
                eo_acc[...] = jnp.broadcast_to(bias_out, eo_acc.shape)
                db_acc[...] = jnp.zeros(db_acc.shape, F32)

                def piece(c, carry, rel=rel, micro=micro, here=here, kept=kept, buf=buf):
                    cols = pl.ds(pl.multiple_of(c * chunk, chunk), chunk)
                    bias = w_in[rel, width : width + 16, cols].astype(F32)[0:1, :]
                    pre[...] = mm(buf[here, :], w_in[rel, 0:width, cols])
                    back[...] = mm_nt(deo_s[micro, here, :], w_out[rel, cols, :])
                    for pos in range(pre.shape[0] // cap_pad):
                        at = slice(pos * cap_pad, (pos + 1) * cap_pad)
                        to = slice(kept.start + pos * cap_pad, kept.start + (pos + 1) * cap_pad)
                        value, slope = gelu_pair(pre[at, :] + bias)
                        hid_s[rel, to, cols] = value.astype(BF16)
                        dh_s[rel, to, cols] = (back[at, :] * slope).astype(BF16)
                    eo_acc[...] += mm(hid_s[rel, kept, cols], w_out[rel, cols, :])
                    db_acc[...] += mm_nt(dh_s[rel, kept, cols], w_in[rel, 0:width, cols])
                    return carry

                lax.fori_loop(0, n_chunks, piece, 0)
                for pos in range(pos_low, pos_low + pre.shape[0] // cap_pad):
                    at = slice((pos - pos_low) * cap_pad, (pos - pos_low + 1) * cap_pad)
                    to = slice(rel * part + pos * cap_pad, rel * part + (pos + 1) * cap_pad)
                    eo = eo_acc[at, :].astype(BF16)
                    eo_send[to, :] = eo
                    db_send[to, :] = db_acc[at, :].astype(BF16)
                    product = cot[to, :].astype(F32) * eo.astype(F32)
                    high = product.astype(BF16)
                    low = (product - high.astype(F32)).astype(BF16)
                    dgate = mm_nt(ones, high) + mm_nt(ones, low)
                    dg_high = dgate.astype(BF16).astype(F32)
                    block = rel * n_pos + pos
                    rows16 = slice(block * 16, (block + 1) * 16)
                    dt_send[micro, rows16, :] = jnp.zeros((16, db_tail_wide), BF16)
                    dt_send[micro, rows16, 0:cap_pad] = jnp.where(
                        tail_id == 0, dg_high, jnp.where(tail_id == 1, dgate - dg_high, 0.0)
                    ).astype(BF16)
            if micro == 0 and rel + 1 < reps:
                coming.append(come(rel + 1))
            blocks = range(rel * n_pos, (rel + 1) * n_pos)
            sent = messages.rows(db_send, db_ret.at[micro], rsend.at[micro, 0], rrecv.at[micro, 0], (rel,))
            sent += messages.tails(
                dt_send.at[micro], dt_ret.at[micro], rsend.at[micro, 1], rrecv.at[micro, 1], blocks
            )
            if micro == 0:
                sent += messages.rows(eo_send, eo_ret, rsend.at[micro, 2], rrecv.at[micro, 2], (rel,))
            else:
                at = pl.ds(rel * part, part)
                copy = pltpu.make_async_copy(eo_send.at[at], eo_next.at[at], rrecv.at[micro, 2, rel])
                copy.start()
                sent.append((copy, False))
            returns[micro].append(sent)

    stores = []
    crossing = []
    core_peer = flip(me, 1)

    def store(kind, slot, c, rel):
        staged = (gin_s, gin_s.at[:, 0:width, :])[kind]
        started = []
        for s in range(c * chunk // ff, (c + 1) * chunk // ff):
            index = s // 2 * reps + rel
            source = staged.at[slot, :, pl.ds(s * ff - c * chunk, ff)]
            if s % 2:
                copy = pltpu.make_async_remote_copy(
                    src_ref=source,
                    dst_ref=(gin_core, gout_core)[kind].at[index],
                    send_sem=hsend.at[kind, index],
                    recv_sem=hrecv.at[kind, index],
                    device_id=(core_peer // n_shard, lax.rem(core_peer, n_shard)),
                    device_id_type=MESH,
                )
                crossing.append(copy)
            else:
                copy = pltpu.make_async_copy(source, (gin_ref, gout_ref)[kind].at[index], gsems.at[kind, index])
            copy.start()
            started.append((copy, s % 2 == 1))
        stores.append(started)

    def stored(started):
        for copy, remote in started:
            if remote:
                copy.wait_send()
            else:
                copy.wait()

    def next_slot():
        if len(stores) >= 2:
            stored(stores[-2])
        return len(stores) % 2

    wide_id = lax.broadcasted_iota(jnp.int32, (16, ff), 0)
    for rel in range(reps)[::-1]:
        here = slice(rel * part, (rel + 1) * part)
        deo_bias = None
        for micro, buf in enumerate((buf0, buf1)):
            turned_s[:, micro * part : (micro + 1) * part] = buf[here, :].T
            total = jnp.sum(deo_s[micro, here, :].astype(F32), axis=0, keepdims=True)
            deo_bias = total if deo_bias is None else deo_bias + total
        for c in range(n_chunks):
            cols = slice(c * chunk, (c + 1) * chunk)
            slot = next_slot()
            dh = dh_s[rel, :, cols]
            gin_s[slot, 0:width, :] = mm(turned_s[...], dh).astype(BF16)
            bias_in = jnp.sum(dh.astype(F32), axis=0, keepdims=True)
            for s in range(c * chunk // ff, (c + 1) * chunk // ff):
                at = slice(s * ff - c * chunk, (s + 1) * ff - c * chunk)
                tail = jnp.where(wide_id == 0, bias_in[:, at], 0.0)
                for i in range(width // ff):
                    tail = jnp.where(wide_id == 1 + i, deo_bias[:, i * ff : (i + 1) * ff], tail)
                gin_s[slot, width : width + 16, at] = tail.astype(BF16)
            store(0, slot, c, rel)
        for micro in range(MICRO):
            turned_s[:, micro * part : (micro + 1) * part] = deo_s[micro, here, :].T
        for c in range(n_chunks):
            slot = next_slot()
            gin_s[slot, 0:width, :] = mm(turned_s[...], hid_s[rel, :, c * chunk : (c + 1) * chunk]).astype(BF16)
            store(1, slot, c, rel)
    for started in stores[-2:]:
        stored(started)
    for copy in crossing:
        copy.wait_recv()
    for sent in returns[0]:
        arrive_remote(sent)
    for sent in returns[1]:
        arrive(sent)
        leave(sent)
    for started in coming:
        leave(started)


def run_second(dims, n_shard, own, weights, slots):
    n_img, seq, pad, group, n_pos, reps, cap, cap_pad, n_exp = dims
    win, wout = weights
    width = slots[0].shape[-1]
    ext, ff = win.shape[1:]
    total = n_shard * ff
    part = n_pos * cap_pad
    n_slots = reps * part
    chunk = max(ff, min(total, 1024 if n_slots <= 1280 else 256))
    block_rows = part if n_slots <= 1280 else n_pos // 4 * cap_pad
    tail_wide = round_up(cap_pad, 128)
    n_pieces = reps * n_shard
    return pl.pallas_call(
        functools.partial(second_kernel, dims, n_shard, chunk),
        out_shape=(
            jax.ShapeDtypeStruct((n_slots, width), BF16),
            jax.ShapeDtypeStruct((n_slots, width), BF16),
            jax.ShapeDtypeStruct((MICRO, n_slots, width), BF16),
            jax.ShapeDtypeStruct((MICRO, n_exp * 16, tail_wide), BF16),
            jax.ShapeDtypeStruct((n_pieces // 2, ext, ff), BF16),
            jax.ShapeDtypeStruct((n_pieces // 2, width, ff), BF16),
            jax.ShapeDtypeStruct((n_pieces // 2, ext, ff), BF16),
            jax.ShapeDtypeStruct((n_pieces // 2, width, ff), BF16),
        ),
        in_specs=[ANY_SPEC] * 4 + [VMEM_SPEC] * 3 + [ANY_SPEC] * 3,
        out_specs=(ANY_SPEC,) * 8,
        scratch_shapes=[
            pltpu.VMEM((n_slots, width), BF16),
            pltpu.VMEM((n_pos * 16, tail_wide), BF16),
            pltpu.VMEM((n_slots, width), BF16),
            pltpu.VMEM((reps, ext, total), BF16),
            pltpu.VMEM((reps, total, width), BF16),
            pltpu.VMEM((reps, MICRO * part, total), BF16),
            pltpu.VMEM((reps, MICRO * part, total), BF16),
            pltpu.VMEM((MICRO, n_slots, width), BF16),
            pltpu.VMEM((block_rows, chunk), F32),
            pltpu.VMEM((block_rows, chunk), F32),
            pltpu.VMEM((block_rows, width), F32),
            pltpu.VMEM((block_rows, width), F32),
            pltpu.VMEM((n_slots, width), BF16),
            pltpu.VMEM((n_slots, width), BF16),
            pltpu.VMEM((MICRO, n_exp * 16, tail_wide), BF16),
            pltpu.VMEM((width, MICRO * part), BF16),
            pltpu.VMEM((2, ext, chunk), BF16),
            pltpu.SemaphoreType.DMA((2, n_pieces)),
            pltpu.SemaphoreType.DMA((3, n_exp)),
            pltpu.SemaphoreType.DMA((3, n_exp)),
            pltpu.SemaphoreType.DMA((MICRO, 3, n_exp)),
            pltpu.SemaphoreType.DMA((MICRO, 3, n_exp)),
            pltpu.SemaphoreType.DMA((2, n_pieces // 2)),
            pltpu.SemaphoreType.DMA((2, n_pieces // 2)),
            pltpu.SemaphoreType.DMA((2, n_pieces // 2)),
        ],
        compiler_params=pltpu.CompilerParams(
            collective_id=1, has_side_effects=True, vmem_limit_bytes=62 * 1024 * 1024
        ),
        cost_estimate=cost(32e9, 60e6, 10e6),
    )(*own, win, wout, *slots)


def combine_group(dims, micro, table, gates, mid, eo, out_ref):
    n_img, seq, pad, group, n_pos, reps, cap, cap_pad, n_exp = dims
    rows = group * pad
    n_slots = reps * n_pos * cap_pad
    ids = lanes(rows, 128).astype(F32)
    along = lanes(rows, n_slots).astype(F32)
    result = mid
    for lane in range(2):
        gate = jnp.sum(jnp.where(ids == table[:, lane : lane + 1], gates, 0.0), axis=1, keepdims=True)
        chosen = (along == table[:, 2 + lane : 3 + lane]).astype(F32).astype(BF16)
        result = result + gate * mm(chosen, eo)
    for n in range(group):
        out_ref[micro * group + n] = result[n * pad : n * pad + seq, :].astype(BF16)


def backward_group(dims, micro, order, hook, refs):
    n_img, seq, pad, group, n_pos, reps, cap, cap_pad, n_exp = dims
    (tok_ref, cot_ref, full_ref, table, state, db, dt, gtok_ref, grad_ref, c_s, x_s, vec_s, dqkv_s, do_s, dg_s) = refs
    a1_ref, qkv_ref, mix_ref, mid_ref, a2_ref, gate_ref, lse_ref = state
    rows = group * pad
    n_slots = reps * n_pos * cap_pad
    width = tok_ref.shape[-1]
    head = width // HEADS
    per_pair = 128 // head
    c = load_group(cot_ref, order, micro, group, seq, pad, c_s)
    small = full_ref[:, 4 * width :]
    turned = small.astype(F32).T
    gain1 = turned[n_exp : n_exp + 1, :]
    gain2 = turned[n_exp + 2 : n_exp + 3, :]
    if micro == 0:
        vec_s[...] = jnp.zeros(vec_s.shape, F32)

    def add_vec(at, value):
        vec_s[n_exp + at : n_exp + at + 1, :] += value

    along = lanes(rows, n_slots).astype(F32)
    chosen = ((along == table[:, 2:3]) | (along == table[:, 3:4])).astype(F32).astype(BF16)
    tails = dt[...].astype(F32)
    spare = round_up(tails.shape[0], 128) - tails.shape[0]
    if spare:
        tails = jnp.concatenate([tails, jnp.zeros((spare, tails.shape[1]), F32)], axis=0)
    tails = tails.T
    lane_slot = lanes(cap_pad, 128)
    me = lax.axis_index("expert")
    for block in range(reps * n_pos):
        at = slice(block * cap_pad, (block + 1) * cap_pad)
        lane = block * 16
        column = tails[0:cap_pad, lane : lane + 1] + tails[0:cap_pad, lane + 1 : lane + 2]
        expert = flip_all(me, block)
        dg_s[at, :] = jnp.where(lane_slot == expert, column, 0.0)
    dg = dg_s[...]
    dg_high = dg.astype(BF16)
    dg_low = (dg - dg_high.astype(F32)).astype(BF16)
    dgates = mm(chosen, dg_high) + mm(chosen, dg_low)
    routed = mm(chosen, db[...])
    gates = gate_ref[...]
    dlogits = (gates * (dgates - jnp.sum(gates * dgates, axis=1, keepdims=True))).astype(BF16)
    grad_small = mm_tn(a2_ref[...], dlogits)
    da2 = mm_nt(dlogits, small) + routed

    def norm_back(values, upstream, gain, at):
        normed, rate = norm_parts(values)
        add_vec(at, jnp.sum(upstream * normed, axis=0, keepdims=True))
        add_vec(at + 1, jnp.sum(upstream, axis=0, keepdims=True))
        scaled = upstream * gain
        return rate * (
            scaled
            - jnp.mean(scaled, axis=-1, keepdims=True)
            - normed * jnp.mean(scaled * normed, axis=-1, keepdims=True)
        )

    def add_grad(low, high, value):
        if micro == 0:
            grad_ref[:, low:high] = value
        else:
            grad_ref[:, low:high] += value

    dmid = c + norm_back(mid_ref[...], da2, gain2, 2)
    c_s[...] = dmid
    dbranch = dmid.astype(BF16)
    add_vec(6, jnp.sum(dbranch.astype(F32), axis=0, keepdims=True))
    add_grad(3 * width, 4 * width, mm_tn(mix_ref[...], dbranch))
    do_s[...] = mm_nt(dbranch, full_ref[:, 3 * width : 4 * width]).astype(BF16)
    hook()

    key_ok = lanes(pad, pad) < seq
    lane = lanes(pad, 128)
    scale = head ** (-0.5)
    for n in range(group):
        at = slice(n * pad, (n + 1) * pad)
        lse = lse_ref[at, :]
        for pair in range(width // 128):
            cols = pair * 128
            q2 = qkv_ref[at, cols : cols + 128]
            k2 = qkv_ref[at, width + cols : width + cols + 128]
            v2 = qkv_ref[at, 2 * width + cols : 2 * width + cols + 128]
            do2 = do_s[at, cols : cols + 128]
            dq2 = dk2 = dv2 = None
            for sub in range(per_pair):
                index = pair * per_pair + sub
                mine = (lane >= sub * head) & (lane < (sub + 1) * head)
                zero = jnp.zeros_like(q2)
                qh = jnp.where(mine, q2, zero)
                kh = jnp.where(mine, k2, zero)
                doh = jnp.where(mine, do2, zero)
                scores = jnp.where(key_ok, mm_nt(qh, k2), -jnp.inf)
                probs = jnp.exp(scores - lse[:, index : index + 1])
                dprobs = mm_nt(doh, v2)
                dscores = (probs * (dprobs - jnp.sum(probs * dprobs, axis=-1, keepdims=True))).astype(BF16)
                dv = mm_tn(probs.astype(BF16), doh)
                dq = mm(dscores, kh)
                dk = mm_tn(dscores, qh)
                dq2 = dq if dq2 is None else dq2 + dq
                dk2 = dk if dk2 is None else dk2 + dk
                dv2 = dv if dv2 is None else dv2 + dv
            dqkv_s[at, cols : cols + 128] = (dq2 * scale).astype(BF16)
            dqkv_s[at, width + cols : width + cols + 128] = dk2.astype(BF16)
            dqkv_s[at, 2 * width + cols : 2 * width + cols + 128] = dv2.astype(BF16)
            hook()
    dqkv = dqkv_s[...]
    add_grad(0, 3 * width, mm_tn(a1_ref[...], dqkv))
    add_vec(4, jnp.sum(dqkv[:, 0:width].astype(F32), axis=0, keepdims=True))
    add_vec(5, jnp.sum(dqkv[:, 2 * width :].astype(F32), axis=0, keepdims=True))
    da1 = mm_nt(dqkv, full_ref[:, 0 : 3 * width])
    x = load_group(tok_ref, order, micro, group, seq, pad, x_s)
    dx = c_s[...] + norm_back(x, da1, gain1, 0)
    for n in range(group):
        gtok_ref[micro * group + n] = dx[n * pad : n * pad + seq, :]
    if micro == MICRO - 1:
        grad_small = grad_small + vec_s[...].T
    add_grad(4 * width, 4 * width + 128, grad_small)


def third_kernel(dims, n_shard, orders, cuts, separate, *refs):
    n_img, seq, pad, group, n_pos, reps, cap, cap_pad, n_exp = dims
    batch_ref, tok_ref, cot_ref, full_ref, col_ref = refs[:5]
    states = (refs[5:12], refs[12:19])
    eo_ref, db_ref, dt_ref, eo_next, gin_ref, gout_ref, gin_core, gout_core = refs[19:27]
    out_ref, gtok_ref, mine_ref, own_in_ref, own_out_ref = refs[27:32]
    (eo_late, out_s, gtok_s, acc_in, acc_out, land_in, land_out, c_s, x_s, vec_s, dqkv_s, do_s, dg_s, grad_s, sends, recvs,
     load_sems, esend, erecv, send_sems, recv_sems, rsend, rrecv) = refs[32:]
    top = n_pos * n_shard
    me = lax.axis_index("expert") * n_shard + lax.axis_index("shard")

    def place(index):
        return (index // n_shard, lax.rem(index, n_shard))

    greet(me, sorted(set(orders[0]) | {pos * n_shard for pos in range(1, n_pos)}), n_shard)
    returning = Messages(n_shard, me, n_pos, reps, cap_pad).rows(eo_next, eo_late, rsend, rrecv)
    order = image_order(batch_ref, n_img)

    levels = n_shard.bit_length() - 1
    bases = [0]
    for level in range(levels):
        bases.append(bases[-1] + (n_shard >> (level + 1)) * reps)
    pieces = ((gin_ref, acc_in, land_in), (gout_ref, acc_out, land_out))
    arriving = {}
    sending = []

    def ship(kind, source, slot, bit):
        copy = pltpu.make_async_remote_copy(
            src_ref=source,
            dst_ref=pieces[kind][2].at[slot],
            send_sem=esend.at[kind, slot],
            recv_sem=erecv.at[kind, slot],
            device_id=place(flip(me, bit)),
            device_id_type=MESH,
        )
        copy.start()
        arriving[kind, slot] = copy
        sending.append(copy)

    loads = {}
    for rel in range(reps)[::-1]:
        for kind in range(2):
            _, acc, land = pieces[kind]
            for j in range(n_shard // 2):
                at = j * reps + rel
                copies = (
                    pltpu.make_async_copy((gin_ref, gout_ref)[kind].at[at], acc.at[at], load_sems.at[kind, 0, at]),
                    pltpu.make_async_copy((gin_core, gout_core)[kind].at[at], land.at[at], load_sems.at[kind, 1, at]),
                )
                for copy in copies:
                    copy.start()
                loads[kind, at] = copies

    def stage(level, rel, kind):
        _, acc, land = pieces[kind]
        for j in list(range(n_shard >> (level + 1)))[::-1]:
            at = (j << level) * reps + rel
            slot = bases[level] + j * reps + rel
            if level == 0:
                for copy in loads[kind, at]:
                    copy.wait()
            else:
                arriving[kind, slot].wait_recv()
            acc[at] = (acc[at].astype(F32) + land[slot].astype(F32)).astype(BF16)
            if level + 1 < levels:
                if j % 2:
                    ship(kind, acc.at[at], bases[level + 1] + j // 2 * reps + rel, 2 << level)
            elif rel:
                ship(kind, acc.at[at], bases[levels], top)

    def last():
        total = []
        for kind in range(2):
            _, acc, land = pieces[kind]
            value = acc[0].astype(F32)
            if reps > 1:
                arriving[kind, bases[levels]].wait_recv()
                value = value + land[bases[levels]].astype(F32)
            total.append(value)
        own_in_ref[...] = total[0]
        own_out_ref[...] = total[1].T

    stages = [
        functools.partial(stage, level, rel, kind)
        for rel in range(reps)[::-1]
        for level in range(levels)
        for kind in range(2)
    ]
    calls = []

    def hook():
        calls.append(0)
        for _ in range(STAGES_AT.get(len(calls), 0)):
            if stages:
                stages.pop(0)()

    hook()
    for micro in range(MICRO):
        backward_group(
            dims, micro, order, hook,
            (tok_ref, cot_ref, full_ref, col_ref[micro], states[micro], db_ref.at[micro], dt_ref.at[micro],
             gtok_s, grad_s, c_s, x_s, vec_s, dqkv_s, do_s, dg_s),
        )

    def combine(micro):
        if micro == MICRO - 1:
            arrive(returning)
        eo = (eo_ref, eo_late)[micro][...]
        combine_group(dims, micro, col_ref[micro], states[micro][5][...], states[micro][3][...], eo, out_s)

    if separate:
        for micro in range(MICRO):
            combine(micro)
        mine_ref[...] = grad_s[...]
    else:
        n_dev, chunk_rows = sends.shape[:2]
        copies = []

        def rows_of(chunk):
            return pl.ds(pl.multiple_of(chunk * chunk_rows, chunk_rows), chunk_rows)

        for step in range(len(orders[0])):
            started = []
            base = n_dev - (n_dev >> step)
            count = n_dev >> (step + 1)
            for part, bits in enumerate(orders):
                peer = flip(me, bits[step])
                low, high = cuts[part]
                for at, combo in enumerate(combos(bits[step + 1 :])):
                    sends[base + at, :, low:high] = grad_s[rows_of(flip_all(peer, combo)), low:high].astype(BF16)
                copy = pltpu.make_async_remote_copy(
                    src_ref=sends.at[base : base + count, :, low:high],
                    dst_ref=recvs.at[base : base + count, :, low:high],
                    send_sem=send_sems.at[part, step],
                    recv_sem=recv_sems.at[part, step],
                    device_id=place(peer),
                    device_id_type=MESH,
                )
                copy.start()
                started.append(copy)
            if step < MICRO:
                combine(step)
            for part, bits in enumerate(orders):
                low, high = cuts[part]
                started[part].wait_recv()
                for at, combo in enumerate(combos(bits[step + 1 :])):
                    grad_s[rows_of(flip_all(me, combo)), low:high] += recvs[base + at, :, low:high].astype(F32)
            copies.extend(started)
        mine_ref[...] = grad_s[rows_of(me), :]
        for copy in copies:
            copy.wait_send()
    for image, rank in enumerate(image_ranks(batch_ref, n_img)):
        out_ref[image] = out_s[rank]
        gtok_ref[image] = gtok_s[rank]
    while stages:
        stages.pop(0)()
    last()
    leave(returning)
    for copy in sending:
        copy.wait_send()


def run_third(dims, n_shard, batch, tokens, cotangent, full, cols, states, returned, grads, chunk_rows):
    n_img, seq, pad, group, n_pos, reps, cap, cap_pad, n_exp = dims
    width = tokens.shape[-1]
    rows = group * pad
    n_slots = reps * n_pos * cap_pad
    n_dev = n_exp * n_shard
    total = full.shape[1]
    ext, ff = grads[0].shape[1:]
    orders = [bits[::-1] for bits in bit_orders(n_exp, n_shard)]
    middle = total // 256 * 128
    cuts = ((0, middle), (middle, total))
    separate = chunk_rows % 16 != 0
    land = (n_shard - 1) * reps + 1
    mine = (width, total) if separate else (chunk_rows, total)
    buffer = (1, 16, 128) if separate else (n_dev, chunk_rows, total)
    return pl.pallas_call(
        functools.partial(third_kernel, dims, n_shard, orders, cuts, separate),
        out_shape=(
            jax.ShapeDtypeStruct((n_img, seq, width), BF16),
            jax.ShapeDtypeStruct((n_img, seq, width), F32),
            jax.ShapeDtypeStruct(mine, F32),
            jax.ShapeDtypeStruct((ext, ff), F32),
            jax.ShapeDtypeStruct((ff, width), F32),
        ),
        in_specs=[SMEM_SPEC] + [VMEM_SPEC] * 21 + [ANY_SPEC] * 5,
        out_specs=(VMEM_SPEC,) * 5,
        scratch_shapes=[
            pltpu.VMEM((n_slots, width), BF16),
            pltpu.VMEM((n_img, seq, width), BF16),
            pltpu.VMEM((n_img, seq, width), F32),
            pltpu.VMEM((n_shard // 2 * reps, ext, ff), BF16),
            pltpu.VMEM((n_shard // 2 * reps, width, ff), BF16),
            pltpu.VMEM((land, ext, ff), BF16),
            pltpu.VMEM((land, width, ff), BF16),
            pltpu.VMEM((rows, width), F32),
            pltpu.VMEM((rows, width), F32),
            pltpu.VMEM((128, width), F32),
            pltpu.VMEM((rows, 3 * width), BF16),
            pltpu.VMEM((rows, width), BF16),
            pltpu.VMEM((n_slots, 128), F32),
            pltpu.VMEM((width, total), F32),
            pltpu.VMEM(buffer, BF16),
            pltpu.VMEM(buffer, BF16),
            pltpu.SemaphoreType.DMA((2, 2, n_shard // 2 * reps)),
            pltpu.SemaphoreType.DMA((2, land)),
            pltpu.SemaphoreType.DMA((2, land)),
            pltpu.SemaphoreType.DMA((2, len(orders[0]))),
            pltpu.SemaphoreType.DMA((2, len(orders[0]))),
            pltpu.SemaphoreType.DMA((n_exp,)),
            pltpu.SemaphoreType.DMA((n_exp,)),
        ],
        compiler_params=pltpu.CompilerParams(
            collective_id=2, has_side_effects=True, vmem_limit_bytes=62 * 1024 * 1024
        ),
        cost_estimate=cost(20e9, 60e6, 4e6),
    )(batch, tokens, cotangent, full, cols, *states[0], *states[1], *returned, *grads)


def on_device(
    tokens, cotangent, routes, batch_of_image, w_qkv, w_attn_out, w_router, norm1_gain, norm1_bias, norm2_gain,
    norm2_bias, bias_query, bias_value, bias_attn_out, w_expert_in, w_expert_out, bias_expert_in, bias_expert_out,
):
    n_img, seq, width = tokens.shape
    n_expert = lax.axis_size("expert")
    n_shard = lax.axis_size("shard")
    n_dev = n_expert * n_shard
    group = n_img // MICRO
    pad = round_up(seq, 16)
    rows = group * pad
    cap = 16 * group * seq // (5 * n_expert)
    cap_pad = round_up(cap, 16)
    reps = 2 if n_expert > 1 else 1
    n_pos = n_expert // reps
    ff = w_expert_in.shape[2]
    dims = (n_img, seq, pad, group, n_pos, reps, cap, cap_pad, n_expert)
    my_shard = lax.axis_index("shard")

    vectors = jnp.concatenate(
        [norm1_gain, norm1_bias, norm2_gain, norm2_bias, bias_query, bias_value, bias_attn_out]
    ).reshape(7, -1).T
    blank = jnp.zeros((vectors.shape[0], 128 - n_expert - 7), BF16)
    packed = jnp.concatenate([w_qkv, w_attn_out, w_router, vectors, blank], axis=1)

    quarter = width // n_shard
    out_bias = jnp.where(jnp.arange(width) // quarter == my_shard, jnp.tile(bias_expert_out[0], n_shard), 0)
    tail = jnp.concatenate(
        [bias_expert_in, out_bias.astype(BF16).reshape(-1, ff), jnp.zeros((15 - width // ff, ff), BF16)], axis=0
    )
    own_in = jnp.concatenate([w_expert_in[0], tail], axis=0)

    cols, full, weights, slots, *states = run_first(
        dims, n_shard, batch_of_image, routes, tokens, cotangent, packed, own_in, w_expert_out[0]
    )
    eo, eo_next, db, dt, *grads = run_second(dims, n_shard, (own_in, w_expert_out[0]), weights, slots)
    layer_out, gtok, mine, own_grad_in, own_grad_out = run_third(
        dims, n_shard, batch_of_image, tokens, cotangent, full, cols, states, (eo, db, dt, eo_next), grads,
        packed.shape[0],
    )
    if mine.shape[0] != packed.shape[0]:
        mine = scatter_params(mine, n_expert, n_shard, 4)
    tail = own_grad_in[width:, :]
    out_bias_grad = tail[1 : 1 + width // ff, :].reshape(width)
    small = mine[:, 4 * width :]
    vec = [small[:, n_expert + i] for i in range(7)]
    return (
        layer_out,
        gtok,
        mine[:, 0 : 3 * width],
        mine[:, 3 * width : 4 * width],
        small[:, 0:n_expert],
        *vec,
        own_grad_in[0:width, :][None],
        own_grad_out[None],
        tail[0:1, :],
        lax.dynamic_slice(out_bias_grad, (my_shard * (width // n_shard),), (width // n_shard,))[None],
    )


def solution(mesh):
    both = ("expert", "shard")
    placed = (
        (P(both, None, None),) * 3
        + (P(both),)
        + (P(both, None),) * 3
        + (P(both),) * 7
        + (P("expert", None, "shard"), P("expert", "shard", None), P("expert", "shard"), P("expert", "shard"))
    )
    return jax.shard_map(
        on_device,
        mesh=mesh,
        in_specs=placed,
        out_specs=(P(both, None, None),) * 2
        + (P(both, None),) * 3
        + (P(both),) * 7
        + (P("expert", None, "shard"), P("expert", "shard", None), P("expert", "shard"), P("expert", "shard")),
        check_vma=False,
    )
```

```python
import functools
import math

import jax
import jax.numpy as jnp
from jax import lax
from jax.experimental import pallas as pl
from jax.experimental.pallas import tpu as pltpu
from jax.sharding import PartitionSpec as P

HEADS = 8
MICRO = 2
EPS = 1e-06
F32 = jnp.float32
BF16 = jnp.bfloat16
MESH = pl.DeviceIdType.MESH
OWN_FIRST = (0, 1, 2, 3)
STAGES_AT = {1: 1, 3: 1, 10: 1, 12: 1, 14: 2}
VMEM_LIMIT = 56 * 1024 * 1024
VMEM_SPEC = pl.BlockSpec(memory_space=pltpu.VMEM)
SMEM_SPEC = pl.BlockSpec(memory_space=pltpu.SMEM)
ANY_SPEC = pl.BlockSpec(memory_space=pl.ANY)


def round_up(value, unit):
    return (value + unit - 1) // unit * unit


def mm(left, right):
    return lax.dot_general(left, right, (((1,), (0,)), ((), ())), preferred_element_type=F32)


def mm_nt(left, right):
    return lax.dot_general(left, right, (((1,), (1,)), ((), ())), preferred_element_type=F32)


def mm_tn(left, right):
    return lax.dot_general(left, right, (((0,), (0,)), ((), ())), preferred_element_type=F32)


def cost(flops, nbytes, trans=0):
    return pl.CostEstimate(flops=int(flops), bytes_accessed=int(nbytes), transcendentals=int(trans))


def plain(name_cost):
    return dict(
        cost_estimate=name_cost,
        compiler_params=pltpu.CompilerParams(vmem_limit_bytes=VMEM_LIMIT),
    )


def image_ranks(batch_ref, n_img):
    keys = [batch_ref[i] * n_img + i for i in range(n_img)]
    ranks = []
    for i in range(n_img):
        rank = jnp.int32(0)
        for j in range(n_img):
            if j != i:
                rank = rank + jnp.where(keys[j] < keys[i], 1, 0)
        ranks.append(rank)
    return ranks


def image_order(batch_ref, n_img):
    ranks = image_ranks(batch_ref, n_img)
    order = []
    for k in range(n_img):
        place = jnp.int32(0)
        for i in range(n_img):
            place = place + jnp.where(ranks[i] == k, i, 0)
        order.append(place)
    return order


def flip(index, bit):
    return index + bit - 2 * bit * lax.rem(index // bit, 2)


def lanes(rows, width):
    return lax.broadcasted_iota(jnp.int32, (rows, width), 1)


def bit_orders(n_expert, n_shard):
    shard_bits = [1 << i for i in range(n_shard.bit_length() - 1)]
    expert_bits = [n_shard << i for i in range(n_expert.bit_length() - 1)]
    core = shard_bits[:1]
    across = shard_bits[1:]
    first = expert_bits[::-1] + across[::-1] + core
    second = expert_bits[:0:-1] + across[::-1] + expert_bits[:1] + core
    return first, second


def combos(bits):
    result = [0]
    for bit in bits:
        result = result + [held + bit for held in result]
    return result


def flip_all(index, combo):
    bit = 1
    while bit <= combo:
        if combo & bit:
            index = flip(index, bit)
        bit *= 2
    return index


def greet(me, bits, n_shard):
    barrier = pltpu.get_barrier_semaphore()
    for bit in bits:
        peer = flip_all(me, bit)
        pl.semaphore_signal(
            barrier, inc=1, device_id=(peer // n_shard, lax.rem(peer, n_shard)), device_id_type=MESH
        )
    pl.semaphore_wait(barrier, len(bits))


def gather_kernel(n_shard, orders, cuts, mine_ref, full_ref, local_sem, send_sems, recv_sems):
    me = lax.axis_index("expert") * n_shard + lax.axis_index("shard")
    greet(me, orders[0], n_shard)
    own = pltpu.make_async_copy(mine_ref, full_ref.at[me], local_sem)
    own.start()
    copies = []
    for step in range(len(orders[0])):
        started = []
        for part, order in enumerate(orders):
            bit = order[step]
            peer = flip(me, bit)
            low, high = cuts[part]
            for at, combo in enumerate(combos(order[:step])):
                chunk = flip_all(me, combo)
                source = mine_ref if combo == 0 else full_ref.at[chunk]
                copy = pltpu.make_async_remote_copy(
                    src_ref=source.at[:, low:high],
                    dst_ref=full_ref.at[chunk, :, low:high],
                    send_sem=send_sems.at[part, (1 << step) - 1 + at],
                    recv_sem=recv_sems.at[part, (1 << step) - 1 + at],
                    device_id=(peer // n_shard, lax.rem(peer, n_shard)),
                    device_id_type=MESH,
                )
                copy.start()
                started.append(copy)
        for copy in started:
            copy.wait_recv()
        copies.extend(started)
    for copy in copies:
        copy.wait_send()
    own.wait()


def gather_params(packed, n_expert, n_shard, collective_id):
    rows, width = packed.shape
    n_dev = n_expert * n_shard
    orders = bit_orders(n_expert, n_shard)
    middle = width // 256 * 128
    cuts = ((0, middle), (middle, width))
    full = pl.pallas_call(
        functools.partial(gather_kernel, n_shard, orders, cuts),
        out_shape=jax.ShapeDtypeStruct((n_dev, rows, width), packed.dtype),
        in_specs=[VMEM_SPEC],
        out_specs=VMEM_SPEC,
        scratch_shapes=[
            pltpu.SemaphoreType.DMA,
            pltpu.SemaphoreType.DMA((2, n_dev - 1)),
            pltpu.SemaphoreType.DMA((2, n_dev - 1)),
        ],
        compiler_params=pltpu.CompilerParams(
            collective_id=collective_id, has_side_effects=True, vmem_limit_bytes=VMEM_LIMIT
        ),
        cost_estimate=cost(1e6, 4 * n_dev * rows * width),
    )(packed)
    return full.reshape(n_dev * rows, width)


def scatter_kernel(n_shard, orders, cuts, full_ref, out_ref, acc, sends, recvs, send_sems, recv_sems):
    me = lax.axis_index("expert") * n_shard + lax.axis_index("shard")
    n_dev = full_ref.shape[0]
    greet(me, orders[0], n_shard)
    n_steps = len(orders[0])
    acc[...] = full_ref[...]
    copies = []
    for step in range(n_steps):
        started = []
        base = n_dev - (n_dev >> step)
        count = n_dev >> (step + 1)
        for part, order in enumerate(orders):
            bit = order[step]
            peer = flip(me, bit)
            low, high = cuts[part]
            for at, combo in enumerate(combos(order[step + 1 :])):
                chunk = flip_all(peer, combo)
                sends[base + at, :, low:high] = acc[chunk, :, low:high].astype(BF16)
            copy = pltpu.make_async_remote_copy(
                src_ref=sends.at[base : base + count, :, low:high],
                dst_ref=recvs.at[base : base + count, :, low:high],
                send_sem=send_sems.at[part, step],
                recv_sem=recv_sems.at[part, step],
                device_id=(peer // n_shard, lax.rem(peer, n_shard)),
                device_id_type=MESH,
            )
            copy.start()
            started.append(copy)
        for part, order in enumerate(orders):
            low, high = cuts[part]
            started[part].wait_recv()
            for at, combo in enumerate(combos(order[step + 1 :])):
                chunk = flip_all(me, combo)
                acc[chunk, :, low:high] += recvs[base + at, :, low:high].astype(F32)
        copies.extend(started)
    out_ref[...] = acc[me]
    for copy in copies:
        copy.wait_send()


def scatter_params(full, n_expert, n_shard, collective_id):
    n_dev = n_expert * n_shard
    width = full.shape[1]
    rows = full.shape[0] // n_dev
    gather_orders = bit_orders(n_expert, n_shard)
    orders = [order[::-1] for order in gather_orders]
    middle = width // 256 * 128
    cuts = ((0, middle), (middle, width))
    return pl.pallas_call(
        functools.partial(scatter_kernel, n_shard, orders, cuts),
        out_shape=jax.ShapeDtypeStruct((rows, width), F32),
        in_specs=[VMEM_SPEC],
        out_specs=VMEM_SPEC,
        scratch_shapes=[
            pltpu.VMEM((n_dev, rows, width), F32),
            pltpu.VMEM((n_dev, rows, width), BF16),
            pltpu.VMEM((n_dev, rows, width), BF16),
            pltpu.SemaphoreType.DMA((2, len(orders[0]))),
            pltpu.SemaphoreType.DMA((2, len(orders[0]))),
        ],
        compiler_params=pltpu.CompilerParams(
            collective_id=collective_id, has_side_effects=True, vmem_limit_bytes=VMEM_LIMIT
        ),
        cost_estimate=cost(1e6, 8 * n_dev * rows * width),
    )(full.reshape(n_dev, rows, width))


def route_tables(dims, rt_s):
    n_img, seq, pad, group, n_pos, reps, cap, cap_pad, n_exp = dims
    rows = group * pad
    lower = (
        lax.broadcasted_iota(jnp.int32, (rows, rows), 0)
        > lax.broadcasted_iota(jnp.int32, (rows, rows), 1)
    ).astype(F32).astype(BF16)
    ids = lanes(rows, 128)
    me = lax.axis_index("expert")
    first = rt_s[:, 0:1]
    second = rt_s[:, 1:2]
    hot_first = (ids == first).astype(F32)
    hot_second = (ids == second).astype(F32)
    earlier_first = mm(lower, hot_first.astype(BF16))
    earlier_second = mm(lower, hot_second.astype(BF16)) + jnp.sum(hot_first, axis=0, keepdims=True)
    table = jnp.where(ids == 0, first.astype(F32), jnp.where(ids == 1, second.astype(F32), 0.0))
    for lane, route, hot, earlier in (
        (2, first, hot_first, earlier_first),
        (3, second, hot_second, earlier_second),
    ):
        slot = jnp.sum(hot * earlier, axis=1, keepdims=True)
        away = jnp.bitwise_xor(jnp.maximum(route, 0), jnp.broadcast_to(me, route.shape)).astype(F32)
        target = away * float(cap_pad) + slot
        target = jnp.where((slot < float(cap)) & (route >= 0), target, -1.0)
        table = jnp.where(ids == lane, target, table)
    spare = round_up(rows, 128) - rows
    turned = jnp.concatenate([table, jnp.full((spare, 128), -1.0, F32)], axis=0).T
    return table, turned[2:3, 0:rows], turned[3:4, 0:rows]


def norm_parts(values):
    center = values - jnp.mean(values, axis=-1, keepdims=True)
    rate = lax.rsqrt(jnp.mean(center * center, axis=-1, keepdims=True) + EPS)
    return center * rate, rate


def load_group(ref, order, micro, group, seq, pad, buf):
    buf[...] = jnp.zeros(buf.shape, F32)
    for n in range(group):
        buf[n * pad : n * pad + seq, :] = ref[order[micro * group + n]].astype(F32)
    return buf[...]


def attention_forward(dims, x, full_ref, out):
    n_img, seq, pad, group, n_pos, reps, cap, cap_pad, n_exp = dims
    a1_ref, qkv_ref, mix_ref, mid_ref, a2_ref, gate_ref, lse_ref = out
    rows = group * pad
    width = x.shape[-1]
    head = width // HEADS
    per_pair = 128 // head
    small = full_ref[:, 4 * width :]
    turned = small.astype(F32).T
    gain1, shift1, gain2, shift2, bias_q, bias_v, bias_o = [
        turned[n_exp + i : n_exp + i + 1, :] for i in range(7)
    ]
    normed, _ = norm_parts(x)
    a1 = (normed * gain1 + shift1).astype(BF16)
    a1_ref[...] = a1
    proj = mm(a1, full_ref[:, 0 : 3 * width])
    scale = head ** (-0.5)
    qkv_ref[:, 0:width] = ((proj[:, 0:width] + bias_q).astype(BF16).astype(F32) * scale).astype(BF16)
    qkv_ref[:, width : 2 * width] = proj[:, width : 2 * width].astype(BF16)
    qkv_ref[:, 2 * width :] = (proj[:, 2 * width :] + bias_v).astype(BF16)
    key_ok = lanes(pad, pad) < seq
    lane = lanes(pad, 128)
    for n in range(group):
        at = slice(n * pad, (n + 1) * pad)
        lse = jnp.zeros((pad, 128), F32)
        for pair in range(width // 128):
            cols = pair * 128
            q2 = qkv_ref[at, cols : cols + 128]
            k2 = qkv_ref[at, width + cols : width + cols + 128]
            v2 = qkv_ref[at, 2 * width + cols : 2 * width + cols + 128]
            mixed = None
            for sub in range(per_pair):
                mine = (lane >= sub * head) & (lane < (sub + 1) * head)
                scores = mm_nt(jnp.where(mine, q2, jnp.zeros_like(q2)), k2)
                scores = jnp.where(key_ok, scores, -jnp.inf)
                top = jnp.max(scores, axis=-1, keepdims=True)
                grown = jnp.exp(scores - top)
                total = jnp.sum(grown, axis=-1, keepdims=True)
                probs = (grown / total).astype(BF16)
                part = mm(probs, jnp.where(mine, v2, jnp.zeros_like(v2)))
                mixed = part if mixed is None else mixed + part
                lse = jnp.where(lane == pair * per_pair + sub, top + jnp.log(total), lse)
            mix_ref[at, cols : cols + 128] = mixed.astype(BF16)
        lse_ref[at, :] = lse
    mid = x + mm(mix_ref[...], full_ref[:, 3 * width : 4 * width]) + bias_o
    mid_ref[...] = mid
    normed2, _ = norm_parts(mid)
    a2 = (normed2 * gain2 + shift2).astype(BF16)
    a2_ref[...] = a2
    ids = lanes(rows, 128)
    logits = jnp.where(ids < n_exp, mm(a2, small), -jnp.inf)
    grown = jnp.exp(logits - jnp.max(logits, axis=-1, keepdims=True))
    gates = grown / jnp.sum(grown, axis=-1, keepdims=True)
    gate_ref[...] = gates


def fill_message(dims, table, gates, a2, chosen, send_ref, tail_ref):
    n_img, seq, pad, group, n_pos, reps, cap, cap_pad, n_exp = dims
    rows = group * pad
    part = n_pos * cap_pad
    ids = lanes(rows, 128).astype(F32)
    gate1 = jnp.sum(jnp.where(ids == table[:, 0:1], gates, 0.0), axis=1, keepdims=True)
    gate2 = jnp.sum(jnp.where(ids == table[:, 1:2], gates, 0.0), axis=1, keepdims=True)
    to1, to2 = table[:, 2:3], table[:, 3:4]
    send_ref[...] = mm(chosen, a2).astype(BF16)
    tail_ref[...] = jnp.zeros(tail_ref.shape, BF16)
    along = lanes(rows, part)
    tail_id = lax.broadcasted_iota(jnp.int32, (16, cap_pad), 0)
    tails = [jnp.zeros((16, cap_pad), F32) for _ in range(n_pos)]
    for rel in range(reps):
        there = (along + rel * part).astype(F32)
        gate_row = jnp.sum(
            jnp.where(there == to1, gate1, 0.0) + jnp.where(there == to2, gate2, 0.0), axis=0, keepdims=True
        )
        high = gate_row.astype(BF16).astype(F32)
        low = gate_row - high
        for pos in range(n_pos):
            at = slice(pos * cap_pad, (pos + 1) * cap_pad)
            tails[pos] = jnp.where(
                tail_id == 2 * rel, high[:, at], jnp.where(tail_id == 2 * rel + 1, low[:, at], tails[pos])
            )
    for pos in range(n_pos):
        tail_ref[pos * 16 : (pos + 1) * 16, 0:cap_pad] = tails[pos].astype(BF16)


class Messages:
    def __init__(self, n_shard, me, n_pos, reps, cap_pad):
        self.n_shard, self.me, self.n_pos, self.reps, self.cap_pad = n_shard, me, n_pos, reps, cap_pad
        self.pending = []

    def move(self, source, target, send_sem, recv_sem, pos):
        if pos == 0:
            copy = pltpu.make_async_copy(source, target, recv_sem)
            copy.start()
            self.pending.append((copy, False))
        else:
            peer = flip_all(self.me, pos * self.n_shard)
            copy = pltpu.make_async_remote_copy(
                src_ref=source,
                dst_ref=target,
                send_sem=send_sem,
                recv_sem=recv_sem,
                device_id=(peer // self.n_shard, lax.rem(peer, self.n_shard)),
                device_id_type=MESH,
            )
            copy.start()
            self.pending.append((copy, True))
        return copy, pos > 0

    def rows(self, source, target, send_sems, recv_sems, rels=None):
        started = []
        for rel in range(self.reps) if rels is None else rels:
            for pos in range(self.n_pos):
                block = rel * self.n_pos + pos
                at = pl.ds(block * self.cap_pad, self.cap_pad)
                started.append(
                    self.move(source.at[at], target.at[at], send_sems.at[block], recv_sems.at[block], pos)
                )
        return started

    def tails(self, source, target, send_sems, recv_sems, blocks):
        started = []
        for block in blocks:
            at = pl.ds(block * 16, 16)
            started.append(
                self.move(source.at[at], target.at[at], send_sems.at[block], recv_sems.at[block], block % self.n_pos)
            )
        return started


def arrive(started):
    for copy, remote in started:
        if remote:
            copy.wait_recv()
        else:
            copy.wait()


def arrive_remote(started):
    arrive([member for member in started if member[1]])


def leave(started):
    for copy, remote in started:
        if remote:
            copy.wait_send()


def first_kernel(dims, n_shard, orders, cuts, gathered, *refs):
    n_img, seq, pad, group, n_pos, reps, cap, cap_pad, n_exp = dims
    (batch_ref, routes_ref, tok_ref, cot_ref, packed_ref, own_in_ref, own_out_ref) = refs[:7]
    refs = refs[7:]
    col_ref, full_out, win_ref, wout_ref, buf_ref, tail_ref, cot_slots_ref = refs[:7]
    next_out, next_tail_out, next_cot_out = refs[7:10]
    state_outs = (refs[10:17], refs[17:24])
    refs = refs[24:]
    states = (refs[0:7], refs[7:14])
    (next_ref, next_tail_ref, next_cot_ref, full_s, x_s, rt_s, chosen_s, asend, tsend, csend, keep_sems, own_sem,
     gsend, grecv, wsend, wrecv, dsend, drecv) = refs[14:]
    full_ref = packed_ref if gathered else full_s
    kept_copies = []

    def keep(source, target):
        copy = pltpu.make_async_copy(source, target, keep_sems.at[len(kept_copies)])
        copy.start()
        kept_copies.append(copy)

    rows = group * pad
    n_slots = reps * n_pos * cap_pad
    top = n_pos * n_shard
    expert, shard = lax.axis_index("expert"), lax.axis_index("shard")
    me = expert * n_shard + shard

    def place(index):
        return (index // n_shard, lax.rem(index, n_shard))

    peers = sorted(set(orders[0]) | {pos * n_shard for pos in range(1, n_pos)})
    barrier = pltpu.get_barrier_semaphore()
    for peer in peers:
        pl.semaphore_signal(barrier, inc=1, device_id=place(flip_all(me, peer)), device_id_type=MESH)
    pl.semaphore_wait(barrier, len(peers))

    chunk_rows = full_ref.shape[0] // (n_exp * n_shard) if not gathered else 0
    gather_copies = []

    def at_chunk(ref, index, low, high):
        return ref.at[pl.ds(pl.multiple_of(index * chunk_rows, chunk_rows), chunk_rows), low:high]

    def gather_start(step):
        for part, order in enumerate(orders):
            low, high = cuts[part]
            for at, combo in enumerate(combos(order[:step])):
                chunk = flip_all(me, combo)
                source = packed_ref.at[:, low:high] if combo == 0 else at_chunk(full_ref, chunk, low, high)
                sem = (1 << step) - 1 + at
                copy = pltpu.make_async_remote_copy(
                    src_ref=source,
                    dst_ref=at_chunk(full_ref, chunk, low, high),
                    send_sem=gsend.at[part, sem],
                    recv_sem=grecv.at[part, sem],
                    device_id=place(flip(me, order[step])),
                    device_id_type=MESH,
                )
                copy.start()
                gather_copies.append(copy)

    def gather_next(step):
        if gathered:
            return
        count = 2 * (1 << step)
        for copy in gather_copies[-count:]:
            copy.wait_recv()
        if step + 1 < len(orders[0]):
            gather_start(step + 1)

    if not gathered:
        gather_start(0)
        own = pltpu.make_async_copy(packed_ref, at_chunk(full_ref, me, 0, full_ref.shape[1]), own_sem)
        own.start()

    bits = ([top] if reps > 1 else []) + [1 << i for i in range(n_shard.bit_length() - 1)][::-1]

    def number(held):
        return (held // top) * n_shard + held % top

    weight_copies = {}

    ext, ff = own_in_ref.shape
    spans = [(0, 0, ext // 32 * 16), (0, ext // 32 * 16, ext), (1, 0, ff // 32 * 16), (1, ff // 32 * 16, ff)]

    def weights_start(span, held, bit):
        kind, low, high = spans[span]
        at = pl.ds(low, high - low)
        source = ((own_in_ref, own_out_ref)[kind]) if held == 0 else (win_ref, wout_ref)[kind].at[number(held)]
        to = number(held + bit)
        copy = pltpu.make_async_remote_copy(
            src_ref=source.at[at],
            dst_ref=(win_ref, wout_ref)[kind].at[to, at],
            send_sem=wsend.at[span, to],
            recv_sem=wrecv.at[span, to],
            device_id=place(flip(me, bit)),
            device_id_type=MESH,
        )
        copy.start()
        weight_copies[span, held + bit] = copy

    def weights_pass(span, held):
        weight_copies[span, held].wait_recv()
        last = min(bit for bit in bits if held & bit)
        for bit in bits:
            if bit < last:
                weights_start(span, held, bit)

    inner_bits = [bit for bit in bits if bit < top]
    if reps > 1:
        weights_start(0, 0, top)
        weights_start(1, 0, top)
    for span in OWN_FIRST:
        for bit in inner_bits:
            weights_start(span, 0, bit)

    order = image_order(batch_ref, n_img)
    messages = Messages(n_shard, me, n_pos, reps, cap_pad)
    arrivals = []

    n_steps = len(orders[0])
    step = 0
    tables = []
    for micro in range(MICRO):
        rt_s[...] = jnp.full(rt_s.shape, -1, jnp.int32)
        for n in range(group):
            rt_s[n * pad : n * pad + seq, 0:2] = routes_ref[order[micro * group + n]]
        table, row_first, row_second = route_tables(dims, rt_s)
        col_ref[micro] = table
        if step < n_steps:
            gather_next(step)
            step += 1
        cot = load_group(cot_ref, order, micro, group, seq, pad, x_s).astype(BF16)
        here = lax.broadcasted_iota(jnp.int32, (n_slots, rows), 0).astype(F32)
        chosen = ((here == row_first) | (here == row_second)).astype(F32).astype(BF16)
        chosen_s[micro] = chosen
        if micro == 0:
            csend[...] = mm(chosen, cot).astype(BF16)
            arrivals += messages.rows(csend, cot_slots_ref, dsend.at[0], drecv.at[0])
        else:
            next_cot_ref[...] = mm(chosen, cot).astype(BF16)
            keep(next_cot_ref, next_cot_out)
        if step < n_steps:
            gather_next(step)
            step += 1
    if reps > 1:
        weights_start(2, 0, top)
    while step < n_steps:
        gather_next(step)
        step += 1
    if not gathered:
        own.wait()
        keep(full_ref, full_out)
    if reps > 1:
        for span in range(2):
            weights_pass(span, top)
        weights_start(3, 0, top)
    for span in range(4):
        if span not in OWN_FIRST:
            for bit in inner_bits:
                weights_start(span, 0, bit)
    inner = sorted((held for held in combos(bits) if held and not held & 1), key=lambda h: (-(h & -h), h))
    early = [held for held in inner if held < top]
    late = [held for held in inner if held > top]
    for micro in range(MICRO):
        x = load_group(tok_ref, order, micro, group, seq, pad, x_s)
        attention_forward(dims, x, full_ref, states[micro])
        table = col_ref[micro]
        gates = states[micro][5][...]
        a2 = states[micro][4][...]
        if micro == 0:
            fill_message(dims, table, gates, a2, chosen_s[micro], asend, tsend)
            arrivals += messages.rows(asend, buf_ref, dsend.at[1], drecv.at[1])
            arrivals += messages.tails(tsend, tail_ref, dsend.at[2], drecv.at[2], range(n_pos))
        else:
            fill_message(dims, table, gates, a2, chosen_s[micro], next_ref, next_tail_ref)
            keep(next_ref, next_out)
            keep(next_tail_ref, next_tail_out)
        for held, kept in zip(states[micro], state_outs[micro]):
            keep(held, kept)
    for span in range(4):
        for held in early:
            weights_pass(span, held)
        if reps > 1 and span >= 2:
            weights_pass(span, top)
        if span < 2:
            for held in late:
                weights_pass(span, held)
    for span in range(2, 4):
        for held in late:
            weights_pass(span, held)
    for (_, held), copy in weight_copies.items():
        if held & 1:
            copy.wait_recv()
    arrive(arrivals)
    leave(arrivals)
    for copy in kept_copies:
        copy.wait()
    for copy in gather_copies:
        copy.wait_send()
    for copy in weight_copies.values():
        copy.wait_send()


def run_first(dims, n_shard, batch, routes, tokens, cotangent, packed, own_in, own_out):
    n_img, seq, pad, group, n_pos, reps, cap, cap_pad, n_exp = dims
    width = tokens.shape[-1]
    rows = group * pad
    n_slots = reps * n_pos * cap_pad
    tail_wide = round_up(cap_pad, 128)
    n_dev = n_exp * n_shard
    n_pieces = reps * n_shard
    total = packed.shape[1]
    orders = bit_orders(n_exp, n_shard)
    middle = total // 256 * 128
    cuts = ((0, middle), (middle, total))
    gathered = packed.shape[0] % 16 != 0
    if gathered:
        packed = gather_params(packed, n_exp, n_shard, 3)
    state = (
        jax.ShapeDtypeStruct((rows, width), BF16),
        jax.ShapeDtypeStruct((rows, 3 * width), BF16),
        jax.ShapeDtypeStruct((rows, width), BF16),
        jax.ShapeDtypeStruct((rows, width), F32),
        jax.ShapeDtypeStruct((rows, width), BF16),
        jax.ShapeDtypeStruct((rows, 128), F32),
        jax.ShapeDtypeStruct((rows, 128), F32),
    )
    full_rows = 16 if gathered else n_dev * packed.shape[0]
    out = pl.pallas_call(
        functools.partial(first_kernel, dims, n_shard, orders, cuts, gathered),
        out_shape=(
            jax.ShapeDtypeStruct((MICRO, rows, 128), F32),
            jax.ShapeDtypeStruct((full_rows, total), BF16),
            jax.ShapeDtypeStruct((n_pieces,) + own_in.shape, BF16),
            jax.ShapeDtypeStruct((n_pieces,) + own_out.shape, BF16),
            jax.ShapeDtypeStruct((n_slots, width), BF16),
            jax.ShapeDtypeStruct((n_pos * 16, tail_wide), BF16),
            jax.ShapeDtypeStruct((n_slots, width), BF16),
            jax.ShapeDtypeStruct((n_slots, width), BF16),
            jax.ShapeDtypeStruct((n_pos * 16, tail_wide), BF16),
            jax.ShapeDtypeStruct((n_slots, width), BF16),
            *state,
            *state,
        ),
        in_specs=[SMEM_SPEC] + [VMEM_SPEC] * 4 + [ANY_SPEC] * 2,
        out_specs=(VMEM_SPEC,) + (ANY_SPEC,) * 23,
        scratch_shapes=[
            *[pltpu.VMEM(shape.shape, shape.dtype) for shape in state + state],
            pltpu.VMEM((n_slots, width), BF16),
            pltpu.VMEM((n_pos * 16, tail_wide), BF16),
            pltpu.VMEM((n_slots, width), BF16),
            pltpu.VMEM((full_rows, total), BF16),
            pltpu.VMEM((rows, width), F32),
            pltpu.VMEM((rows, 128), jnp.int32),
            pltpu.VMEM((MICRO, n_slots, rows), BF16),
            pltpu.VMEM((n_slots, width), BF16),
            pltpu.VMEM((n_pos * 16, tail_wide), BF16),
            pltpu.VMEM((n_slots, width), BF16),
            pltpu.SemaphoreType.DMA((18,)),
            pltpu.SemaphoreType.DMA,
            pltpu.SemaphoreType.DMA((2, n_dev - 1)),
            pltpu.SemaphoreType.DMA((2, n_dev - 1)),
            pltpu.SemaphoreType.DMA((4, n_pieces)),
            pltpu.SemaphoreType.DMA((4, n_pieces)),
            pltpu.SemaphoreType.DMA((4, n_exp)),
            pltpu.SemaphoreType.DMA((4, n_exp)),
        ],
        compiler_params=pltpu.CompilerParams(
            collective_id=0, has_side_effects=True, vmem_limit_bytes=VMEM_LIMIT
        ),
        cost_estimate=cost(20e9, 60e6, 4e6),
    )(batch, routes, tokens, cotangent, packed, own_in, own_out)
    return out[0], packed if gathered else out[1], out[2:4], out[4:10], out[10:17], out[17:24]


def gelu_pair(v):
    size = jnp.abs(v)
    bell = jnp.exp(v * v * -0.5)
    t = 1.0 / (1.0 + (0.3275911 / math.sqrt(2.0)) * size)
    series = t * (
        0.5 * 0.254829592
        + t * (0.5 * -0.284496736 + t * (0.5 * 1.421413741 + t * (0.5 * -1.453152027 + t * (0.5 * 1.061405429))))
    )
    tail = series * bell
    share = jnp.where(v >= 0.0, 1.0 - tail, tail)
    return v * share, share + v * bell * (1.0 / math.sqrt(2.0 * math.pi))


def second_kernel(dims, n_shard, chunk, *refs):
    n_img, seq, pad, group, n_pos, reps, cap, cap_pad, n_exp = dims
    own_in_ref, own_out_ref, win_ref, wout_ref, buf0, tail0, cot0, next_ref, next_tail_ref, next_cot_ref = refs[:10]
    eo_ret, eo_next, db_ret, dt_ret, gin_ref, gout_ref, gin_core, gout_core = refs[10:18]
    (buf1, tail1, cot1, w_in, w_out, hid_s, dh_s, deo_s, pre, back, eo_acc, db_acc, eo_send, db_send, dt_send,
     turned_s, gin_s, wsems, dsend, drecv, rsend, rrecv, gsems, hsend, hrecv) = refs[18:]
    width = buf0.shape[-1]
    ff = win_ref.shape[-1]
    part = n_pos * cap_pad
    n_pieces = reps * n_shard
    n_chunks = n_shard * ff // chunk
    expert, shard = lax.axis_index("expert"), lax.axis_index("shard")
    me = expert * n_shard + shard
    peers = [1] + [pos * n_shard for pos in range(1, n_pos)]
    if peers:
        barrier = pltpu.get_barrier_semaphore()
        for peer in peers:
            to = flip_all(me, peer)
            pl.semaphore_signal(
                barrier, inc=1, device_id=(to // n_shard, lax.rem(to, n_shard)), device_id_type=MESH
            )
        pl.semaphore_wait(barrier, len(peers))
    messages = Messages(n_shard, me, n_pos, reps, cap_pad)

    def come(rel):
        started = messages.rows(next_ref, buf1, dsend.at[0], drecv.at[0], (rel,))
        started += messages.rows(next_cot_ref, cot1, dsend.at[1], drecv.at[1], (rel,))
        if rel == 0:
            started += messages.tails(next_tail_ref, tail1, dsend.at[2], drecv.at[2], range(n_pos))
        return started

    coming = [come(0)]
    loads = []
    for rel in range(reps):
        for s in range(n_shard):
            piece = rel * n_shard + s
            cols = pl.ds(s * ff, ff)
            from_in = win_ref.at[piece] if piece else own_in_ref
            from_out = wout_ref.at[piece] if piece else own_out_ref
            copies = (
                pltpu.make_async_copy(from_in, w_in.at[rel, :, cols], wsems.at[0, piece]),
                pltpu.make_async_copy(from_out, w_out.at[rel, cols, :], wsems.at[1, piece]),
            )
            for copy in copies:
                copy.start()
            loads.append(copies)
    returns = ([], [])
    tail_id = lax.broadcasted_iota(jnp.int32, (16, cap_pad), 0)
    ones = jnp.ones((16, width), BF16)
    db_tail_wide = dt_send.shape[-1]
    for micro in range(MICRO):
        buf, tail, cot = ((buf0, tail0, cot0), (buf1, tail1, cot1))[micro]
        if micro == 1:
            arrive(coming[0])
        tails = tail[...].astype(F32)
        spare = round_up(n_pos * 16, 128) - n_pos * 16
        if spare:
            tails = jnp.concatenate([tails, jnp.zeros((spare, tails.shape[1]), F32)], axis=0)
        turned = tails.T
        for rel in range(reps):
            if micro > 0 and rel > 0:
                arrive(coming[rel])
            for pos in range(n_pos):
                at = slice(rel * part + pos * cap_pad, rel * part + (pos + 1) * cap_pad)
                lane = pos * 16 + 2 * rel
                gate = turned[0:cap_pad, lane : lane + 1] + turned[0:cap_pad, lane + 1 : lane + 2]
                deo_s[micro, at, :] = (cot[at, :].astype(F32) * gate).astype(BF16)
            if micro == 0:
                for s in range(n_shard):
                    for copy in loads[rel * n_shard + s]:
                        copy.wait()
            bias = w_in[rel, width : width + 16, :].astype(F32)
            bias_out = None
            for s in range(n_shard):
                row = jnp.concatenate(
                    [bias[1 + i : 2 + i, s * ff : (s + 1) * ff] for i in range(width // ff)], axis=1
                )
                bias_out = row if bias_out is None else bias_out + row
            if micro > 0:
                leave(returns[0][rel])
                arrive([member for member in returns[0][rel] if not member[1]])
            for pos_low in range(0, n_pos, pre.shape[0] // cap_pad):
                here = slice(rel * part + pos_low * cap_pad, rel * part + pos_low * cap_pad + pre.shape[0])
                kept = slice(micro * part + pos_low * cap_pad, micro * part + pos_low * cap_pad + pre.shape[0])
                eo_acc[...] = jnp.broadcast_to(bias_out, eo_acc.shape)
                db_acc[...] = jnp.zeros(db_acc.shape, F32)

                def piece(c, carry, rel=rel, micro=micro, here=here, kept=kept, buf=buf):
                    cols = pl.ds(pl.multiple_of(c * chunk, chunk), chunk)
                    bias = w_in[rel, width : width + 16, cols].astype(F32)[0:1, :]
                    pre[...] = mm(buf[here, :], w_in[rel, 0:width, cols])
                    back[...] = mm_nt(deo_s[micro, here, :], w_out[rel, cols, :])
                    for pos in range(pre.shape[0] // cap_pad):
                        at = slice(pos * cap_pad, (pos + 1) * cap_pad)
                        to = slice(kept.start + pos * cap_pad, kept.start + (pos + 1) * cap_pad)
                        value, slope = gelu_pair(pre[at, :] + bias)
                        hid_s[rel, to, cols] = value.astype(BF16)
                        dh_s[rel, to, cols] = (back[at, :] * slope).astype(BF16)
                    eo_acc[...] += mm(hid_s[rel, kept, cols], w_out[rel, cols, :])
                    db_acc[...] += mm_nt(dh_s[rel, kept, cols], w_in[rel, 0:width, cols])
                    return carry

                lax.fori_loop(0, n_chunks, piece, 0)
                for pos in range(pos_low, pos_low + pre.shape[0] // cap_pad):
                    at = slice((pos - pos_low) * cap_pad, (pos - pos_low + 1) * cap_pad)
                    to = slice(rel * part + pos * cap_pad, rel * part + (pos + 1) * cap_pad)
                    eo = eo_acc[at, :].astype(BF16)
                    eo_send[to, :] = eo
                    db_send[to, :] = db_acc[at, :].astype(BF16)
                    product = cot[to, :].astype(F32) * eo.astype(F32)
                    high = product.astype(BF16)
                    low = (product - high.astype(F32)).astype(BF16)
                    dgate = mm_nt(ones, high) + mm_nt(ones, low)
                    dg_high = dgate.astype(BF16).astype(F32)
                    block = rel * n_pos + pos
                    rows16 = slice(block * 16, (block + 1) * 16)
                    dt_send[micro, rows16, :] = jnp.zeros((16, db_tail_wide), BF16)
                    dt_send[micro, rows16, 0:cap_pad] = jnp.where(
                        tail_id == 0, dg_high, jnp.where(tail_id == 1, dgate - dg_high, 0.0)
                    ).astype(BF16)
            if micro == 0 and rel + 1 < reps:
                coming.append(come(rel + 1))
            blocks = range(rel * n_pos, (rel + 1) * n_pos)
            sent = messages.rows(db_send, db_ret.at[micro], rsend.at[micro, 0], rrecv.at[micro, 0], (rel,))
            sent += messages.tails(
                dt_send.at[micro], dt_ret.at[micro], rsend.at[micro, 1], rrecv.at[micro, 1], blocks
            )
            if micro == 0:
                sent += messages.rows(eo_send, eo_ret, rsend.at[micro, 2], rrecv.at[micro, 2], (rel,))
            else:
                at = pl.ds(rel * part, part)
                copy = pltpu.make_async_copy(eo_send.at[at], eo_next.at[at], rrecv.at[micro, 2, rel])
                copy.start()
                sent.append((copy, False))
            returns[micro].append(sent)

    stores = []
    crossing = []
    core_peer = flip(me, 1)

    def store(kind, slot, c, rel):
        staged = (gin_s, gin_s.at[:, 0:width, :])[kind]
        started = []
        for s in range(c * chunk // ff, (c + 1) * chunk // ff):
            index = s // 2 * reps + rel
            source = staged.at[slot, :, pl.ds(s * ff - c * chunk, ff)]
            if s % 2:
                copy = pltpu.make_async_remote_copy(
                    src_ref=source,
                    dst_ref=(gin_core, gout_core)[kind].at[index],
                    send_sem=hsend.at[kind, index],
                    recv_sem=hrecv.at[kind, index],
                    device_id=(core_peer // n_shard, lax.rem(core_peer, n_shard)),
                    device_id_type=MESH,
                )
                crossing.append(copy)
            else:
                copy = pltpu.make_async_copy(source, (gin_ref, gout_ref)[kind].at[index], gsems.at[kind, index])
            copy.start()
            started.append((copy, s % 2 == 1))
        stores.append(started)

    def stored(started):
        for copy, remote in started:
            if remote:
                copy.wait_send()
            else:
                copy.wait()

    def next_slot():
        if len(stores) >= 2:
            stored(stores[-2])
        return len(stores) % 2

    wide_id = lax.broadcasted_iota(jnp.int32, (16, ff), 0)
    for rel in range(reps)[::-1]:
        here = slice(rel * part, (rel + 1) * part)
        deo_bias = None
        for micro, buf in enumerate((buf0, buf1)):
            turned_s[:, micro * part : (micro + 1) * part] = buf[here, :].T
            total = jnp.sum(deo_s[micro, here, :].astype(F32), axis=0, keepdims=True)
            deo_bias = total if deo_bias is None else deo_bias + total
        for c in range(n_chunks):
            cols = slice(c * chunk, (c + 1) * chunk)
            slot = next_slot()
            dh = dh_s[rel, :, cols]
            gin_s[slot, 0:width, :] = mm(turned_s[...], dh).astype(BF16)
            bias_in = jnp.sum(dh.astype(F32), axis=0, keepdims=True)
            for s in range(c * chunk // ff, (c + 1) * chunk // ff):
                at = slice(s * ff - c * chunk, (s + 1) * ff - c * chunk)
                tail = jnp.where(wide_id == 0, bias_in[:, at], 0.0)
                for i in range(width // ff):
                    tail = jnp.where(wide_id == 1 + i, deo_bias[:, i * ff : (i + 1) * ff], tail)
                gin_s[slot, width : width + 16, at] = tail.astype(BF16)
            store(0, slot, c, rel)
        for micro in range(MICRO):
            turned_s[:, micro * part : (micro + 1) * part] = deo_s[micro, here, :].T
        for c in range(n_chunks):
            slot = next_slot()
            gin_s[slot, 0:width, :] = mm(turned_s[...], hid_s[rel, :, c * chunk : (c + 1) * chunk]).astype(BF16)
            store(1, slot, c, rel)
    for started in stores[-2:]:
        stored(started)
    for copy in crossing:
        copy.wait_recv()
    for sent in returns[0]:
        arrive_remote(sent)
    for sent in returns[1]:
        arrive(sent)
        leave(sent)
    for started in coming:
        leave(started)


def run_second(dims, n_shard, own, weights, slots):
    n_img, seq, pad, group, n_pos, reps, cap, cap_pad, n_exp = dims
    win, wout = weights
    width = slots[0].shape[-1]
    ext, ff = win.shape[1:]
    total = n_shard * ff
    part = n_pos * cap_pad
    n_slots = reps * part
    chunk = max(ff, min(total, 1024 if n_slots <= 1280 else 256))
    block_rows = part if n_slots <= 1280 else n_pos // 4 * cap_pad
    tail_wide = round_up(cap_pad, 128)
    n_pieces = reps * n_shard
    return pl.pallas_call(
        functools.partial(second_kernel, dims, n_shard, chunk),
        out_shape=(
            jax.ShapeDtypeStruct((n_slots, width), BF16),
            jax.ShapeDtypeStruct((n_slots, width), BF16),
            jax.ShapeDtypeStruct((MICRO, n_slots, width), BF16),
            jax.ShapeDtypeStruct((MICRO, n_exp * 16, tail_wide), BF16),
            jax.ShapeDtypeStruct((n_pieces // 2, ext, ff), BF16),
            jax.ShapeDtypeStruct((n_pieces // 2, width, ff), BF16),
            jax.ShapeDtypeStruct((n_pieces // 2, ext, ff), BF16),
            jax.ShapeDtypeStruct((n_pieces // 2, width, ff), BF16),
        ),
        in_specs=[ANY_SPEC] * 4 + [VMEM_SPEC] * 3 + [ANY_SPEC] * 3,
        out_specs=(ANY_SPEC,) * 8,
        scratch_shapes=[
            pltpu.VMEM((n_slots, width), BF16),
            pltpu.VMEM((n_pos * 16, tail_wide), BF16),
            pltpu.VMEM((n_slots, width), BF16),
            pltpu.VMEM((reps, ext, total), BF16),
            pltpu.VMEM((reps, total, width), BF16),
            pltpu.VMEM((reps, MICRO * part, total), BF16),
            pltpu.VMEM((reps, MICRO * part, total), BF16),
            pltpu.VMEM((MICRO, n_slots, width), BF16),
            pltpu.VMEM((block_rows, chunk), F32),
            pltpu.VMEM((block_rows, chunk), F32),
            pltpu.VMEM((block_rows, width), F32),
            pltpu.VMEM((block_rows, width), F32),
            pltpu.VMEM((n_slots, width), BF16),
            pltpu.VMEM((n_slots, width), BF16),
            pltpu.VMEM((MICRO, n_exp * 16, tail_wide), BF16),
            pltpu.VMEM((width, MICRO * part), BF16),
            pltpu.VMEM((2, ext, chunk), BF16),
            pltpu.SemaphoreType.DMA((2, n_pieces)),
            pltpu.SemaphoreType.DMA((3, n_exp)),
            pltpu.SemaphoreType.DMA((3, n_exp)),
            pltpu.SemaphoreType.DMA((MICRO, 3, n_exp)),
            pltpu.SemaphoreType.DMA((MICRO, 3, n_exp)),
            pltpu.SemaphoreType.DMA((2, n_pieces // 2)),
            pltpu.SemaphoreType.DMA((2, n_pieces // 2)),
            pltpu.SemaphoreType.DMA((2, n_pieces // 2)),
        ],
        compiler_params=pltpu.CompilerParams(
            collective_id=1, has_side_effects=True, vmem_limit_bytes=62 * 1024 * 1024
        ),
        cost_estimate=cost(32e9, 60e6, 10e6),
    )(*own, win, wout, *slots)


def combine_group(dims, micro, table, gates, mid, eo, out_ref):
    n_img, seq, pad, group, n_pos, reps, cap, cap_pad, n_exp = dims
    rows = group * pad
    n_slots = reps * n_pos * cap_pad
    ids = lanes(rows, 128).astype(F32)
    along = lanes(rows, n_slots).astype(F32)
    result = mid
    for lane in range(2):
        gate = jnp.sum(jnp.where(ids == table[:, lane : lane + 1], gates, 0.0), axis=1, keepdims=True)
        chosen = (along == table[:, 2 + lane : 3 + lane]).astype(F32).astype(BF16)
        result = result + gate * mm(chosen, eo)
    for n in range(group):
        out_ref[micro * group + n] = result[n * pad : n * pad + seq, :].astype(BF16)


def backward_group(dims, micro, order, hook, refs):
    n_img, seq, pad, group, n_pos, reps, cap, cap_pad, n_exp = dims
    (tok_ref, cot_ref, full_ref, table, state, db, dt, gtok_ref, grad_ref, c_s, x_s, vec_s, dqkv_s, do_s, dg_s) = refs
    a1_ref, qkv_ref, mix_ref, mid_ref, a2_ref, gate_ref, lse_ref = state
    rows = group * pad
    n_slots = reps * n_pos * cap_pad
    width = tok_ref.shape[-1]
    head = width // HEADS
    per_pair = 128 // head
    c = load_group(cot_ref, order, micro, group, seq, pad, c_s)
    small = full_ref[:, 4 * width :]
    turned = small.astype(F32).T
    gain1 = turned[n_exp : n_exp + 1, :]
    gain2 = turned[n_exp + 2 : n_exp + 3, :]
    if micro == 0:
        vec_s[...] = jnp.zeros(vec_s.shape, F32)

    def add_vec(at, value):
        vec_s[n_exp + at : n_exp + at + 1, :] += value

    along = lanes(rows, n_slots).astype(F32)
    chosen = ((along == table[:, 2:3]) | (along == table[:, 3:4])).astype(F32).astype(BF16)
    tails = dt[...].astype(F32)
    spare = round_up(tails.shape[0], 128) - tails.shape[0]
    if spare:
        tails = jnp.concatenate([tails, jnp.zeros((spare, tails.shape[1]), F32)], axis=0)
    tails = tails.T
    lane_slot = lanes(cap_pad, 128)
    me = lax.axis_index("expert")
    for block in range(reps * n_pos):
        at = slice(block * cap_pad, (block + 1) * cap_pad)
        lane = block * 16
        column = tails[0:cap_pad, lane : lane + 1] + tails[0:cap_pad, lane + 1 : lane + 2]
        expert = flip_all(me, block)
        dg_s[at, :] = jnp.where(lane_slot == expert, column, 0.0)
    dg = dg_s[...]
    dg_high = dg.astype(BF16)
    dg_low = (dg - dg_high.astype(F32)).astype(BF16)
    dgates = mm(chosen, dg_high) + mm(chosen, dg_low)
    routed = mm(chosen, db[...])
    gates = gate_ref[...]
    dlogits = (gates * (dgates - jnp.sum(gates * dgates, axis=1, keepdims=True))).astype(BF16)
    grad_small = mm_tn(a2_ref[...], dlogits)
    da2 = mm_nt(dlogits, small) + routed

    def norm_back(values, upstream, gain, at):
        normed, rate = norm_parts(values)
        add_vec(at, jnp.sum(upstream * normed, axis=0, keepdims=True))
        add_vec(at + 1, jnp.sum(upstream, axis=0, keepdims=True))
        scaled = upstream * gain
        return rate * (
            scaled
            - jnp.mean(scaled, axis=-1, keepdims=True)
            - normed * jnp.mean(scaled * normed, axis=-1, keepdims=True)
        )

    def add_grad(low, high, value):
        if micro == 0:
            grad_ref[:, low:high] = value
        else:
            grad_ref[:, low:high] += value

    dmid = c + norm_back(mid_ref[...], da2, gain2, 2)
    c_s[...] = dmid
    dbranch = dmid.astype(BF16)
    add_vec(6, jnp.sum(dbranch.astype(F32), axis=0, keepdims=True))
    add_grad(3 * width, 4 * width, mm_tn(mix_ref[...], dbranch))
    do_s[...] = mm_nt(dbranch, full_ref[:, 3 * width : 4 * width]).astype(BF16)
    hook()

    key_ok = lanes(pad, pad) < seq
    lane = lanes(pad, 128)
    scale = head ** (-0.5)
    for n in range(group):
        at = slice(n * pad, (n + 1) * pad)
        lse = lse_ref[at, :]
        for pair in range(width // 128):
            cols = pair * 128
            q2 = qkv_ref[at, cols : cols + 128]
            k2 = qkv_ref[at, width + cols : width + cols + 128]
            v2 = qkv_ref[at, 2 * width + cols : 2 * width + cols + 128]
            do2 = do_s[at, cols : cols + 128]
            dq2 = dk2 = dv2 = None
            for sub in range(per_pair):
                index = pair * per_pair + sub
                mine = (lane >= sub * head) & (lane < (sub + 1) * head)
                zero = jnp.zeros_like(q2)
                qh = jnp.where(mine, q2, zero)
                kh = jnp.where(mine, k2, zero)
                doh = jnp.where(mine, do2, zero)
                scores = jnp.where(key_ok, mm_nt(qh, k2), -jnp.inf)
                probs = jnp.exp(scores - lse[:, index : index + 1])
                dprobs = mm_nt(doh, v2)
                dscores = (probs * (dprobs - jnp.sum(probs * dprobs, axis=-1, keepdims=True))).astype(BF16)
                dv = mm_tn(probs.astype(BF16), doh)
                dq = mm(dscores, kh)
                dk = mm_tn(dscores, qh)
                dq2 = dq if dq2 is None else dq2 + dq
                dk2 = dk if dk2 is None else dk2 + dk
                dv2 = dv if dv2 is None else dv2 + dv
            dqkv_s[at, cols : cols + 128] = (dq2 * scale).astype(BF16)
            dqkv_s[at, width + cols : width + cols + 128] = dk2.astype(BF16)
            dqkv_s[at, 2 * width + cols : 2 * width + cols + 128] = dv2.astype(BF16)
            hook()
    dqkv = dqkv_s[...]
    add_grad(0, 3 * width, mm_tn(a1_ref[...], dqkv))
    add_vec(4, jnp.sum(dqkv[:, 0:width].astype(F32), axis=0, keepdims=True))
    add_vec(5, jnp.sum(dqkv[:, 2 * width :].astype(F32), axis=0, keepdims=True))
    da1 = mm_nt(dqkv, full_ref[:, 0 : 3 * width])
    x = load_group(tok_ref, order, micro, group, seq, pad, x_s)
    dx = c_s[...] + norm_back(x, da1, gain1, 0)
    for n in range(group):
        gtok_ref[micro * group + n] = dx[n * pad : n * pad + seq, :]
    if micro == MICRO - 1:
        grad_small = grad_small + vec_s[...].T
    add_grad(4 * width, 4 * width + 128, grad_small)


def third_kernel(dims, n_shard, orders, cuts, separate, *refs):
    n_img, seq, pad, group, n_pos, reps, cap, cap_pad, n_exp = dims
    batch_ref, tok_ref, cot_ref, full_ref, col_ref = refs[:5]
    states = (refs[5:12], refs[12:19])
    eo_ref, db_ref, dt_ref, eo_next, gin_ref, gout_ref, gin_core, gout_core = refs[19:27]
    out_ref, gtok_ref, mine_ref, own_in_ref, own_out_ref = refs[27:32]
    (eo_late, out_s, gtok_s, acc_in, acc_out, land_in, land_out, c_s, x_s, vec_s, dqkv_s, do_s, dg_s, grad_s, sends, recvs,
     load_sems, esend, erecv, send_sems, recv_sems, rsend, rrecv) = refs[32:]
    top = n_pos * n_shard
    me = lax.axis_index("expert") * n_shard + lax.axis_index("shard")

    def place(index):
        return (index // n_shard, lax.rem(index, n_shard))

    greet(me, sorted(set(orders[0]) | {pos * n_shard for pos in range(1, n_pos)}), n_shard)
    returning = Messages(n_shard, me, n_pos, reps, cap_pad).rows(eo_next, eo_late, rsend, rrecv)
    order = image_order(batch_ref, n_img)

    levels = n_shard.bit_length() - 1
    bases = [0]
    for level in range(levels):
        bases.append(bases[-1] + (n_shard >> (level + 1)) * reps)
    pieces = ((gin_ref, acc_in, land_in), (gout_ref, acc_out, land_out))
    arriving = {}
    sending = []

    def ship(kind, source, slot, bit):
        copy = pltpu.make_async_remote_copy(
            src_ref=source,
            dst_ref=pieces[kind][2].at[slot],
            send_sem=esend.at[kind, slot],
            recv_sem=erecv.at[kind, slot],
            device_id=place(flip(me, bit)),
            device_id_type=MESH,
        )
        copy.start()
        arriving[kind, slot] = copy
        sending.append(copy)

    loads = {}
    for rel in range(reps)[::-1]:
        for kind in range(2):
            _, acc, land = pieces[kind]
            for j in range(n_shard // 2):
                at = j * reps + rel
                copies = (
                    pltpu.make_async_copy((gin_ref, gout_ref)[kind].at[at], acc.at[at], load_sems.at[kind, 0, at]),
                    pltpu.make_async_copy((gin_core, gout_core)[kind].at[at], land.at[at], load_sems.at[kind, 1, at]),
                )
                for copy in copies:
                    copy.start()
                loads[kind, at] = copies

    def stage(level, rel, kind):
        _, acc, land = pieces[kind]
        for j in list(range(n_shard >> (level + 1)))[::-1]:
            at = (j << level) * reps + rel
            slot = bases[level] + j * reps + rel
            if level == 0:
                for copy in loads[kind, at]:
                    copy.wait()
            else:
                arriving[kind, slot].wait_recv()
            acc[at] = (acc[at].astype(F32) + land[slot].astype(F32)).astype(BF16)
            if level + 1 < levels:
                if j % 2:
                    ship(kind, acc.at[at], bases[level + 1] + j // 2 * reps + rel, 2 << level)
            elif rel:
                ship(kind, acc.at[at], bases[levels], top)

    def last():
        total = []
        for kind in range(2):
            _, acc, land = pieces[kind]
            value = acc[0].astype(F32)
            if reps > 1:
                arriving[kind, bases[levels]].wait_recv()
                value = value + land[bases[levels]].astype(F32)
            total.append(value)
        own_in_ref[...] = total[0]
        own_out_ref[...] = total[1].T

    stages = [
        functools.partial(stage, level, rel, kind)
        for rel in range(reps)[::-1]
        for level in range(levels)
        for kind in range(2)
    ]
    calls = []

    def hook():
        calls.append(0)
        for _ in range(STAGES_AT.get(len(calls), 0)):
            if stages:
                stages.pop(0)()

    hook()
    for micro in range(MICRO):
        backward_group(
            dims, micro, order, hook,
            (tok_ref, cot_ref, full_ref, col_ref[micro], states[micro], db_ref.at[micro], dt_ref.at[micro],
             gtok_s, grad_s, c_s, x_s, vec_s, dqkv_s, do_s, dg_s),
        )

    def combine(micro):
        if micro == MICRO - 1:
            arrive(returning)
        eo = (eo_ref, eo_late)[micro][...]
        combine_group(dims, micro, col_ref[micro], states[micro][5][...], states[micro][3][...], eo, out_s)

    if separate:
        for micro in range(MICRO):
            combine(micro)
        mine_ref[...] = grad_s[...]
    else:
        n_dev, chunk_rows = sends.shape[:2]
        copies = []

        def rows_of(chunk):
            return pl.ds(pl.multiple_of(chunk * chunk_rows, chunk_rows), chunk_rows)

        for step in range(len(orders[0])):
            started = []
            base = n_dev - (n_dev >> step)
            count = n_dev >> (step + 1)
            for part, bits in enumerate(orders):
                peer = flip(me, bits[step])
                low, high = cuts[part]
                for at, combo in enumerate(combos(bits[step + 1 :])):
                    sends[base + at, :, low:high] = grad_s[rows_of(flip_all(peer, combo)), low:high].astype(BF16)
                copy = pltpu.make_async_remote_copy(
                    src_ref=sends.at[base : base + count, :, low:high],
                    dst_ref=recvs.at[base : base + count, :, low:high],
                    send_sem=send_sems.at[part, step],
                    recv_sem=recv_sems.at[part, step],
                    device_id=place(peer),
                    device_id_type=MESH,
                )
                copy.start()
                started.append(copy)
            if step < MICRO:
                combine(step)
            for part, bits in enumerate(orders):
                low, high = cuts[part]
                started[part].wait_recv()
                for at, combo in enumerate(combos(bits[step + 1 :])):
                    grad_s[rows_of(flip_all(me, combo)), low:high] += recvs[base + at, :, low:high].astype(F32)
            copies.extend(started)
        mine_ref[...] = grad_s[rows_of(me), :]
        for copy in copies:
            copy.wait_send()
    for image, rank in enumerate(image_ranks(batch_ref, n_img)):
        out_ref[image] = out_s[rank]
        gtok_ref[image] = gtok_s[rank]
    while stages:
        stages.pop(0)()
    last()
    leave(returning)
    for copy in sending:
        copy.wait_send()


def run_third(dims, n_shard, batch, tokens, cotangent, full, cols, states, returned, grads, chunk_rows):
    n_img, seq, pad, group, n_pos, reps, cap, cap_pad, n_exp = dims
    width = tokens.shape[-1]
    rows = group * pad
    n_slots = reps * n_pos * cap_pad
    n_dev = n_exp * n_shard
    total = full.shape[1]
    ext, ff = grads[0].shape[1:]
    orders = [bits[::-1] for bits in bit_orders(n_exp, n_shard)]
    middle = total // 256 * 128
    cuts = ((0, middle), (middle, total))
    separate = chunk_rows % 16 != 0
    land = (n_shard - 1) * reps + 1
    mine = (width, total) if separate else (chunk_rows, total)
    buffer = (1, 16, 128) if separate else (n_dev, chunk_rows, total)
    return pl.pallas_call(
        functools.partial(third_kernel, dims, n_shard, orders, cuts, separate),
        out_shape=(
            jax.ShapeDtypeStruct((n_img, seq, width), BF16),
            jax.ShapeDtypeStruct((n_img, seq, width), F32),
            jax.ShapeDtypeStruct(mine, F32),
            jax.ShapeDtypeStruct((ext, ff), F32),
            jax.ShapeDtypeStruct((ff, width), F32),
        ),
        in_specs=[SMEM_SPEC] + [VMEM_SPEC] * 21 + [ANY_SPEC] * 5,
        out_specs=(VMEM_SPEC,) * 5,
        scratch_shapes=[
            pltpu.VMEM((n_slots, width), BF16),
            pltpu.VMEM((n_img, seq, width), BF16),
            pltpu.VMEM((n_img, seq, width), F32),
            pltpu.VMEM((n_shard // 2 * reps, ext, ff), BF16),
            pltpu.VMEM((n_shard // 2 * reps, width, ff), BF16),
            pltpu.VMEM((land, ext, ff), BF16),
            pltpu.VMEM((land, width, ff), BF16),
            pltpu.VMEM((rows, width), F32),
            pltpu.VMEM((rows, width), F32),
            pltpu.VMEM((128, width), F32),
            pltpu.VMEM((rows, 3 * width), BF16),
            pltpu.VMEM((rows, width), BF16),
            pltpu.VMEM((n_slots, 128), F32),
            pltpu.VMEM((width, total), F32),
            pltpu.VMEM(buffer, BF16),
            pltpu.VMEM(buffer, BF16),
            pltpu.SemaphoreType.DMA((2, 2, n_shard // 2 * reps)),
            pltpu.SemaphoreType.DMA((2, land)),
            pltpu.SemaphoreType.DMA((2, land)),
            pltpu.SemaphoreType.DMA((2, len(orders[0]))),
            pltpu.SemaphoreType.DMA((2, len(orders[0]))),
            pltpu.SemaphoreType.DMA((n_exp,)),
            pltpu.SemaphoreType.DMA((n_exp,)),
        ],
        compiler_params=pltpu.CompilerParams(
            collective_id=2, has_side_effects=True, vmem_limit_bytes=62 * 1024 * 1024
        ),
        cost_estimate=cost(20e9, 60e6, 4e6),
    )(batch, tokens, cotangent, full, cols, *states[0], *states[1], *returned, *grads)


def on_device(
    tokens, cotangent, routes, batch_of_image, w_qkv, w_attn_out, w_router, norm1_gain, norm1_bias, norm2_gain,
    norm2_bias, bias_query, bias_value, bias_attn_out, w_expert_in, w_expert_out, bias_expert_in, bias_expert_out,
):
    n_img, seq, width = tokens.shape
    n_expert = lax.axis_size("expert")
    n_shard = lax.axis_size("shard")
    n_dev = n_expert * n_shard
    group = n_img // MICRO
    pad = round_up(seq, 16)
    rows = group * pad
    cap = 16 * group * seq // (5 * n_expert)
    cap_pad = round_up(cap, 16)
    reps = 2 if n_expert > 1 else 1
    n_pos = n_expert // reps
    ff = w_expert_in.shape[2]
    dims = (n_img, seq, pad, group, n_pos, reps, cap, cap_pad, n_expert)
    my_shard = lax.axis_index("shard")

    vectors = jnp.concatenate(
        [norm1_gain, norm1_bias, norm2_gain, norm2_bias, bias_query, bias_value, bias_attn_out]
    ).reshape(7, -1).T
    blank = jnp.zeros((vectors.shape[0], 128 - n_expert - 7), BF16)
    packed = jnp.concatenate([w_qkv, w_attn_out, w_router, vectors, blank], axis=1)

    quarter = width // n_shard
    out_bias = jnp.where(jnp.arange(width) // quarter == my_shard, jnp.tile(bias_expert_out[0], n_shard), 0)
    tail = jnp.concatenate(
        [bias_expert_in, out_bias.astype(BF16).reshape(-1, ff), jnp.zeros((15 - width // ff, ff), BF16)], axis=0
    )
    own_in = jnp.concatenate([w_expert_in[0], tail], axis=0)

    cols, full, weights, slots, *states = run_first(
        dims, n_shard, batch_of_image, routes, tokens, cotangent, packed, own_in, w_expert_out[0]
    )
    eo, eo_next, db, dt, *grads = run_second(dims, n_shard, (own_in, w_expert_out[0]), weights, slots)
    layer_out, gtok, mine, own_grad_in, own_grad_out = run_third(
        dims, n_shard, batch_of_image, tokens, cotangent, full, cols, states, (eo, db, dt, eo_next), grads,
        packed.shape[0],
    )
    if mine.shape[0] != packed.shape[0]:
        mine = scatter_params(mine, n_expert, n_shard, 4)
    tail = own_grad_in[width:, :]
    out_bias_grad = tail[1 : 1 + width // ff, :].reshape(width)
    small = mine[:, 4 * width :]
    vec = [small[:, n_expert + i] for i in range(7)]
    return (
        layer_out,
        gtok,
        mine[:, 0 : 3 * width],
        mine[:, 3 * width : 4 * width],
        small[:, 0:n_expert],
        *vec,
        own_grad_in[0:width, :][None],
        own_grad_out[None],
        tail[0:1, :],
        lax.dynamic_slice(out_bias_grad, (my_shard * (width // n_shard),), (width // n_shard,))[None],
    )


def solution(mesh):
    both = ("expert", "shard")
    placed = (
        (P(both, None, None),) * 3
        + (P(both),)
        + (P(both, None),) * 3
        + (P(both),) * 7
        + (P("expert", None, "shard"), P("expert", "shard", None), P("expert", "shard"), P("expert", "shard"))
    )
    return jax.shard_map(
        on_device,
        mesh=mesh,
        in_specs=placed,
        out_specs=(P(both, None, None),) * 2
        + (P(both, None),) * 3
        + (P(both),) * 7
        + (P("expert", None, "shard"), P("expert", "shard", None), P("expert", "shard"), P("expert", "shard")),
        check_vma=False,
    )
```
